32 devices in a mesh: row: 4 (over x, core), col: 8 (over z, y).
Axes of the slice: x: 2, y: 2, z: 4, core: 2. Of those that a mesh axis runs over, the one named last changes fastest.
Arguments:
- interactions: bfloat16 [4096, 2048], P('col', 'row'), may hold values from -1 to 1
- regular: float32 [4096], P('col'), may hold values from 0.2 to 2
Outputs:
- factored: float32 [4, 1024, 4096], P(None, 'row', 'col')
The draws below stay inside these ranges and needn't reach their ends.
All inputs are finite; a program needn't handle non-finite values.
Results may differ from the reference program's by a relative error of at most 0.0003.
Values may be sent and summed in bfloat16 or wider, within the bound.
No kernel may reach another device: no remote copies, remote signals or barrier semaphores. Data moves between devices by JAX's collectives and lax.ppermute only.
A program may use at most 128 MiB of HBM per device.

```python
import math
import jax
import jax.numpy as jnp
from jax import lax

PANEL = 1024
SPAN = 4
NI = 4096
USERS = 2048


def draw_interactions(key, part):
    key = jax.random.fold_in(key, 7)
    subkeys = jax.random.split(key, 4)
    cluster = jax.random.randint(subkeys[0], (NI,), 0, 64)
    loading = jax.random.truncated_normal(subkeys[1], -2.5, 2.5, (NI,), jnp.float32)
    profile = jax.random.truncated_normal(subkeys[2], -2.5, 2.5, (64, USERS), jnp.float32)
    noise_part = jax.random.truncated_normal(subkeys[3], -3.5, 3.5, (NI, USERS), jnp.float32)
    strength = 0.7
    shared = profile[cluster]
    values = (noise_part + strength * loading[:, None] * shared) / math.sqrt(USERS)
    return jnp.clip(values, -1.0, 1.0).astype(jnp.bfloat16)


def level_of(rng, dims, cuts, low, largest):
    def one(axis_at, shards_of):
        heights = jax.random.uniform(jax.random.fold_in(jax.random.fold_in(rng, 6), axis_at), (shards_of,), jnp.float32, low / len(cuts), largest / len(cuts))
        return jnp.repeat(jnp.exp(heights), dims[axis_at] // shards_of).reshape((-1,) + (1,) * (len(dims) - axis_at - 1))

    gain = one(*cuts[0])
    for cut in cuts[1:]:
        gain = gain * one(*cut)
    return gain


def setup_inputs(seed: int = 0) -> dict:
    seeds = jax.random.split(jax.random.key(seed), 3)
    interactions = draw_interactions(jax.random.fold_in(seeds[2], 71), 0)
    regular = jnp.clip(jnp.exp(math.log(2.0) - 2.3025851 * jax.random.uniform(seeds[1], (NI,), jnp.float32) ** level_of(seeds[1], (NI,), ((0, 8),), -0.2, 0.2)), 0.2, 2.0)
    return dict(interactions=interactions, regular=regular)


def reference(interactions, regular):
    gram_matrix = jnp.dot(interactions.astype(jnp.float32), interactions.T.astype(jnp.float32), preferred_element_type=jnp.float32)
    matrix = gram_matrix + jnp.diag(regular)
    lower_factor = jnp.linalg.cholesky(matrix[:PANEL, :PANEL])
    inverse = lax.linalg.triangular_solve(lower_factor, jnp.eye(PANEL, dtype=jnp.float32), left_side=True, lower=True)
    left_panel = jnp.dot(matrix[PANEL:, :PANEL], inverse.T, precision=lax.Precision.HIGHEST)
    trailing = matrix[PANEL:, PANEL:] - jnp.dot(left_panel, left_panel.T, precision=lax.Precision.HIGHEST)
    top_rows = jnp.concatenate([lower_factor, jnp.zeros((PANEL, NI - PANEL), jnp.float32)], 1)
    bottom = jnp.concatenate([left_panel, trailing], 1)
    return jnp.concatenate([top_rows, bottom], 0).reshape(SPAN, PANEL, NI)
```

```python
import functools
import jax
import jax.numpy as jnp
from jax import lax
from jax.experimental import pallas as pl
from jax.experimental.pallas import tpu as pltpu
from jax.sharding import PartitionSpec as P

PANEL = 1024
SPAN = 4
BLOCK = 128
WIDE = 256
SUB = 8
NBLOCKS = PANEL // BLOCK
PARTS = 16
VMEM = pltpu.VMEM
f32 = jnp.float32
bf16 = jnp.bfloat16


def dot_nt(a, b):
    return lax.dot_general(a, b, (((1,), (1,)), ((), ())), preferred_element_type=f32)


def split(value):
    high = value.astype(bf16)
    return high, (value - high.astype(f32)).astype(bf16)


def dot_nt3(a, b):
    return dot_nt(a[0], b[0]) + (dot_nt(a[0], b[1]) + dot_nt(a[1], b[0]))


def dot_nn3(a, b):
    def dot(x, y):
        return jnp.dot(x, y, preferred_element_type=f32)

    return dot(a[0], b[0]) + (dot(a[0], b[1]) + dot(a[1], b[0]))


def lanes(value, lane):
    return jnp.broadcast_to(value[:, lane : lane + 1], (SUB, BLOCK))


def sublanes(value, row):
    return jnp.broadcast_to(value[row : row + 1, :], (SUB, BLOCK))


def factor_block(block_ref, inverse_ref):
    tiles_count = BLOCK // SUB
    row_in_tile = lax.broadcasted_iota(jnp.int32, (SUB, BLOCK), 0)
    lane = lax.broadcasted_iota(jnp.int32, (SUB, BLOCK), 1)
    sides = [block_ref[pl.ds(SUB * t, SUB), :] for t in range(tiles_count)]
    inverses = [(lane == row_in_tile + SUB * t).astype(f32) for t in range(tiles_count)]
    uppers = []
    for step in range(tiles_count):
        base = SUB * step
        side, inverse = sides[step], inverses[step]
        columns = [lanes(side, base + b) for b in range(SUB)]
        entry = {(a, b): sublanes(columns[b], a) for b in range(SUB) for a in range(b, SUB)}
        ahead = [lanes(sides[step + 1], base + b) for b in range(SUB)] if step + 1 < tiles_count else None
        tops = [sublanes(side, a) for a in range(SUB)]
        insides = [sublanes(inverse, a) for a in range(SUB)]
        scale = []
        for m in range(SUB):
            root = lax.rsqrt(entry[m, m])
            scale.append(root)
            for a in range(m + 1, SUB):
                entry[a, m] = entry[a, m] * root
            for b in range(m + 1, SUB):
                for a in range(b, SUB):
                    entry[a, b] = entry[a, b] - entry[a, m] * entry[b, m]
            tops[m] = tops[m] * root
            insides[m] = insides[m] * root
            for a in range(m + 1, SUB):
                tops[a] = tops[a] - entry[a, m] * tops[m]
                insides[a] = insides[a] - entry[a, m] * insides[m]
            if ahead is not None:
                ahead[m] = ahead[m] * root
                for b in range(m + 1, SUB):
                    ahead[b] = ahead[b] - entry[b, m] * ahead[m]
        upper, lower_inverse = tops[0], insides[0]
        for m in range(1, SUB):
            upper = jnp.where(row_in_tile == m, tops[m], upper)
            lower_inverse = jnp.where(row_in_tile == m, insides[m], lower_inverse)
        uppers.append(jnp.where(lane >= row_in_tile + base, upper, 0.0))
        inverse_ref[pl.ds(base, SUB), :] = lower_inverse
        if ahead is not None:
            for m in range(SUB):
                sides[step + 1] = sides[step + 1] - ahead[m] * tops[m]
                inverses[step + 1] = inverses[step + 1] - ahead[m] * insides[m]
        if step + 2 < tiles_count:
            weights_top, weights_in = [None] * SUB, [None] * SUB
            for m in reversed(range(SUB)):
                top, inside = tops[m], insides[m]
                for b in range(m + 1, SUB):
                    top = top - entry[b, m] * weights_top[b]
                    inside = inside - entry[b, m] * weights_in[b]
                weights_top[m], weights_in[m] = top * scale[m], inside * scale[m]
            for t in range(step + 2, tiles_count):
                for m in range(SUB):
                    column = lanes(sides[t], base + m)
                    if m == 0:
                        top_sum, in_sum = column * weights_top[m], column * weights_in[m]
                    else:
                        top_sum = top_sum + column * weights_top[m]
                        in_sum = in_sum + column * weights_in[m]
                sides[t] = sides[t] - top_sum
                inverses[t] = inverses[t] - in_sum
    block_ref[...] = jnp.concatenate(uppers, 0).T


def place_pieces(place_ref, first, pieces, helds, sem):
    copies = []
    for i, (piece, held_ref) in enumerate(zip(pieces, helds)):
        rows, users = piece.shape
        row = pl.multiple_of(place_ref[first + 2 * i], rows)
        user = pl.multiple_of(place_ref[first + 2 * i + 1], users)
        copy = pltpu.make_async_copy(
            piece, held_ref.at[pl.ds(row, rows), pl.ds(user, users)], sem.at[i]
        )
        copy.start()
        copies.append(copy)
    return copies


def panel_kernel(views, count, width, place_ref, *refs):
    pieces, refs = refs[:count], refs[count:]
    outs, (high_ref, low_ref, inv_high_ref, inv_low_ref, lower_ref, block_ref, inverse_ref, items_ref, parts_ref, sem, out_sem) = refs[:4], refs[4:]
    held = [parts_ref if is_part else items_ref for _, _, _, is_part in views]
    views = [pieces[which].at[pl.ds(start, rows)] for which, start, rows, _ in views]
    for copy in place_pieces(place_ref, 0, views, held, sem):
        copy.wait()
    on_diagonal = lax.broadcasted_iota(jnp.int32, (BLOCK, BLOCK), 0) == lax.broadcasted_iota(
        jnp.int32, (BLOCK, BLOCK), 1
    )

    def before(k):
        start = k * BLOCK
        here = pl.ds(start, BLOCK)
        column = dot_nt(items_ref[pl.ds(start, PANEL - start), :], items_ref[here, :])
        if k > 0:
            high, low = high_ref[pl.ds(start, PANEL - start), :start], low_ref[pl.ds(start, PANEL - start), :start]
            column = column - dot_nt3((high, low), (high[:BLOCK], low[:BLOCK]))
        part, lane = PARTS * (start // width), start % width
        parts = parts_ref[pl.ds(part, PARTS), pl.ds(lane, BLOCK)].astype(f32)
        regular = parts[0:1] + parts[1:2] + parts[2:3]
        block_ref[...] = column[:BLOCK] + jnp.where(on_diagonal, regular, 0.0)
        if k + 1 < NBLOCKS:
            lower_ref[pl.ds(start + BLOCK, PANEL - start - BLOCK), :] = column[BLOCK:]

    def after(k):
        start = k * BLOCK
        here = pl.ds(start, BLOCK)
        diagonal = block_ref[...]
        inverse = split(inverse_ref[...])
        inv_high_ref[here, :], inv_low_ref[here, :] = inverse
        high_ref[here, here], low_ref[here, here] = split(diagonal)
        if k > 0:
            above = jnp.zeros((start, BLOCK), bf16)
            high_ref[pl.ds(0, start), here], low_ref[pl.ds(0, start), here] = above, above
        if k + 1 < NBLOCKS:
            rest = pl.ds(start + BLOCK, PANEL - start - BLOCK)
            high_ref[rest, here], low_ref[rest, here] = split(dot_nt3(split(lower_ref[rest, :]), inverse))

    def leave(k):
        column = pl.ds(k * BLOCK, BLOCK)
        return [
            pltpu.make_async_copy(high_ref.at[:, column], outs[0].at[:, column], out_sem.at[0, k]),
            pltpu.make_async_copy(low_ref.at[:, column], outs[1].at[:, column], out_sem.at[1, k]),
            pltpu.make_async_copy(inv_high_ref.at[column, :], outs[2].at[column, :], out_sem.at[2, k]),
            pltpu.make_async_copy(inv_low_ref.at[column, :], outs[3].at[column, :], out_sem.at[3, k]),
        ]

    before(0)

    def turn(k, carry):
        factor_block(block_ref, inverse_ref)
        for which in range(NBLOCKS):

            @pl.when(k == which)
            def _():
                after(which)
                for copy in leave(which):
                    copy.start()
                if which + 1 < NBLOCKS:
                    before(which + 1)

        return carry

    lax.fori_loop(0, NBLOCKS, turn, 0)
    for k in range(NBLOCKS):
        for copy in leave(k):
            copy.wait()


def room(users):
    return (2 * PANEL * users + 32 * 1024 * 1024) // 2**20 * 2**20


def factor_panel(place, pieces, views, width, users):
    outs = [
        ((PANEL, PANEL), bf16),
        ((PANEL, PANEL), bf16),
        ((PANEL, BLOCK), bf16),
        ((PANEL, BLOCK), bf16),
    ]
    held = [
        ((PANEL, BLOCK), f32),
        ((BLOCK, BLOCK), f32),
        ((BLOCK, BLOCK), f32),
        ((PANEL, users), bf16),
        ((PANEL // width * PARTS, users), bf16),
    ]
    return pl.pallas_call(
        functools.partial(panel_kernel, views, len(pieces), width),
        out_shape=[pltpu.HBM(*out) for out in outs],
        in_specs=[pl.BlockSpec(memory_space=pltpu.SMEM)]
        + [pl.BlockSpec(memory_space=pl.ANY)] * len(pieces),
        out_specs=[pl.BlockSpec(memory_space=pltpu.HBM)] * len(outs),
        scratch_shapes=[VMEM(*one) for one in outs + held]
        + [pltpu.SemaphoreType.DMA((len(views),)), pltpu.SemaphoreType.DMA((len(outs), NBLOCKS))],
        compiler_params=pltpu.CompilerParams(vmem_limit_bytes=room(users)),
        cost_estimate=pl.CostEstimate(flops=4 * 10**10, bytes_accessed=16 * 2**20, transcendentals=1024),
        name="factor_panel",
    )(place, *pieces)


def tile_kernel(counts, views, place_ref, regular_ref, *refs):
    factors, refs = refs[:4], refs[4:]
    pieces, refs = refs[: sum(counts)], refs[sum(counts) :]
    out_ref, refs = refs[0], refs[1:]
    high_ref, low_ref, inv_high_ref, inv_low_ref, left_high_ref, left_low_ref, wide_high_ref, wide_low_ref = refs[:8]
    panel_ref, rows_ref, cols_ref, sem, factor_sem = refs[8:]
    targets = [panel_ref] * counts[0] + [rows_ref] * counts[1] + [cols_ref] * counts[2]
    held = [targets[which] for which, *_ in views]
    views = [pieces[which].at[pl.ds(start, rows)] for which, start, rows in views]
    fetches = [
        pltpu.make_async_copy(factor, ref, factor_sem.at[i])
        for i, (factor, ref) in enumerate(zip(factors, (high_ref, low_ref, inv_high_ref, inv_low_ref)))
    ]
    for fetch in fetches:
        fetch.start()
    copies = place_pieces(place_ref, 2, views, held, sem)
    for fetch in fetches:
        fetch.wait()
    row_index, col_index = place_ref[0], place_ref[1]
    width, band = cols_ref.shape[0], rows_ref.shape[0] // SPAN
    row_count = (SPAN - 1) * band
    lower_items = rows_ref.at[pl.ds(band, row_count), :]
    panel_blocks = PANEL // width
    in_panel = col_index < panel_blocks
    slot = jnp.minimum(col_index, panel_blocks - 1)
    at = pl.ds(pl.multiple_of(slot * width, width), width)
    below, right = pl.ds(0, row_count), pl.ds(row_count, width)

    for start in range(0, PANEL, WIDE):
        first, second = pl.ds(start, BLOCK), pl.ds(start + BLOCK, BLOCK)
        between = dot_nn3((high_ref[second, first], low_ref[second, first]), (inv_high_ref[first, :], inv_low_ref[first, :]))
        corner = split(-dot_nn3((inv_high_ref[second, :], inv_low_ref[second, :]), split(between)))
        for wide_ref, inv_ref, part in ((wide_high_ref, inv_high_ref, corner[0]), (wide_low_ref, inv_low_ref, corner[1])):
            wide_ref[first, pl.ds(0, BLOCK)] = inv_ref[first, :]
            wide_ref[first, pl.ds(BLOCK, BLOCK)] = jnp.zeros((BLOCK, BLOCK), bf16)
            wide_ref[second, pl.ds(0, BLOCK)] = part
            wide_ref[second, pl.ds(BLOCK, BLOCK)] = inv_ref[second, :]

    def solve(items_ref, mine):
        for start in range(0, PANEL, WIDE):
            here = pl.ds(start, WIDE)
            column = dot_nt(items_ref[...], panel_ref[here, :])
            if start > 0:
                column = column - dot_nt3(
                    (left_high_ref[mine, :start], left_low_ref[mine, :start]), (high_ref[here, :start], low_ref[here, :start])
                )
            column = dot_nt3(split(column), (wide_high_ref[here, :], wide_low_ref[here, :]))
            left_high_ref[mine, here], left_low_ref[mine, here] = split(column)

    for copy, target in zip(copies, held):
        if target is not rows_ref:
            copy.wait()
    solve(cols_ref, right)
    for copy, target in zip(copies, held):
        if target is rows_ref:
            copy.wait()
    solve(lower_items, below)

    @pl.when(in_panel)
    def _():
        mine = pl.ds(pl.multiple_of(row_index * band, band), band)
        out_ref[pl.ds(0, band), :] = high_ref[mine, at].astype(f32) + low_ref[mine, at].astype(f32)
        out_ref[pl.ds(band, row_count), :] = left_high_ref[below, at].astype(f32) + left_low_ref[below, at].astype(f32)

    @pl.when(jnp.logical_not(in_panel))
    def _():
        out_ref[pl.ds(0, band), :] = jnp.zeros((band, width), f32)
        items = lax.broadcasted_iota(jnp.int32, (band, width), 0) + row_index * band
        columns = lax.broadcasted_iota(jnp.int32, (band, width), 1) + col_index * width
        for part in range(SPAN - 1):
            mine = pl.ds(part * band, band)
            tile = dot_nt(lower_items[mine, :], cols_ref[...])
            tile = tile + jnp.where(items + (part + 1) * PANEL == columns, regular_ref[...], 0.0)
            out_ref[pl.ds((part + 1) * band, band), :] = tile - dot_nt3(
                (left_high_ref[mine, :], left_low_ref[mine, :]), (left_high_ref[right, :], left_low_ref[right, :])
            )


def finish_tile(place, regular, factors, panel, rows, cols, views, band, users):
    spec = pl.BlockSpec(memory_space=VMEM)
    width = regular.shape[1]
    rows, cols = ([pltpu.with_memory_space_constraint(x, pltpu.HBM) for x in group] for group in (rows, cols))
    factors = [pltpu.with_memory_space_constraint(x, pltpu.HBM) for x in factors]
    pieces = panel + rows + cols
    out = ((SPAN * band, width), f32)
    below = (SPAN - 1) * band + width
    held = [
        ((below, PANEL), bf16),
        ((below, PANEL), bf16),
        ((PANEL, WIDE), bf16),
        ((PANEL, WIDE), bf16),
        ((PANEL, users), bf16),
        ((SPAN * band, users), bf16),
        ((width, users), bf16),
    ]
    return pl.pallas_call(
        functools.partial(tile_kernel, (len(panel), len(rows), len(cols)), views),
        out_shape=jax.ShapeDtypeStruct(*out),
        in_specs=[pl.BlockSpec(memory_space=pltpu.SMEM)]
        + [spec]
        + [pl.BlockSpec(memory_space=pltpu.HBM)] * len(factors)
        + [pl.BlockSpec(memory_space=pl.ANY)] * len(panel)
        + [pl.BlockSpec(memory_space=pltpu.HBM)] * (len(rows) + len(cols)),
        out_specs=spec,
        scratch_shapes=[VMEM(factor.shape, factor.dtype) for factor in factors]
        + [VMEM(*one) for one in held]
        + [pltpu.SemaphoreType.DMA((len(views),)), pltpu.SemaphoreType.DMA((len(factors),))],
        compiler_params=pltpu.CompilerParams(vmem_limit_bytes=room(users)),
        cost_estimate=pl.CostEstimate(flops=20 * 10**9, bytes_accessed=24 * 2**20, transcendentals=0),
        name="finish_tile",
    )(place, regular, *factors, *pieces)


CORES = 2


def body(interactions, regular):
    row_count, col_count = lax.axis_size("row"), lax.axis_size("col")
    row_index, col_index = lax.axis_index("row"), lax.axis_index("col")
    width, users = interactions.shape
    band = PANEL // row_count
    ways = PANEL // width
    assert row_count == CORES * ways and col_count == SPAN * ways and users >= width
    slot, way = col_index // ways, col_index % ways
    pair, core = row_index // CORES, row_index % CORES
    all_users = row_count * users

    def exchange(value, move, only=None):
        perm = []
        for source_row in range(row_count):
            for source_col in range(col_count):
                place = (source_row // CORES, source_row % CORES, source_col // ways, source_col % ways)
                if only is None or only(*place):
                    to = move(*place)
                    target = (to[0] * CORES + to[1]) * col_count + to[2] * ways + to[3]
                    perm.append((source_row * col_count + source_col, target))
        return lax.ppermute(value, ("row", "col"), perm)

    def after(value, *others):
        return lax.optimization_barrier((value, *others))[0]

    high = lax.reduce_precision(regular, 8, 7)
    middle = lax.reduce_precision(regular - high, 8, 7)
    parts = jnp.stack([high, middle, regular - high - middle]).astype(bf16)
    parts = jnp.pad(parts, ((0, PARTS - 3), (0, users - width)))

    half = width // 2
    shared = [interactions[:half], jnp.concatenate([interactions[half:], parts], 0)]
    reach = SPAN // 2
    while reach:
        got = [
            exchange(part, lambda p, h, s, w: (p, h, s + reach, w), lambda p, h, s, w: s % (2 * reach) == 0)
            for part in shared
        ]
        shared = [jnp.where(slot % (2 * reach) == reach, new, old) for new, old in zip(got, shared)]
        reach //= 2

    halves = interactions.reshape(CORES, band, users)
    offers = [lax.dynamic_index_in_dim(halves, core ^ flip, 0, False) for flip in range(CORES)]

    def numbers(values):
        return jnp.stack([jnp.asarray(v, jnp.int32) for v in values])

    panel, panel_views, panel_place, part_views, part_place = [], [], [], [], []
    cols, cols_place = [interactions], [0, row_index * users]
    rows, rows_views, rows_place = [], [], []

    def over_core(value):
        return exchange(value, lambda p, h, s, w: (p, 1 - h, s, w))

    def over_pair(value):
        return exchange(value, lambda p, h, s, w: (1 - p, h, s, w))

    def over_way(value, only=None):
        return exchange(value, lambda p, h, s, w: (p, h, s, 1 - w), only)

    if ways == 2:
        swapped = jnp.concatenate(
            [exchange(offers[flip], lambda p, h, s, w: (w, h ^ flip, s, p)) for flip in range(CORES)], 0
        )
        shared = [after(part, swapped) for part in shared]
        pair_side = [over_pair(part) for part in shared]
        way_side = [over_way(part) for part in shared]
        diagonal = [over_way(pair_side[0]), over_pair(way_side[1])]
        for from_pair, from_way, pieces in (
            (pair, way, shared),
            (1 - pair, way, pair_side),
            (pair, 1 - way, way_side),
            (1 - pair, 1 - way, diagonal),
        ):
            for which, piece in enumerate(pieces):
                for from_core, value in ((core, piece), (1 - core, over_core(piece))):
                    if which and value is piece and (pieces is shared or pieces is way_side):
                        part_views.append((len(panel), half, PARTS, True))
                        part_place += [from_way * PARTS, 0]
                    panel_views.append((len(panel), 0, half, False))
                    panel_place += [from_way * width + which * half, (from_pair * CORES + from_core) * users]
                    panel.append(value)
        crossed = [*pair_side, *way_side, *diagonal]
        held = after(interactions, *crossed)
        for flip in range(1, row_count):
            cols.append(lax.ppermute(held, "row", [(r, r ^ flip) for r in range(row_count)]))
            cols_place += [0, (row_index ^ flip) * users]
        for turn in range(SPAN):
            piece = swapped
            if turn:
                piece = exchange(
                    swapped if turn == 1 else after(swapped, *got),
                    lambda p, h, s, w: (p, h, (s - turn) % SPAN, w),
                    lambda p, h, s, w: s > 0,
                )
            twin = over_way(after(piece, *crossed), lambda p, h, s, w: (s + turn) % SPAN > 0)
            for from_way, value in ((way, piece), (1 - way, twin)):
                for flip in range(CORES):
                    rows_views.append((len(rows), flip * band, band))
                    rows_place += [(slot + turn) % SPAN * band, (from_way * CORES + (core ^ flip)) * users]
                rows.append(value)
    else:
        groups = [[s * ways + w for w in range(ways)] for s in range(SPAN)]
        shared = lax.all_gather(jnp.concatenate(shared, 0), "col", axis=0, axis_index_groups=groups)
        parts = shared[:, width:].reshape(ways * PARTS, users)
        shared = shared[:, :width].reshape(PANEL, users)
        panel, panel_place = [lax.all_gather(shared, "row", axis=1, tiled=True), parts], [0, 0]
        panel_views = [(0, 0, PANEL, False)]
        part_views, part_place = [(1, 0, ways * PARTS, True)], [0, 0]
        cols, cols_place = [lax.all_gather(interactions, "row", axis=1, tiled=True)], [0, 0]
        quarters, quarter_users = [], []
        for turn in range(ways):
            for flip in range(CORES):
                quarters.append(exchange(offers[flip], lambda p, h, s, w: (w, h ^ flip, s, (p + turn) % ways)))
                quarter_users.append(((way - turn) % ways * CORES + (core ^ flip)) * users)
        groups = [[s * ways + w for s in range(SPAN)] for w in range(ways)]
        rows = [lax.all_gather(jnp.concatenate(quarters, 0), "col", axis=0, tiled=True, axis_index_groups=groups)]
        for from_slot in range(1, SPAN):
            for which, from_users in enumerate(quarter_users):
                rows_views.append((0, (from_slot * len(quarters) + which) * band, band))
                rows_place += [from_slot * band, from_users]

    factors = factor_panel(
        numbers(panel_place + part_place), panel, panel_views + part_views, width, all_users
    )
    views = [view[:3] for view in panel_views]
    views += [(len(panel) + i, start, count) for i, start, count in rows_views]
    views += [(len(panel) + len(rows) + i, 0, width) for i in range(len(cols))]
    tile = finish_tile(
        numbers([row_index, col_index] + panel_place + rows_place + cols_place),
        regular[None, :], factors, panel, rows, cols, views, band, all_users,
    )
    return tile.reshape(SPAN, band, width)


def solution(mesh):
    return jax.shard_map(
        body,
        mesh=mesh,
        in_specs=(P("col", "row"), P("col")),
        out_specs=P(None, "row", "col"),
        check_vma=False,
    )
```

```python
import functools
import math
import jax
import jax.numpy as jnp
from jax import lax
from jax.experimental import pallas as pl
from jax.experimental.pallas import tpu as pltpu
from jax.sharding import PartitionSpec as P

PANEL = 1024
SPAN = 4
BLOCK = 128
WIDE = 256
SUB = 8
NBLOCKS = PANEL // BLOCK
PARTS = 16
VMEM = pltpu.VMEM
f32 = jnp.float32
bf16 = jnp.bfloat16


def dot_nt(a, b):
    return lax.dot_general(a, b, (((1,), (1,)), ((), ())), preferred_element_type=f32)


def split(value):
    high = value.astype(bf16)
    return high, (value - high.astype(f32)).astype(bf16)


def dot_nt3(a, b):
    return dot_nt(a[0], b[0]) + (dot_nt(a[0], b[1]) + dot_nt(a[1], b[0]))


def dot_nn3(a, b):
    def dot(x, y):
        return jnp.dot(x, y, preferred_element_type=f32)

    return dot(a[0], b[0]) + (dot(a[0], b[1]) + dot(a[1], b[0]))


def lanes(value, lane):
    return jnp.broadcast_to(value[:, lane : lane + 1], (SUB, BLOCK))


def sublanes(value, row):
    return jnp.broadcast_to(value[row : row + 1, :], (SUB, BLOCK))


def factor_block(block_ref, inverse_ref):
    tiles_count = BLOCK // SUB
    row_in_tile = lax.broadcasted_iota(jnp.int32, (SUB, BLOCK), 0)
    lane = lax.broadcasted_iota(jnp.int32, (SUB, BLOCK), 1)
    sides = [block_ref[pl.ds(SUB * t, SUB), :] for t in range(tiles_count)]
    inverses = [(lane == row_in_tile + SUB * t).astype(f32) for t in range(tiles_count)]
    uppers = []
    for step in range(tiles_count):
        base = SUB * step
        side, inverse = sides[step], inverses[step]
        columns = [lanes(side, base + b) for b in range(SUB)]
        entry = {(a, b): sublanes(columns[b], a) for b in range(SUB) for a in range(b, SUB)}
        ahead = [lanes(sides[step + 1], base + b) for b in range(SUB)] if step + 1 < tiles_count else None
        tops = [sublanes(side, a) for a in range(SUB)]
        insides = [sublanes(inverse, a) for a in range(SUB)]
        scale = []
        for m in range(SUB):
            root = lax.rsqrt(entry[m, m])
            scale.append(root)
            for a in range(m + 1, SUB):
                entry[a, m] = entry[a, m] * root
            for b in range(m + 1, SUB):
                for a in range(b, SUB):
                    entry[a, b] = entry[a, b] - entry[a, m] * entry[b, m]
            tops[m] = tops[m] * root
            insides[m] = insides[m] * root
            for a in range(m + 1, SUB):
                tops[a] = tops[a] - entry[a, m] * tops[m]
                insides[a] = insides[a] - entry[a, m] * insides[m]
            if ahead is not None:
                ahead[m] = ahead[m] * root
                for b in range(m + 1, SUB):
                    ahead[b] = ahead[b] - entry[b, m] * ahead[m]
        upper, lower_inverse = tops[0], insides[0]
        for m in range(1, SUB):
            upper = jnp.where(row_in_tile == m, tops[m], upper)
            lower_inverse = jnp.where(row_in_tile == m, insides[m], lower_inverse)
        uppers.append(jnp.where(lane >= row_in_tile + base, upper, 0.0))
        inverse_ref[pl.ds(base, SUB), :] = lower_inverse
        if ahead is not None:
            for m in range(SUB):
                sides[step + 1] = sides[step + 1] - ahead[m] * tops[m]
                inverses[step + 1] = inverses[step + 1] - ahead[m] * insides[m]
        if step + 2 < tiles_count:
            weights_top, weights_in = [None] * SUB, [None] * SUB
            for m in reversed(range(SUB)):
                top, inside = tops[m], insides[m]
                for b in range(m + 1, SUB):
                    top = top - entry[b, m] * weights_top[b]
                    inside = inside - entry[b, m] * weights_in[b]
                weights_top[m], weights_in[m] = top * scale[m], inside * scale[m]
            for t in range(step + 2, tiles_count):
                for m in range(SUB):
                    column = lanes(sides[t], base + m)
                    if m == 0:
                        top_sum, in_sum = column * weights_top[m], column * weights_in[m]
                    else:
                        top_sum = top_sum + column * weights_top[m]
                        in_sum = in_sum + column * weights_in[m]
                sides[t] = sides[t] - top_sum
                inverses[t] = inverses[t] - in_sum
    block_ref[...] = jnp.concatenate(uppers, 0).T


def place_pieces(place_ref, first, pieces, helds, sem):
    waits = []
    for i, (piece, held_ref) in enumerate(zip(pieces, helds)):
        rows, users = piece.shape
        row = place_ref[first + 2 * i]
        user = pl.multiple_of(place_ref[first + 2 * i + 1], users)
        to = held_ref.at[pl.ds(pl.multiple_of(jnp.maximum(row, 0), rows), rows), pl.ds(user, users)]
        copy = pltpu.make_async_copy(piece, to, sem.at[i])
        pl.when(row >= 0)(copy.start)
        waits.append(functools.partial(pl.when(row >= 0), copy.wait))
    return waits


def panel_kernel(views, count, width, place_ref, *refs):
    pieces, refs = refs[:count], refs[count:]
    outs, (high_ref, low_ref, inv_high_ref, inv_low_ref, lower_ref, block_ref, inverse_ref, items_ref, parts_ref, sem, out_sem) = refs[:4], refs[4:]
    held = [parts_ref if is_part else items_ref for _, _, _, is_part in views]
    views = [pieces[which].at[pl.ds(start, rows)] for which, start, rows, _ in views]
    for wait in place_pieces(place_ref, 0, views, held, sem):
        wait()
    on_diagonal = lax.broadcasted_iota(jnp.int32, (BLOCK, BLOCK), 0) == lax.broadcasted_iota(
        jnp.int32, (BLOCK, BLOCK), 1
    )

    def before(k):
        start = k * BLOCK
        here = pl.ds(start, BLOCK)
        column = dot_nt(items_ref[pl.ds(start, PANEL - start), :], items_ref[here, :])
        if k > 0:
            high, low = high_ref[pl.ds(start, PANEL - start), :start], low_ref[pl.ds(start, PANEL - start), :start]
            column = column - dot_nt3((high, low), (high[:BLOCK], low[:BLOCK]))
        part, lane = PARTS * (start // width), start % width
        parts = parts_ref[pl.ds(part, PARTS), pl.ds(lane, BLOCK)].astype(f32)
        regular = parts[0:1] + parts[1:2] + parts[2:3]
        block_ref[...] = column[:BLOCK] + jnp.where(on_diagonal, regular, 0.0)
        if k + 1 < NBLOCKS:
            lower_ref[pl.ds(start + BLOCK, PANEL - start - BLOCK), :] = column[BLOCK:]

    def after(k):
        start = k * BLOCK
        here = pl.ds(start, BLOCK)
        diagonal = block_ref[...]
        inverse = split(inverse_ref[...])
        inv_high_ref[here, :], inv_low_ref[here, :] = inverse
        high_ref[here, here], low_ref[here, here] = split(diagonal)
        if k > 0:
            above = jnp.zeros((start, BLOCK), bf16)
            high_ref[pl.ds(0, start), here], low_ref[pl.ds(0, start), here] = above, above
        if k + 1 < NBLOCKS:
            rest = pl.ds(start + BLOCK, PANEL - start - BLOCK)
            high_ref[rest, here], low_ref[rest, here] = split(dot_nt3(split(lower_ref[rest, :]), inverse))

    def leave(k):
        column = pl.ds(k * BLOCK, BLOCK)
        return [
            pltpu.make_async_copy(high_ref.at[:, column], outs[0].at[:, column], out_sem.at[0, k]),
            pltpu.make_async_copy(low_ref.at[:, column], outs[1].at[:, column], out_sem.at[1, k]),
            pltpu.make_async_copy(inv_high_ref.at[column, :], outs[2].at[column, :], out_sem.at[2, k]),
            pltpu.make_async_copy(inv_low_ref.at[column, :], outs[3].at[column, :], out_sem.at[3, k]),
        ]

    before(0)

    def turn(k, carry):
        factor_block(block_ref, inverse_ref)
        for which in range(NBLOCKS):

            @pl.when(k == which)
            def _():
                after(which)
                for copy in leave(which):
                    copy.start()
                if which + 1 < NBLOCKS:
                    before(which + 1)

        return carry

    lax.fori_loop(0, NBLOCKS, turn, 0)
    for k in range(NBLOCKS):
        for copy in leave(k):
            copy.wait()


def room(*arrays):
    return sum(math.prod(shape) * jnp.dtype(dtype).itemsize for shape, dtype in arrays) + 8 * 2**20


def factor_panel(place, pieces, views, width, users):
    outs = [
        ((PANEL, PANEL), bf16),
        ((PANEL, PANEL), bf16),
        ((PANEL, BLOCK), bf16),
        ((PANEL, BLOCK), bf16),
    ]
    held = [
        ((PANEL, BLOCK), f32),
        ((BLOCK, BLOCK), f32),
        ((BLOCK, BLOCK), f32),
        ((PANEL, users), bf16),
        ((PANEL // width * PARTS, users), bf16),
    ]
    return pl.pallas_call(
        functools.partial(panel_kernel, views, len(pieces), width),
        out_shape=[pltpu.HBM(*out) for out in outs],
        in_specs=[pl.BlockSpec(memory_space=pltpu.SMEM)]
        + [pl.BlockSpec(memory_space=pl.ANY)] * len(pieces),
        out_specs=[pl.BlockSpec(memory_space=pltpu.HBM)] * len(outs),
        scratch_shapes=[VMEM(*one) for one in outs + held]
        + [pltpu.SemaphoreType.DMA((len(views),)), pltpu.SemaphoreType.DMA((len(outs), NBLOCKS))],
        compiler_params=pltpu.CompilerParams(vmem_limit_bytes=room(*outs, *held)),
        cost_estimate=pl.CostEstimate(flops=4 * 10**10, bytes_accessed=16 * 2**20, transcendentals=1024),
        name="factor_panel",
    )(place, *pieces)


def tile_kernel(counts, views, place_ref, regular_ref, *refs):
    factors, refs = refs[:4], refs[4:]
    pieces, refs = refs[: sum(counts)], refs[sum(counts) :]
    out_ref, refs = refs[0], refs[1:]
    high_ref, low_ref, inv_high_ref, inv_low_ref, left_high_ref, left_low_ref, wide_high_ref, wide_low_ref = refs[:8]
    panel_ref, rows_ref, cols_ref, sem, factor_sem = refs[8:]
    targets = [panel_ref] * counts[0] + [rows_ref] * counts[1] + [cols_ref] * counts[2]
    held = [targets[which] for which, *_ in views]
    views = [pieces[which].at[pl.ds(start, rows)] for which, start, rows in views]
    fetches = [
        pltpu.make_async_copy(factor, ref, factor_sem.at[i])
        for i, (factor, ref) in enumerate(zip(factors, (high_ref, low_ref, inv_high_ref, inv_low_ref)))
    ]
    for fetch in fetches:
        fetch.start()
    waits = place_pieces(place_ref, 2, views, held, sem)
    for fetch in fetches:
        fetch.wait()
    row_index, col_index = place_ref[0], place_ref[1]
    width, band = cols_ref.shape[0], rows_ref.shape[0] // (SPAN - 1)
    row_count = (SPAN - 1) * band
    panel_blocks = PANEL // width
    in_panel = col_index < panel_blocks
    slot = jnp.minimum(col_index, panel_blocks - 1)
    at = pl.ds(pl.multiple_of(slot * width, width), width)
    below, right = pl.ds(0, row_count), pl.ds(row_count, width)

    for start in range(0, PANEL, WIDE):
        first, second = pl.ds(start, BLOCK), pl.ds(start + BLOCK, BLOCK)
        between = dot_nn3((high_ref[second, first], low_ref[second, first]), (inv_high_ref[first, :], inv_low_ref[first, :]))
        corner = split(-dot_nn3((inv_high_ref[second, :], inv_low_ref[second, :]), split(between)))
        for wide_ref, inv_ref, part in ((wide_high_ref, inv_high_ref, corner[0]), (wide_low_ref, inv_low_ref, corner[1])):
            wide_ref[first, pl.ds(0, BLOCK)] = inv_ref[first, :]
            wide_ref[first, pl.ds(BLOCK, BLOCK)] = jnp.zeros((BLOCK, BLOCK), bf16)
            wide_ref[second, pl.ds(0, BLOCK)] = part
            wide_ref[second, pl.ds(BLOCK, BLOCK)] = inv_ref[second, :]

    def solve(items_ref, mine):
        for start in range(0, PANEL, WIDE):
            here = pl.ds(start, WIDE)
            column = dot_nt(items_ref[...], panel_ref[here, :])
            if start > 0:
                column = column - dot_nt3(
                    (left_high_ref[mine, :start], left_low_ref[mine, :start]), (high_ref[here, :start], low_ref[here, :start])
                )
            column = dot_nt3(split(column), (wide_high_ref[here, :], wide_low_ref[here, :]))
            left_high_ref[mine, here], left_low_ref[mine, here] = split(column)

    for wait, target in zip(waits, held):
        if target is not rows_ref:
            wait()
    solve(cols_ref, right)
    for wait, target in zip(waits, held):
        if target is rows_ref:
            wait()
    solve(rows_ref, below)

    @pl.when(in_panel)
    def _():
        mine = pl.ds(pl.multiple_of(row_index * band, band), band)
        out_ref[pl.ds(0, band), :] = high_ref[mine, at].astype(f32) + low_ref[mine, at].astype(f32)
        out_ref[pl.ds(band, row_count), :] = left_high_ref[below, at].astype(f32) + left_low_ref[below, at].astype(f32)

    @pl.when(jnp.logical_not(in_panel))
    def _():
        out_ref[pl.ds(0, band), :] = jnp.zeros((band, width), f32)
        items = lax.broadcasted_iota(jnp.int32, (band, width), 0) + row_index * band
        columns = lax.broadcasted_iota(jnp.int32, (band, width), 1) + col_index * width
        for part in range(SPAN - 1):
            mine = pl.ds(part * band, band)
            tile = dot_nt(rows_ref[mine, :], cols_ref[...])
            tile = tile + jnp.where(items + (part + 1) * PANEL == columns, regular_ref[...], 0.0)
            out_ref[pl.ds((part + 1) * band, band), :] = tile - dot_nt3(
                (left_high_ref[mine, :], left_low_ref[mine, :]), (left_high_ref[right, :], left_low_ref[right, :])
            )


def finish_tile(place, regular, factors, panel, rows, cols, views, band, users):
    spec = pl.BlockSpec(memory_space=VMEM)
    width = regular.shape[1]
    factors = [pltpu.with_memory_space_constraint(x, pltpu.HBM) for x in factors]
    pieces = panel + rows + cols
    out = ((SPAN * band, width), f32)
    below = (SPAN - 1) * band + width
    held = [
        ((below, PANEL), bf16),
        ((below, PANEL), bf16),
        ((PANEL, WIDE), bf16),
        ((PANEL, WIDE), bf16),
        ((PANEL, users), bf16),
        (((SPAN - 1) * band, users), bf16),
        ((width, users), bf16),
    ]
    return pl.pallas_call(
        functools.partial(tile_kernel, (len(panel), len(rows), len(cols)), views),
        out_shape=jax.ShapeDtypeStruct(*out),
        in_specs=[pl.BlockSpec(memory_space=pltpu.SMEM)]
        + [spec]
        + [pl.BlockSpec(memory_space=pltpu.HBM)] * len(factors)
        + [pl.BlockSpec(memory_space=pl.ANY)] * len(pieces),
        out_specs=spec,
        scratch_shapes=[VMEM(factor.shape, factor.dtype) for factor in factors]
        + [VMEM(*one) for one in held]
        + [pltpu.SemaphoreType.DMA((len(views),)), pltpu.SemaphoreType.DMA((len(factors),))],
        compiler_params=pltpu.CompilerParams(vmem_limit_bytes=room(out, *held, *((factor.shape, factor.dtype) for factor in factors))),
        cost_estimate=pl.CostEstimate(flops=20 * 10**9, bytes_accessed=24 * 2**20, transcendentals=0),
        name="finish_tile",
    )(place, regular, *factors, *pieces)


CORES = 2


def body(interactions, regular):
    row_count, col_count = lax.axis_size("row"), lax.axis_size("col")
    row_index, col_index = lax.axis_index("row"), lax.axis_index("col")
    width, users = interactions.shape
    band = PANEL // row_count
    ways = PANEL // width
    assert row_count == CORES * ways and col_count == SPAN * ways and users >= width
    slot, way = col_index // ways, col_index % ways
    pair, core = row_index // CORES, row_index % CORES
    all_users = row_count * users

    def exchange(value, move, only=None):
        perm = []
        for source_row in range(row_count):
            for source_col in range(col_count):
                place = (source_row // CORES, source_row % CORES, source_col // ways, source_col % ways)
                if only is None or only(*place):
                    to = move(*place)
                    target = (to[0] * CORES + to[1]) * col_count + to[2] * ways + to[3]
                    perm.append((source_row * col_count + source_col, target))
        return lax.ppermute(value, ("row", "col"), perm)

    def after(value, *others):
        return lax.optimization_barrier((value, *others))[0]

    high = lax.reduce_precision(regular, 8, 7)
    middle = lax.reduce_precision(regular - high, 8, 7)
    parts = jnp.stack([high, middle, regular - high - middle]).astype(bf16)
    parts = jnp.pad(parts, ((0, PARTS - 3), (0, users - width)))

    halves = interactions.reshape(CORES, band, users)
    offers = [lax.dynamic_index_in_dim(halves, core ^ flip, 0, False) for flip in range(CORES)]

    half = width // 2
    shared = jnp.concatenate([interactions, parts], 0)
    quarters, quarter_users = [], []
    reach = SPAN // 2
    while reach:
        got = exchange(
            shared, lambda p, h, s, w: (p, h, s + reach, w), lambda p, h, s, w: s % (2 * reach) == 0
        )
        if reach == SPAN // 2:
            for turn in reversed(range(ways)):
                for flip in range(CORES):
                    quarters.append(
                        exchange(offers[flip], lambda p, h, s, w: (w, h ^ flip, s, (p + turn) % ways))
                    )
                    quarter_users.append(((way - turn) % ways * CORES + (core ^ flip)) * users)
            got = after(got, *quarters[:CORES])
        shared = jnp.where(slot % (2 * reach) == reach, got, shared)
        reach //= 2
    quarters = jnp.concatenate(quarters, 0)

    def numbers(values):
        return jnp.stack([jnp.asarray(v, jnp.int32) for v in values])

    panel, panel_views, panel_place, part_views, part_place = [], [], [], [], []
    cols, cols_place = [interactions], [0, row_index * users]
    rows, rows_views, rows_place = [], [], []

    def over_core(value):
        return exchange(value, lambda p, h, s, w: (p, 1 - h, s, w))

    def over_pair(value):
        return exchange(value, lambda p, h, s, w: (1 - p, h, s, w))

    def over_way(value, only=None):
        return exchange(value, lambda p, h, s, w: (p, h, s, 1 - w), only)

    if ways == 2:
        twin_items = over_core(interactions)
        shared = after(shared, quarters, twin_items)
        pair_side, way_side = over_pair(shared), over_way(shared)
        own_twin = over_core(shared)
        diagonal = [over_way(after(pair_side, own_twin)[:half]), over_pair(after(way_side, own_twin)[half:])]
        for from_pair, from_way, first_row, piece in (
            (pair, way, 0, shared),
            (1 - pair, way, 0, pair_side),
            (pair, 1 - way, 0, way_side),
            (1 - pair, 1 - way, 0, diagonal[0]),
            (1 - pair, 1 - way, half, diagonal[1]),
        ):
            twin = own_twin if piece is shared else over_core(piece)
            for from_core, value in ((core, piece), (1 - core, twin)):
                if value is shared or value is way_side:
                    part_views.append((len(panel), width, PARTS, True))
                    part_place += [from_way * PARTS, 0]
                count = min(value.shape[0], half if value.shape[0] < width else width)
                panel_views.append((len(panel), 0, count, False))
                panel_place += [from_way * width + first_row, (from_pair * CORES + from_core) * users]
                panel.append(value)
        crossed = [pair_side, way_side, *diagonal]
        held = after(interactions, *crossed)
        cols += [twin_items, over_pair(held), exchange(held, lambda p, h, s, w: (1 - p, 1 - h, s, w))]
        cols_place += [0, (row_index ^ 1) * users, 0, (row_index ^ 2) * users, 0, (row_index ^ 3) * users]
        first = exchange(quarters, lambda p, h, s, w: (p, h, s - 1, w), lambda p, h, s, w: s > 0)
        relayed, ready = lax.optimization_barrier((first, quarters, *crossed))[:2]
        second = exchange(relayed, lambda p, h, s, w: (p, h, s - 1, w), lambda p, h, s, w: 0 < s < SPAN - 1)
        ring = exchange(ready, lambda p, h, s, w: (p, h, (s + 1) % SPAN, w), lambda p, h, s, w: s > 0)
        leap = exchange(ready, lambda p, h, s, w: (p, h, s + 2, w), lambda p, h, s, w: s == 1)
        rows = [quarters, first, second, ring, leap]
        from_slots = [
            slot,
            jnp.where(slot < 3, slot + 1, 0),
            jnp.where(slot < 2, slot + 2, 0),
            jnp.where(slot == 1, 0, (slot + 3) % SPAN),
            jnp.where(slot == 3, 1, 0),
        ]
        for from_slot, piece in enumerate(rows):
            for which, from_users in enumerate(quarter_users):
                rows_views.append((from_slot, which * band, band))
                rows_place += [(from_slots[from_slot] - 1) * band, from_users]
    else:
        groups = [[s * ways + w for w in range(ways)] for s in range(SPAN)]
        shared = lax.all_gather(shared, "col", axis=0, axis_index_groups=groups)
        parts = shared[:, width:].reshape(ways * PARTS, users)
        shared = shared[:, :width].reshape(PANEL, users)
        panel, panel_place = [lax.all_gather(shared, "row", axis=1, tiled=True), parts], [0, 0]
        panel_views = [(0, 0, PANEL, False)]
        part_views, part_place = [(1, 0, ways * PARTS, True)], [0, 0]
        cols, cols_place = [lax.all_gather(interactions, "row", axis=1, tiled=True)], [0, 0]
        groups = [[s * ways + w for s in range(SPAN)] for w in range(ways)]
        rows = [lax.all_gather(quarters, "col", axis=0, tiled=True, axis_index_groups=groups)]
        for from_slot in range(1, SPAN):
            for which, from_users in enumerate(quarter_users):
                rows_views.append((0, (from_slot * len(quarter_users) + which) * band, band))
                rows_place += [(from_slot - 1) * band, from_users]

    factors = factor_panel(
        numbers(panel_place + part_place), panel, panel_views + part_views, width, all_users
    )
    views = [view[:3] for view in panel_views]
    views += [(len(panel) + i, start, count) for i, start, count in rows_views]
    views += [(len(panel) + len(rows) + i, 0, width) for i in range(len(cols))]
    tile = finish_tile(
        numbers([row_index, col_index] + panel_place + rows_place + cols_place),
        regular[None, :], factors, panel, rows, cols, views, band, all_users,
    )
    return tile.reshape(SPAN, band, width)


def solution(mesh):
    return jax.shard_map(
        body,
        mesh=mesh,
        in_specs=(P("col", "row"), P("col")),
        out_specs=P(None, "row", "col"),
        check_vma=False,
    )
```

```python
import functools
import math
import jax
import jax.numpy as jnp
from jax import lax
from jax.experimental import pallas as pl
from jax.experimental.pallas import tpu as pltpu
from jax.sharding import PartitionSpec as P

PANEL = 1024
SPAN = 4
BLOCK = 128
WIDE = 256
SUB = 8
NBLOCKS = PANEL // BLOCK
PARTS = 16
VMEM = pltpu.VMEM
f32 = jnp.float32
bf16 = jnp.bfloat16


def dot_nt(a, b):
    return lax.dot_general(a, b, (((1,), (1,)), ((), ())), preferred_element_type=f32)


def split(value):
    high = value.astype(bf16)
    return high, (value - high.astype(f32)).astype(bf16)


def dot_nt3(a, b):
    return dot_nt(a[0], b[0]) + (dot_nt(a[0], b[1]) + dot_nt(a[1], b[0]))


def dot_nn3(a, b):
    def dot(x, y):
        return jnp.dot(x, y, preferred_element_type=f32)

    return dot(a[0], b[0]) + (dot(a[0], b[1]) + dot(a[1], b[0]))


def lanes(value, lane):
    return jnp.broadcast_to(value[:, lane : lane + 1], (SUB, BLOCK))


def sublanes(value, row):
    return jnp.broadcast_to(value[row : row + 1, :], (SUB, BLOCK))


def factor_block(block_ref, inverse_ref):
    tiles_count = BLOCK // SUB
    row_in_tile = lax.broadcasted_iota(jnp.int32, (SUB, BLOCK), 0)
    lane = lax.broadcasted_iota(jnp.int32, (SUB, BLOCK), 1)
    sides = [block_ref[pl.ds(SUB * t, SUB), :] for t in range(tiles_count)]
    inverses = [(lane == row_in_tile + SUB * t).astype(f32) for t in range(tiles_count)]
    uppers = []
    for step in range(tiles_count):
        base = SUB * step
        side, inverse = sides[step], inverses[step]
        columns = [lanes(side, base + b) for b in range(SUB)]
        entry = {(a, b): sublanes(columns[b], a) for b in range(SUB) for a in range(b, SUB)}
        vectors = [[sublanes(side, a) for a in range(SUB)], [sublanes(inverse, a) for a in range(SUB)]]
        if step + 1 < tiles_count:
            vectors.append([lanes(sides[step + 1], base + b) for b in range(SUB)])
        scale = [None] * SUB
        for m in range(0, SUB, 2):
            n = m + 1
            first, cross, second = entry[m, m], entry[n, m], entry[n, n]
            root = lax.rsqrt(first)
            det_root = lax.rsqrt(first * second - cross * cross)
            scale[m], scale[n] = root, det_root * (first * root)
            det_square = det_root * det_root
            link = cross * root
            entry[n, m] = link
            rest = range(n + 1, SUB)
            for x in rest:
                entry[x, m] = entry[x, m] * root
                entry[x, n] = entry[x, n] - entry[x, m] * link
            weighted = {x: entry[x, n] * first for x in rest}
            for y in rest:
                for x in range(y, SUB):
                    entry[x, y] = (entry[x, y] - entry[x, m] * entry[y, m]) - (weighted[x] * entry[y, n]) * det_square
            for x in rest:
                entry[x, n] = entry[x, n] * scale[n]
            for vector in vectors:
                vector[m] = vector[m] * root
                vector[n] = (vector[n] - link * vector[m]) * scale[n]
                for x in rest:
                    vector[x] = (vector[x] - entry[x, m] * vector[m]) - entry[x, n] * vector[n]
        tops, insides = vectors[:2]
        upper, lower_inverse = tops[0], insides[0]
        for m in range(1, SUB):
            upper = jnp.where(row_in_tile == m, tops[m], upper)
            lower_inverse = jnp.where(row_in_tile == m, insides[m], lower_inverse)
        uppers.append(jnp.where(lane >= row_in_tile + base, upper, 0.0))
        inverse_ref[pl.ds(base, SUB), :] = lower_inverse
        if step + 1 < tiles_count:
            ahead = vectors[2]
            for m in range(SUB):
                sides[step + 1] = sides[step + 1] - ahead[m] * tops[m]
                inverses[step + 1] = inverses[step + 1] - ahead[m] * insides[m]
        if step + 2 < tiles_count:
            weights_top, weights_in = [None] * SUB, [None] * SUB
            for m in reversed(range(SUB)):
                top, inside = tops[m], insides[m]
                for b in range(m + 1, SUB):
                    top = top - entry[b, m] * weights_top[b]
                    inside = inside - entry[b, m] * weights_in[b]
                weights_top[m], weights_in[m] = top * scale[m], inside * scale[m]
            for t in range(step + 2, tiles_count):
                for m in range(SUB):
                    column = lanes(sides[t], base + m)
                    if m == 0:
                        top_sum, in_sum = column * weights_top[m], column * weights_in[m]
                    else:
                        top_sum = top_sum + column * weights_top[m]
                        in_sum = in_sum + column * weights_in[m]
                sides[t] = sides[t] - top_sum
                inverses[t] = inverses[t] - in_sum
    block_ref[...] = jnp.concatenate(uppers, 0).T


def place_pieces(place_ref, first, pieces, helds, sem):
    waits = []
    for i, (piece, held_ref) in enumerate(zip(pieces, helds)):
        rows, users = piece.shape
        row = place_ref[first + 2 * i]
        user = pl.multiple_of(place_ref[first + 2 * i + 1], users)
        to = held_ref.at[pl.ds(pl.multiple_of(jnp.maximum(row, 0), rows), rows), pl.ds(user, users)]
        copy = pltpu.make_async_copy(piece, to, sem.at[i])
        pl.when(row >= 0)(copy.start)
        waits.append(functools.partial(pl.when(row >= 0), copy.wait))
    return waits


def panel_kernel(views, count, width, place_ref, *refs):
    pieces, refs = refs[:count], refs[count:]
    outs, (high_ref, low_ref, inv_high_ref, inv_low_ref, lower_ref, coming_ref, *refs) = refs[:4], refs[4:]
    block_ref, inverse_ref, items_ref, parts_ref, sem, out_sem = refs
    held = [parts_ref if is_part else items_ref for _, _, _, is_part in views]
    views = [pieces[which].at[pl.ds(start, rows)] for which, start, rows, _ in views]
    waits = place_pieces(place_ref, 0, views, held, sem)
    for k in range(1, NBLOCKS):
        for ref in (high_ref, low_ref):
            ref[pl.ds(0, k * BLOCK), pl.ds(k * BLOCK, BLOCK)] = jnp.zeros((k * BLOCK, BLOCK), bf16)
    for wait in waits:
        wait()
    on_diagonal = lax.broadcasted_iota(jnp.int32, (BLOCK, BLOCK), 0) == lax.broadcasted_iota(
        jnp.int32, (BLOCK, BLOCK), 1
    )

    def before(k):
        start = k * BLOCK
        here, rest = pl.ds(start, BLOCK), pl.ds(start, PANEL - start)
        if k % 2 == 0:
            both = pl.ds(start, 2 * BLOCK)
            columns = dot_nt(items_ref[rest, :], items_ref[both, :])
            if k > 0:
                columns = columns - dot_nt3(
                    (high_ref[rest, :start], low_ref[rest, :start]), (high_ref[both, :start], low_ref[both, :start])
                )
            column = columns[:, :BLOCK]
            coming_ref[pl.ds(start + BLOCK, PANEL - start - BLOCK), :] = columns[BLOCK:, BLOCK:]
        else:
            last = pl.ds(start - BLOCK, BLOCK)
            high, low = high_ref[rest, last], low_ref[rest, last]
            column = coming_ref[rest, :] - dot_nt3((high, low), (high[:BLOCK], low[:BLOCK]))
        part, lane = PARTS * (start // width), start % width
        parts = parts_ref[pl.ds(part, PARTS), pl.ds(lane, BLOCK)].astype(f32)
        block_ref[...] = column[:BLOCK] + jnp.where(on_diagonal, parts[0:1] + parts[1:2] + parts[2:3], 0.0)
        if k + 1 < NBLOCKS:
            lower_ref[pl.ds(start + BLOCK, PANEL - start - BLOCK), :] = column[BLOCK:]

    def after(k):
        start = k * BLOCK
        here = pl.ds(start, BLOCK)
        inverse = split(inverse_ref[...])
        inv_high_ref[here, :], inv_low_ref[here, :] = inverse
        high_ref[here, here], low_ref[here, here] = split(block_ref[...])
        if k + 1 < NBLOCKS:
            rest = pl.ds(start + BLOCK, PANEL - start - BLOCK)
            high_ref[rest, here], low_ref[rest, here] = split(dot_nt3(split(lower_ref[rest, :]), inverse))

    def leave(k):
        column = pl.ds(k * BLOCK, BLOCK)
        return [
            pltpu.make_async_copy(high_ref.at[:, column], outs[0].at[:, column], out_sem.at[0, k]),
            pltpu.make_async_copy(low_ref.at[:, column], outs[1].at[:, column], out_sem.at[1, k]),
            pltpu.make_async_copy(inv_high_ref.at[column, :], outs[2].at[column, :], out_sem.at[2, k]),
            pltpu.make_async_copy(inv_low_ref.at[column, :], outs[3].at[column, :], out_sem.at[3, k]),
        ]

    before(0)

    def turn(k, carry):
        factor_block(block_ref, inverse_ref)
        for which in range(NBLOCKS):

            @pl.when(k == which)
            def _():
                after(which)
                for copy in leave(which):
                    copy.start()
                if which + 1 < NBLOCKS:
                    before(which + 1)

        return carry

    lax.fori_loop(0, NBLOCKS, turn, 0)
    for k in range(NBLOCKS):
        for copy in leave(k):
            copy.wait()


def room(*arrays):
    return sum(math.prod(shape) * jnp.dtype(dtype).itemsize for shape, dtype in arrays) + 8 * 2**20


def factor_panel(place, pieces, views, width, users):
    outs = [
        ((PANEL, PANEL), bf16),
        ((PANEL, PANEL), bf16),
        ((PANEL, BLOCK), bf16),
        ((PANEL, BLOCK), bf16),
    ]
    held = [
        ((PANEL, BLOCK), f32),
        ((PANEL, BLOCK), f32),
        ((BLOCK, BLOCK), f32),
        ((BLOCK, BLOCK), f32),
        ((PANEL, users), bf16),
        ((PANEL // width * PARTS, users), bf16),
    ]
    return pl.pallas_call(
        functools.partial(panel_kernel, views, len(pieces), width),
        out_shape=[pltpu.HBM(*out) for out in outs],
        in_specs=[pl.BlockSpec(memory_space=pltpu.SMEM)]
        + [pl.BlockSpec(memory_space=pl.ANY)] * len(pieces),
        out_specs=[pl.BlockSpec(memory_space=pltpu.HBM)] * len(outs),
        scratch_shapes=[VMEM(*one) for one in outs + held]
        + [pltpu.SemaphoreType.DMA((len(views),)), pltpu.SemaphoreType.DMA((len(outs), NBLOCKS))],
        compiler_params=pltpu.CompilerParams(vmem_limit_bytes=room(*outs, *held)),
        cost_estimate=pl.CostEstimate(flops=4 * 10**10, bytes_accessed=16 * 2**20, transcendentals=1024),
        name="factor_panel",
    )(place, *pieces)


def tile_kernel(counts, views, place_ref, regular_ref, *refs):
    factors, refs = refs[:4], refs[4:]
    pieces, refs = refs[: sum(counts)], refs[sum(counts) :]
    out_ref, refs = refs[0], refs[1:]
    high_ref, low_ref, inv_high_ref, inv_low_ref, left_high_ref, left_low_ref, wide_high_ref, wide_low_ref = refs[:8]
    panel_ref, rows_ref, cols_ref, sem, factor_sem = refs[8:]
    targets = [panel_ref] * counts[0] + [rows_ref] * counts[1] + [cols_ref] * counts[2]
    held = [targets[which] for which, *_ in views]
    views = [pieces[which].at[pl.ds(start, rows)] for which, start, rows in views]
    fetches = [
        pltpu.make_async_copy(factor, ref, factor_sem.at[i])
        for i, (factor, ref) in enumerate(zip(factors, (high_ref, low_ref, inv_high_ref, inv_low_ref)))
    ]
    for fetch in fetches:
        fetch.start()
    waits = place_pieces(place_ref, 2, views, held, sem)
    row_index, col_index = place_ref[0], place_ref[1]
    width, band = cols_ref.shape[0], rows_ref.shape[0] // (SPAN - 1)
    row_count = (SPAN - 1) * band
    panel_blocks = PANEL // width
    in_panel = col_index < panel_blocks
    slot = jnp.minimum(col_index, panel_blocks - 1)
    at = pl.ds(pl.multiple_of(slot * width, width), width)
    below, right = pl.ds(0, row_count), pl.ds(row_count, width)

    for wait in waits:
        wait()
    step = min(WIDE, width)
    groups = [(cols_ref, at_row, pl.ds(row_count + at_row, step), step) for at_row in range(0, width, step)]
    groups += [(rows_ref, at_row, pl.ds(at_row, band), band) for at_row in range(0, row_count, band)]

    def grams(start):
        block = panel_ref[pl.ds(start, WIDE), :]
        return [dot_nt(ref[pl.ds(at_row, count), :], block) for ref, at_row, _, count in groups]

    columns = grams(0)
    for fetch in fetches:
        fetch.wait()

    for start in range(0, PANEL, WIDE):
        first, second = pl.ds(start, BLOCK), pl.ds(start + BLOCK, BLOCK)
        between = dot_nn3((high_ref[second, first], low_ref[second, first]), (inv_high_ref[first, :], inv_low_ref[first, :]))
        corner = split(-dot_nn3((inv_high_ref[second, :], inv_low_ref[second, :]), split(between)))
        for wide_ref, inv_ref, part in ((wide_high_ref, inv_high_ref, corner[0]), (wide_low_ref, inv_low_ref, corner[1])):
            wide_ref[first, pl.ds(0, BLOCK)] = inv_ref[first, :]
            wide_ref[first, pl.ds(BLOCK, BLOCK)] = jnp.zeros((BLOCK, BLOCK), bf16)
            wide_ref[second, pl.ds(0, BLOCK)] = part
            wide_ref[second, pl.ds(BLOCK, BLOCK)] = inv_ref[second, :]

    for start in range(0, PANEL, WIDE):
        here = pl.ds(start, WIDE)
        if start > 0:
            columns = [
                column
                - dot_nt3(
                    (left_high_ref[mine, :start], left_low_ref[mine, :start]), (high_ref[here, :start], low_ref[here, :start])
                )
                for column, (_, _, mine, _) in zip(grams(start), groups)
            ]
        for column, (_, _, mine, _) in zip(columns, groups):
            column = dot_nt3(split(column), (wide_high_ref[here, :], wide_low_ref[here, :]))
            left_high_ref[mine, here], left_low_ref[mine, here] = split(column)

    @pl.when(in_panel)
    def _():
        mine = pl.ds(pl.multiple_of(row_index * band, band), band)
        out_ref[pl.ds(0, band), :] = high_ref[mine, at].astype(f32) + low_ref[mine, at].astype(f32)
        out_ref[pl.ds(band, row_count), :] = left_high_ref[below, at].astype(f32) + left_low_ref[below, at].astype(f32)

    @pl.when(jnp.logical_not(in_panel))
    def _():
        out_ref[pl.ds(0, band), :] = jnp.zeros((band, width), f32)
        items = lax.broadcasted_iota(jnp.int32, (band, width), 0) + row_index * band
        columns = lax.broadcasted_iota(jnp.int32, (band, width), 1) + col_index * width
        for part in range(SPAN - 1):
            mine = pl.ds(part * band, band)
            tile = dot_nt(rows_ref[mine, :], cols_ref[...])
            tile = tile + jnp.where(items + (part + 1) * PANEL == columns, regular_ref[...], 0.0)
            out_ref[pl.ds((part + 1) * band, band), :] = tile - dot_nt3(
                (left_high_ref[mine, :], left_low_ref[mine, :]), (left_high_ref[right, :], left_low_ref[right, :])
            )


def finish_tile(place, regular, factors, panel, rows, cols, views, band, users):
    spec = pl.BlockSpec(memory_space=VMEM)
    width = regular.shape[1]
    factors = [pltpu.with_memory_space_constraint(x, pltpu.HBM) for x in factors]
    pieces = panel + rows + cols
    out = ((SPAN * band, width), f32)
    below = (SPAN - 1) * band + width
    held = [
        ((below, PANEL), bf16),
        ((below, PANEL), bf16),
        ((PANEL, WIDE), bf16),
        ((PANEL, WIDE), bf16),
        ((PANEL, users), bf16),
        (((SPAN - 1) * band, users), bf16),
        ((width, users), bf16),
    ]
    return pl.pallas_call(
        functools.partial(tile_kernel, (len(panel), len(rows), len(cols)), views),
        out_shape=jax.ShapeDtypeStruct(*out),
        in_specs=[pl.BlockSpec(memory_space=pltpu.SMEM)]
        + [spec]
        + [pl.BlockSpec(memory_space=pltpu.HBM)] * len(factors)
        + [pl.BlockSpec(memory_space=pl.ANY)] * len(pieces),
        out_specs=spec,
        scratch_shapes=[VMEM(factor.shape, factor.dtype) for factor in factors]
        + [VMEM(*one) for one in held]
        + [pltpu.SemaphoreType.DMA((len(views),)), pltpu.SemaphoreType.DMA((len(factors),))],
        compiler_params=pltpu.CompilerParams(vmem_limit_bytes=room(out, *held, *((factor.shape, factor.dtype) for factor in factors))),
        cost_estimate=pl.CostEstimate(flops=20 * 10**9, bytes_accessed=24 * 2**20, transcendentals=0),
        name="finish_tile",
    )(place, regular, *factors, *pieces)


CORES = 2


def body(interactions, regular):
    row_count, col_count = lax.axis_size("row"), lax.axis_size("col")
    row_index, col_index = lax.axis_index("row"), lax.axis_index("col")
    width, users = interactions.shape
    band = PANEL // row_count
    ways = PANEL // width
    assert row_count == CORES * ways and col_count == SPAN * ways and users >= width
    slot, way = col_index // ways, col_index % ways
    pair, core = row_index // CORES, row_index % CORES
    all_users = row_count * users

    def exchange(value, move, only=None):
        perm = []
        for source_row in range(row_count):
            for source_col in range(col_count):
                place = (source_row // CORES, source_row % CORES, source_col // ways, source_col % ways)
                if only is None or only(*place):
                    to = move(*place)
                    target = (to[0] * CORES + to[1]) * col_count + to[2] * ways + to[3]
                    perm.append((source_row * col_count + source_col, target))
        return lax.ppermute(value, ("row", "col"), perm)

    def after(value, *others):
        return lax.optimization_barrier((value, *others))[0]

    high = lax.reduce_precision(regular, 8, 7)
    middle = lax.reduce_precision(regular - high, 8, 7)
    parts = jnp.stack([high, middle, regular - high - middle]).astype(bf16)
    parts = jnp.pad(parts, ((0, PARTS - 3), (0, users - width)))

    halves = interactions.reshape(CORES, band, users)
    offers = [lax.dynamic_index_in_dim(halves, core ^ flip, 0, False) for flip in range(CORES)]

    half = width // 2
    shared = jnp.concatenate([interactions, parts], 0)
    quarters, quarter_users = [], []
    reach = SPAN // 2
    while reach:
        got = exchange(
            shared, lambda p, h, s, w: (p, h, s + reach, w), lambda p, h, s, w: s % (2 * reach) == 0
        )
        if reach == SPAN // 2:
            for turn in reversed(range(ways)):
                for flip in range(CORES):
                    quarters.append(
                        exchange(offers[flip], lambda p, h, s, w: (w, h ^ flip, s, (p + turn) % ways))
                    )
                    quarter_users.append(((way - turn) % ways * CORES + (core ^ flip)) * users)
        shared = jnp.where(slot % (2 * reach) == reach, got, shared)
        reach //= 2
    quarters = jnp.concatenate(quarters, 0)

    def numbers(values):
        return jnp.stack([jnp.asarray(v, jnp.int32) for v in values])

    panel, panel_views, panel_place, part_views, part_place = [], [], [], [], []
    cols, cols_place = [interactions], [0, row_index * users]
    rows, rows_views, rows_place = [], [], []

    def over_core(value):
        return exchange(value, lambda p, h, s, w: (p, 1 - h, s, w))

    def over_pair(value):
        return exchange(value, lambda p, h, s, w: (1 - p, h, s, w))

    def over_way(value, only=None):
        return exchange(value, lambda p, h, s, w: (p, h, s, 1 - w), only)

    if ways == 2:
        twin_items = over_core(interactions)
        shared = after(shared, quarters, twin_items)
        pair_side, way_side = over_pair(shared), over_way(shared)
        own_twin = over_core(shared)
        diagonal = [over_way(after(pair_side, own_twin)[:half]), over_pair(after(way_side, own_twin)[half:])]
        for from_pair, from_way, first_row, piece in (
            (pair, way, 0, shared),
            (1 - pair, way, 0, pair_side),
            (pair, 1 - way, 0, way_side),
            (1 - pair, 1 - way, 0, diagonal[0]),
            (1 - pair, 1 - way, half, diagonal[1]),
        ):
            twin = own_twin if piece is shared else over_core(piece)
            for from_core, value in ((core, piece), (1 - core, twin)):
                if value is shared or value is way_side:
                    part_views.append((len(panel), width, PARTS, True))
                    part_place += [from_way * PARTS, 0]
                count = min(value.shape[0], half if value.shape[0] < width else width)
                panel_views.append((len(panel), 0, count, False))
                panel_place += [from_way * width + first_row, (from_pair * CORES + from_core) * users]
                panel.append(value)
        crossed = [pair_side, way_side, *diagonal]
        held = after(interactions, *crossed)
        cols += [twin_items, over_pair(held), exchange(held, lambda p, h, s, w: (1 - p, 1 - h, s, w))]
        cols_place += [0, (row_index ^ 1) * users, 0, (row_index ^ 2) * users, 0, (row_index ^ 3) * users]
        first = exchange(quarters, lambda p, h, s, w: (p, h, s - 1, w), lambda p, h, s, w: s > 0)
        relayed, ready = lax.optimization_barrier((first, quarters, *crossed))[:2]
        second = exchange(relayed, lambda p, h, s, w: (p, h, s - 1, w), lambda p, h, s, w: 0 < s < SPAN - 1)
        ring = exchange(ready, lambda p, h, s, w: (p, h, (s + 1) % SPAN, w), lambda p, h, s, w: s > 0)
        leap = exchange(ready, lambda p, h, s, w: (p, h, s + 2, w), lambda p, h, s, w: s == 1)
        rows = [quarters, first, second, ring, leap]
        from_slots = [
            slot,
            jnp.where(slot < 3, slot + 1, 0),
            jnp.where(slot < 2, slot + 2, 0),
            jnp.where(slot == 1, 0, (slot + 3) % SPAN),
            jnp.where(slot == 3, 1, 0),
        ]
        for from_slot, piece in enumerate(rows):
            for which, from_users in enumerate(quarter_users):
                rows_views.append((from_slot, which * band, band))
                rows_place += [(from_slots[from_slot] - 1) * band, from_users]
    else:
        groups = [[s * ways + w for w in range(ways)] for s in range(SPAN)]
        shared = lax.all_gather(shared, "col", axis=0, axis_index_groups=groups)
        parts = shared[:, width:].reshape(ways * PARTS, users)
        shared = shared[:, :width].reshape(PANEL, users)
        panel, panel_place = [lax.all_gather(shared, "row", axis=1, tiled=True), parts], [0, 0]
        panel_views = [(0, 0, PANEL, False)]
        part_views, part_place = [(1, 0, ways * PARTS, True)], [0, 0]
        cols, cols_place = [lax.all_gather(interactions, "row", axis=1, tiled=True)], [0, 0]
        groups = [[s * ways + w for s in range(SPAN)] for w in range(ways)]
        rows = [lax.all_gather(quarters, "col", axis=0, tiled=True, axis_index_groups=groups)]
        for from_slot in range(1, SPAN):
            for which, from_users in enumerate(quarter_users):
                rows_views.append((0, (from_slot * len(quarter_users) + which) * band, band))
                rows_place += [(from_slot - 1) * band, from_users]

    factors = factor_panel(
        numbers(panel_place + part_place), panel, panel_views + part_views, width, all_users
    )
    views = [view[:3] for view in panel_views]
    views += [(len(panel) + i, start, count) for i, start, count in rows_views]
    views += [(len(panel) + len(rows) + i, 0, width) for i in range(len(cols))]
    tile = finish_tile(
        numbers([row_index, col_index] + panel_place + rows_place + cols_place),
        regular[None, :], factors, panel, rows, cols, views, band, all_users,
    )
    return tile.reshape(SPAN, band, width)


def solution(mesh):
    return jax.shard_map(
        body,
        mesh=mesh,
        in_specs=(P("col", "row"), P("col")),
        out_specs=P(None, "row", "col"),
        check_vma=False,
    )
```

```python
import functools
import math
import jax
import jax.numpy as jnp
from jax import lax
from jax.experimental import pallas as pl
from jax.experimental.pallas import tpu as pltpu
from jax.sharding import PartitionSpec as P

PANEL = 1024
SPAN = 4
BLOCK = 128
WIDE = 256
SUB = 8
NBLOCKS = PANEL // BLOCK
PARTS = 16
VMEM = pltpu.VMEM
f32 = jnp.float32
bf16 = jnp.bfloat16


def dot_nt(a, b):
    return lax.dot_general(a, b, (((1,), (1,)), ((), ())), preferred_element_type=f32)


def split(value):
    high = value.astype(bf16)
    return high, (value - high.astype(f32)).astype(bf16)


def dot_nt3(a, b):
    return dot_nt(a[0], b[0]) + (dot_nt(a[0], b[1]) + dot_nt(a[1], b[0]))


def dot_nn3(a, b):
    def dot(x, y):
        return jnp.dot(x, y, preferred_element_type=f32)

    return dot(a[0], b[0]) + (dot(a[0], b[1]) + dot(a[1], b[0]))


def lanes(value, lane):
    return jnp.broadcast_to(value[:, lane : lane + 1], (SUB, BLOCK))


def sublanes(value, row):
    return jnp.broadcast_to(value[row : row + 1, :], (SUB, BLOCK))


def factor_block(block_ref, inverse_ref):
    tiles_count = BLOCK // SUB
    row_in_tile = lax.broadcasted_iota(jnp.int32, (SUB, BLOCK), 0)
    lane = lax.broadcasted_iota(jnp.int32, (SUB, BLOCK), 1)
    sides = [block_ref[pl.ds(SUB * t, SUB), :] for t in range(tiles_count)]
    inverses = [(lane == row_in_tile + SUB * t).astype(f32) for t in range(tiles_count)]
    uppers = []
    for step in range(tiles_count):
        base = SUB * step
        side, inverse = sides[step], inverses[step]
        if step == 0:
            columns = [lanes(side, base + b) for b in range(SUB)]
        entry = {(a, b): sublanes(columns[b], a) for b in range(SUB) for a in range(b, SUB)}
        vectors = [[sublanes(side, a) for a in range(SUB)], [sublanes(inverse, a) for a in range(SUB)]]
        if step + 1 < tiles_count:
            vectors.append([lanes(sides[step + 1], base + b) for b in range(SUB)])
            columns = [lanes(sides[step + 1], base + SUB + b) for b in range(SUB)]
        scale = [None] * SUB
        for m in range(0, SUB, 2):
            n = m + 1
            first, cross, second = entry[m, m], entry[n, m], entry[n, n]
            root = lax.rsqrt(first)
            det_root = lax.rsqrt(first * second - cross * cross)
            scale[m], scale[n] = root, det_root * (first * root)
            det_square = det_root * det_root
            link = cross * root
            entry[n, m] = link
            rest = range(n + 1, SUB)
            for x in rest:
                entry[x, m] = entry[x, m] * root
                entry[x, n] = entry[x, n] - entry[x, m] * link
            weighted = {x: entry[x, n] * first for x in rest}
            for y in rest:
                for x in range(y, SUB):
                    entry[x, y] = (entry[x, y] - entry[x, m] * entry[y, m]) - (weighted[x] * entry[y, n]) * det_square
            for x in rest:
                entry[x, n] = entry[x, n] * scale[n]
            for vector in vectors:
                vector[m] = vector[m] * root
                vector[n] = (vector[n] - link * vector[m]) * scale[n]
                for x in rest:
                    vector[x] = (vector[x] - entry[x, m] * vector[m]) - entry[x, n] * vector[n]
            if step + 1 < tiles_count:
                left, right = vectors[2][m], vectors[2][n]
                columns = [
                    (column - left * sublanes(left, b)) - right * sublanes(right, b)
                    for b, column in enumerate(columns)
                ]
        tops, insides = vectors[:2]
        upper, lower_inverse = tops[0], insides[0]
        for m in range(1, SUB):
            upper = jnp.where(row_in_tile == m, tops[m], upper)
            lower_inverse = jnp.where(row_in_tile == m, insides[m], lower_inverse)
        uppers.append(jnp.where(lane >= row_in_tile + base, upper, 0.0))
        inverse_ref[pl.ds(base, SUB), :] = lower_inverse
        if step + 1 < tiles_count:
            ahead = vectors[2]
            for m in range(SUB):
                sides[step + 1] = sides[step + 1] - ahead[m] * tops[m]
                inverses[step + 1] = inverses[step + 1] - ahead[m] * insides[m]
        if step + 2 < tiles_count:
            weights_top, weights_in = [None] * SUB, [None] * SUB
            for m in reversed(range(SUB)):
                top, inside = tops[m], insides[m]
                for b in range(m + 1, SUB):
                    top = top - entry[b, m] * weights_top[b]
                    inside = inside - entry[b, m] * weights_in[b]
                weights_top[m], weights_in[m] = top * scale[m], inside * scale[m]
            for t in range(step + 2, tiles_count):
                for m in range(SUB):
                    column = lanes(sides[t], base + m)
                    if m == 0:
                        top_sum, in_sum = column * weights_top[m], column * weights_in[m]
                    else:
                        top_sum = top_sum + column * weights_top[m]
                        in_sum = in_sum + column * weights_in[m]
                sides[t] = sides[t] - top_sum
                inverses[t] = inverses[t] - in_sum
    block_ref[...] = jnp.concatenate(uppers, 0).T


def place_pieces(place_ref, first, pieces, helds, sem):
    waits = []
    for i, (piece, held_ref) in enumerate(zip(pieces, helds)):
        rows, users = piece.shape
        row = place_ref[first + 2 * i]
        user = pl.multiple_of(place_ref[first + 2 * i + 1], users)
        to = held_ref.at[pl.ds(pl.multiple_of(jnp.maximum(row, 0), rows), rows), pl.ds(user, users)]
        copy = pltpu.make_async_copy(piece, to, sem.at[i])
        pl.when(row >= 0)(copy.start)
        waits.append(functools.partial(pl.when(row >= 0), copy.wait))
    return waits


def panel_kernel(views, count, width, place_ref, *refs):
    pieces, refs = refs[:count], refs[count:]
    outs, (high_ref, low_ref, inv_high_ref, inv_low_ref, lower_ref, coming_ref, *refs) = refs[:4], refs[4:]
    block_ref, inverse_ref, items_ref, parts_ref, sem, out_sem = refs
    held = [parts_ref if is_part else items_ref for _, _, _, is_part in views]
    views = [pieces[which].at[pl.ds(start, rows)] for which, start, rows, _ in views]
    waits = place_pieces(place_ref, 0, views, held, sem)
    for k in range(1, NBLOCKS):
        for ref in (high_ref, low_ref):
            ref[pl.ds(0, k * BLOCK), pl.ds(k * BLOCK, BLOCK)] = jnp.zeros((k * BLOCK, BLOCK), bf16)
    for wait in waits:
        wait()
    on_diagonal = lax.broadcasted_iota(jnp.int32, (BLOCK, BLOCK), 0) == lax.broadcasted_iota(
        jnp.int32, (BLOCK, BLOCK), 1
    )

    def before(k):
        start = k * BLOCK
        here, rest = pl.ds(start, BLOCK), pl.ds(start, PANEL - start)
        if k % 2 == 0:
            both = pl.ds(start, 2 * BLOCK)
            columns = dot_nt(items_ref[rest, :], items_ref[both, :])
            if k > 0:
                columns = columns - dot_nt3(
                    (high_ref[rest, :start], low_ref[rest, :start]), (high_ref[both, :start], low_ref[both, :start])
                )
            column = columns[:, :BLOCK]
            coming_ref[pl.ds(start + BLOCK, PANEL - start - BLOCK), :] = columns[BLOCK:, BLOCK:]
        else:
            last = pl.ds(start - BLOCK, BLOCK)
            high, low = high_ref[rest, last], low_ref[rest, last]
            column = coming_ref[rest, :] - dot_nt3((high, low), (high[:BLOCK], low[:BLOCK]))
        part, lane = PARTS * (start // width), start % width
        parts = parts_ref[pl.ds(part, PARTS), pl.ds(lane, BLOCK)].astype(f32)
        block_ref[...] = column[:BLOCK] + jnp.where(on_diagonal, parts[0:1] + parts[1:2] + parts[2:3], 0.0)
        if k + 1 < NBLOCKS:
            lower_ref[pl.ds(start + BLOCK, PANEL - start - BLOCK), :] = column[BLOCK:]

    def after(k):
        start = k * BLOCK
        here = pl.ds(start, BLOCK)
        inverse = split(inverse_ref[...])
        inv_high_ref[here, :], inv_low_ref[here, :] = inverse
        high_ref[here, here], low_ref[here, here] = split(block_ref[...])
        if k + 1 < NBLOCKS:
            rest = pl.ds(start + BLOCK, PANEL - start - BLOCK)
            high_ref[rest, here], low_ref[rest, here] = split(dot_nt3(split(lower_ref[rest, :]), inverse))

    def leave(k):
        column = pl.ds(k * BLOCK, BLOCK)
        return [
            pltpu.make_async_copy(high_ref.at[:, column], outs[0].at[:, column], out_sem.at[0, k]),
            pltpu.make_async_copy(low_ref.at[:, column], outs[1].at[:, column], out_sem.at[1, k]),
            pltpu.make_async_copy(inv_high_ref.at[column, :], outs[2].at[column, :], out_sem.at[2, k]),
            pltpu.make_async_copy(inv_low_ref.at[column, :], outs[3].at[column, :], out_sem.at[3, k]),
        ]

    before(0)

    def turn(k, carry):
        factor_block(block_ref, inverse_ref)
        for which in range(NBLOCKS):

            @pl.when(k == which)
            def _():
                after(which)
                for copy in leave(which):
                    copy.start()
                if which + 1 < NBLOCKS:
                    before(which + 1)

        return carry

    lax.fori_loop(0, NBLOCKS, turn, 0)
    for k in range(NBLOCKS):
        for copy in leave(k):
            copy.wait()


def room(*arrays):
    return sum(math.prod(shape) * jnp.dtype(dtype).itemsize for shape, dtype in arrays) + 8 * 2**20


def factor_panel(place, pieces, views, width, users):
    outs = [
        ((PANEL, PANEL), bf16),
        ((PANEL, PANEL), bf16),
        ((PANEL, BLOCK), bf16),
        ((PANEL, BLOCK), bf16),
    ]
    held = [
        ((PANEL, BLOCK), f32),
        ((PANEL, BLOCK), f32),
        ((BLOCK, BLOCK), f32),
        ((BLOCK, BLOCK), f32),
        ((PANEL, users), bf16),
        ((PANEL // width * PARTS, users), bf16),
    ]
    return pl.pallas_call(
        functools.partial(panel_kernel, views, len(pieces), width),
        out_shape=[pltpu.HBM(*out) for out in outs],
        in_specs=[pl.BlockSpec(memory_space=pltpu.SMEM)]
        + [pl.BlockSpec(memory_space=pl.ANY)] * len(pieces),
        out_specs=[pl.BlockSpec(memory_space=pltpu.HBM)] * len(outs),
        scratch_shapes=[VMEM(*one) for one in outs + held]
        + [pltpu.SemaphoreType.DMA((len(views),)), pltpu.SemaphoreType.DMA((len(outs), NBLOCKS))],
        compiler_params=pltpu.CompilerParams(vmem_limit_bytes=room(*outs, *held)),
        cost_estimate=pl.CostEstimate(flops=4 * 10**10, bytes_accessed=16 * 2**20, transcendentals=1024),
        name="factor_panel",
    )(place, *pieces)


def tile_kernel(counts, views, place_ref, regular_ref, *refs):
    factors, refs = refs[:4], refs[4:]
    pieces, refs = refs[: sum(counts)], refs[sum(counts) :]
    out_ref, refs = refs[0], refs[1:]
    high_ref, low_ref, inv_high_ref, inv_low_ref, left_high_ref, left_low_ref, wide_high_ref, wide_low_ref = refs[:8]
    panel_ref, rows_ref, cols_ref, sem, factor_sem = refs[8:]
    targets = [panel_ref] * counts[0] + [rows_ref] * counts[1] + [cols_ref] * counts[2]
    held = [targets[which] for which, *_ in views]
    views = [pieces[which].at[pl.ds(start, rows)] for which, start, rows in views]
    fetches = [
        pltpu.make_async_copy(factor, ref, factor_sem.at[i])
        for i, (factor, ref) in enumerate(zip(factors, (high_ref, low_ref, inv_high_ref, inv_low_ref)))
    ]
    for fetch in fetches:
        fetch.start()
    waits = place_pieces(place_ref, 2, views, held, sem)
    row_index, col_index = place_ref[0], place_ref[1]
    width, band = cols_ref.shape[0], rows_ref.shape[0] // (SPAN - 1)
    row_count = (SPAN - 1) * band
    panel_blocks = PANEL // width
    in_panel = col_index < panel_blocks
    slot = jnp.minimum(col_index, panel_blocks - 1)
    at = pl.ds(pl.multiple_of(slot * width, width), width)
    below, right = pl.ds(0, row_count), pl.ds(row_count, width)

    for wait in waits:
        wait()
    step = min(WIDE, width)
    groups = [(cols_ref, at_row, pl.ds(row_count + at_row, step), step) for at_row in range(0, width, step)]
    groups += [(rows_ref, at_row, pl.ds(at_row, band), band) for at_row in range(0, row_count, band)]

    def grams(start):
        block = panel_ref[pl.ds(start, WIDE), :]
        return [dot_nt(ref[pl.ds(at_row, count), :], block) for ref, at_row, _, count in groups]

    columns = grams(0)
    for fetch in fetches:
        fetch.wait()

    for start in range(0, PANEL, WIDE):
        first, second = pl.ds(start, BLOCK), pl.ds(start + BLOCK, BLOCK)
        between = dot_nn3((high_ref[second, first], low_ref[second, first]), (inv_high_ref[first, :], inv_low_ref[first, :]))
        corner = split(-dot_nn3((inv_high_ref[second, :], inv_low_ref[second, :]), split(between)))
        for wide_ref, inv_ref, part in ((wide_high_ref, inv_high_ref, corner[0]), (wide_low_ref, inv_low_ref, corner[1])):
            wide_ref[first, pl.ds(0, BLOCK)] = inv_ref[first, :]
            wide_ref[first, pl.ds(BLOCK, BLOCK)] = jnp.zeros((BLOCK, BLOCK), bf16)
            wide_ref[second, pl.ds(0, BLOCK)] = part
            wide_ref[second, pl.ds(BLOCK, BLOCK)] = inv_ref[second, :]

    for start in range(0, PANEL, WIDE):
        here = pl.ds(start, WIDE)
        if start > 0:
            columns = [
                column
                - dot_nt3(
                    (left_high_ref[mine, :start], left_low_ref[mine, :start]), (high_ref[here, :start], low_ref[here, :start])
                )
                for column, (_, _, mine, _) in zip(grams(start), groups)
            ]
        for column, (_, _, mine, _) in zip(columns, groups):
            column = dot_nt3(split(column), (wide_high_ref[here, :], wide_low_ref[here, :]))
            left_high_ref[mine, here], left_low_ref[mine, here] = split(column)

    @pl.when(in_panel)
    def _():
        mine = pl.ds(pl.multiple_of(row_index * band, band), band)
        out_ref[pl.ds(0, band), :] = high_ref[mine, at].astype(f32) + low_ref[mine, at].astype(f32)
        out_ref[pl.ds(band, row_count), :] = left_high_ref[below, at].astype(f32) + left_low_ref[below, at].astype(f32)

    @pl.when(jnp.logical_not(in_panel))
    def _():
        out_ref[pl.ds(0, band), :] = jnp.zeros((band, width), f32)
        items = lax.broadcasted_iota(jnp.int32, (band, width), 0) + row_index * band
        columns = lax.broadcasted_iota(jnp.int32, (band, width), 1) + col_index * width
        for part in range(SPAN - 1):
            mine = pl.ds(part * band, band)
            tile = dot_nt(rows_ref[mine, :], cols_ref[...])
            tile = tile + jnp.where(items + (part + 1) * PANEL == columns, regular_ref[...], 0.0)
            out_ref[pl.ds((part + 1) * band, band), :] = tile - dot_nt3(
                (left_high_ref[mine, :], left_low_ref[mine, :]), (left_high_ref[right, :], left_low_ref[right, :])
            )


def finish_tile(place, regular, factors, panel, rows, cols, views, band, users):
    spec = pl.BlockSpec(memory_space=VMEM)
    width = regular.shape[1]
    factors = [pltpu.with_memory_space_constraint(x, pltpu.HBM) for x in factors]
    pieces = panel + rows + cols
    out = ((SPAN * band, width), f32)
    below = (SPAN - 1) * band + width
    held = [
        ((below, PANEL), bf16),
        ((below, PANEL), bf16),
        ((PANEL, WIDE), bf16),
        ((PANEL, WIDE), bf16),
        ((PANEL, users), bf16),
        (((SPAN - 1) * band, users), bf16),
        ((width, users), bf16),
    ]
    return pl.pallas_call(
        functools.partial(tile_kernel, (len(panel), len(rows), len(cols)), views),
        out_shape=jax.ShapeDtypeStruct(*out),
        in_specs=[pl.BlockSpec(memory_space=pltpu.SMEM)]
        + [spec]
        + [pl.BlockSpec(memory_space=pltpu.HBM)] * len(factors)
        + [pl.BlockSpec(memory_space=pl.ANY)] * len(pieces),
        out_specs=spec,
        scratch_shapes=[VMEM(factor.shape, factor.dtype) for factor in factors]
        + [VMEM(*one) for one in held]
        + [pltpu.SemaphoreType.DMA((len(views),)), pltpu.SemaphoreType.DMA((len(factors),))],
        compiler_params=pltpu.CompilerParams(vmem_limit_bytes=room(out, *held, *((factor.shape, factor.dtype) for factor in factors))),
        cost_estimate=pl.CostEstimate(flops=20 * 10**9, bytes_accessed=24 * 2**20, transcendentals=0),
        name="finish_tile",
    )(place, regular, *factors, *pieces)


CORES = 2


def body(interactions, regular):
    row_count, col_count = lax.axis_size("row"), lax.axis_size("col")
    row_index, col_index = lax.axis_index("row"), lax.axis_index("col")
    width, users = interactions.shape
    band = PANEL // row_count
    ways = PANEL // width
    assert row_count == CORES * ways and col_count == SPAN * ways and users >= width
    slot, way = col_index // ways, col_index % ways
    pair, core = row_index // CORES, row_index % CORES
    all_users = row_count * users

    def exchange(value, move, only=None):
        perm = []
        for source_row in range(row_count):
            for source_col in range(col_count):
                place = (source_row // CORES, source_row % CORES, source_col // ways, source_col % ways)
                if only is None or only(*place):
                    to = move(*place)
                    target = (to[0] * CORES + to[1]) * col_count + to[2] * ways + to[3]
                    perm.append((source_row * col_count + source_col, target))
        return lax.ppermute(value, ("row", "col"), perm)

    def after(value, *others):
        return lax.optimization_barrier((value, *others))[0]

    high = lax.reduce_precision(regular, 8, 7)
    middle = lax.reduce_precision(regular - high, 8, 7)
    parts = jnp.stack([high, middle, regular - high - middle]).astype(bf16)
    parts = jnp.pad(parts, ((0, PARTS - 3), (0, users - width)))

    halves = interactions.reshape(CORES, band, users)
    offers = [lax.dynamic_index_in_dim(halves, core ^ flip, 0, False) for flip in range(CORES)]

    half = width // 2
    shared = jnp.concatenate([interactions, parts], 0)
    quarters, quarter_users = [], []
    reach = SPAN // 2
    while reach:
        got = exchange(
            shared, lambda p, h, s, w: (p, h, s + reach, w), lambda p, h, s, w: s % (2 * reach) == 0
        )
        if reach == SPAN // 2:
            for turn in range(ways):
                for flip in range(CORES):
                    quarters.append(
                        exchange(offers[flip], lambda p, h, s, w: (w, h ^ flip, s, (p + turn) % ways))
                    )
                    quarter_users.append(((way - turn) % ways * CORES + (core ^ flip)) * users)
        shared = jnp.where(slot % (2 * reach) == reach, got, shared)
        reach //= 2
    quarters = jnp.concatenate(quarters, 0)

    def numbers(values):
        return jnp.stack([jnp.asarray(v, jnp.int32) for v in values])

    panel, panel_views, panel_place, part_views, part_place = [], [], [], [], []
    cols, cols_place = [interactions], [0, row_index * users]
    rows, rows_views, rows_place = [], [], []

    def over_core(value):
        return exchange(value, lambda p, h, s, w: (p, 1 - h, s, w))

    def over_pair(value):
        return exchange(value, lambda p, h, s, w: (1 - p, h, s, w))

    def over_way(value, only=None):
        return exchange(value, lambda p, h, s, w: (p, h, s, 1 - w), only)

    if ways == 2:
        twin_items = over_core(interactions)
        shared = after(shared, quarters, twin_items)
        pair_side, way_side = over_pair(shared), over_way(shared)
        own_twin = over_core(shared)
        diagonal = [over_way(after(pair_side, own_twin)[:half]), over_pair(after(way_side, own_twin)[half:])]
        for from_pair, from_way, first_row, piece in (
            (pair, way, 0, shared),
            (1 - pair, way, 0, pair_side),
            (pair, 1 - way, 0, way_side),
            (1 - pair, 1 - way, 0, diagonal[0]),
            (1 - pair, 1 - way, half, diagonal[1]),
        ):
            twin = own_twin if piece is shared else over_core(piece)
            for from_core, value in ((core, piece), (1 - core, twin)):
                if value is shared or value is way_side:
                    part_views.append((len(panel), width, PARTS, True))
                    part_place += [from_way * PARTS, 0]
                count = min(value.shape[0], half if value.shape[0] < width else width)
                panel_views.append((len(panel), 0, count, False))
                panel_place += [from_way * width + first_row, (from_pair * CORES + from_core) * users]
                panel.append(value)
        crossed = [pair_side, way_side, *diagonal]
        held = after(interactions, *crossed)
        cols += [twin_items, over_pair(held), exchange(held, lambda p, h, s, w: (1 - p, 1 - h, s, w))]
        cols_place += [0, (row_index ^ 1) * users, 0, (row_index ^ 2) * users, 0, (row_index ^ 3) * users]
        first = exchange(quarters, lambda p, h, s, w: (p, h, s - 1, w), lambda p, h, s, w: s > 0)
        relayed, ready = lax.optimization_barrier((first, quarters, *crossed))[:2]
        second = exchange(relayed, lambda p, h, s, w: (p, h, s - 1, w), lambda p, h, s, w: 0 < s < SPAN - 1)
        ring = exchange(ready, lambda p, h, s, w: (p, h, (s + 1) % SPAN, w), lambda p, h, s, w: s > 0)
        leap = exchange(ready, lambda p, h, s, w: (p, h, s + 2, w), lambda p, h, s, w: s == 1)
        rows = [quarters, first, second, ring, leap]
        from_slots = [
            slot,
            jnp.where(slot < 3, slot + 1, 0),
            jnp.where(slot < 2, slot + 2, 0),
            jnp.where(slot == 1, 0, (slot + 3) % SPAN),
            jnp.where(slot == 3, 1, 0),
        ]
        for from_slot, piece in enumerate(rows):
            for which, from_users in enumerate(quarter_users):
                rows_views.append((from_slot, which * band, band))
                rows_place += [(from_slots[from_slot] - 1) * band, from_users]
    else:
        groups = [[s * ways + w for w in range(ways)] for s in range(SPAN)]
        shared = lax.all_gather(shared, "col", axis=0, axis_index_groups=groups)
        parts = shared[:, width:].reshape(ways * PARTS, users)
        shared = shared[:, :width].reshape(PANEL, users)
        panel, panel_place = [lax.all_gather(shared, "row", axis=1, tiled=True), parts], [0, 0]
        panel_views = [(0, 0, PANEL, False)]
        part_views, part_place = [(1, 0, ways * PARTS, True)], [0, 0]
        cols, cols_place = [lax.all_gather(interactions, "row", axis=1, tiled=True)], [0, 0]
        groups = [[s * ways + w for s in range(SPAN)] for w in range(ways)]
        rows = [lax.all_gather(quarters, "col", axis=0, tiled=True, axis_index_groups=groups)]
        for from_slot in range(1, SPAN):
            for which, from_users in enumerate(quarter_users):
                rows_views.append((0, (from_slot * len(quarter_users) + which) * band, band))
                rows_place += [(from_slot - 1) * band, from_users]

    factors = factor_panel(
        numbers(panel_place + part_place), panel, panel_views + part_views, width, all_users
    )
    views = [view[:3] for view in panel_views]
    views += [(len(panel) + i, start, count) for i, start, count in rows_views]
    views += [(len(panel) + len(rows) + i, 0, width) for i in range(len(cols))]
    tile = finish_tile(
        numbers([row_index, col_index] + panel_place + rows_place + cols_place),
        regular[None, :], factors, panel, rows, cols, views, band, all_users,
    )
    return tile.reshape(SPAN, band, width)


def solution(mesh):
    return jax.shard_map(
        body,
        mesh=mesh,
        in_specs=(P("col", "row"), P("col")),
        out_specs=P(None, "row", "col"),
        check_vma=False,
    )
```

```python
import functools
import math
import jax
import jax.numpy as jnp
from jax import lax
from jax.experimental import pallas as pl
from jax.experimental.pallas import tpu as pltpu
from jax.sharding import PartitionSpec as P

PANEL = 1024
SPAN = 4
BLOCK = 128
WIDE = 256
SUB = 8
NBLOCKS = PANEL // BLOCK
PARTS = 16
VMEM = pltpu.VMEM
f32 = jnp.float32
bf16 = jnp.bfloat16


def dot_nt(a, b):
    return lax.dot_general(a, b, (((1,), (1,)), ((), ())), preferred_element_type=f32)


def split(value):
    high = value.astype(bf16)
    return high, (value - high.astype(f32)).astype(bf16)


def dot_nt3(a, b):
    return dot_nt(a[0], b[0]) + (dot_nt(a[0], b[1]) + dot_nt(a[1], b[0]))


def dot_nn3(a, b):
    def dot(x, y):
        return jnp.dot(x, y, preferred_element_type=f32)

    return dot(a[0], b[0]) + (dot(a[0], b[1]) + dot(a[1], b[0]))


def lanes(value, lane):
    return jnp.broadcast_to(value[:, lane : lane + 1], (SUB, BLOCK))


def sublanes(value, row):
    return jnp.broadcast_to(value[row : row + 1, :], (SUB, BLOCK))


def factor_block(block_ref, inverse_ref):
    tiles_count = BLOCK // SUB
    row_in_tile = lax.broadcasted_iota(jnp.int32, (SUB, BLOCK), 0)
    lane = lax.broadcasted_iota(jnp.int32, (SUB, BLOCK), 1)
    sides = [block_ref[pl.ds(SUB * t, SUB), :] for t in range(tiles_count)]
    inverses = [(lane == row_in_tile + SUB * t).astype(f32) for t in range(tiles_count)]
    uppers = []
    for step in range(tiles_count):
        base = SUB * step
        side, inverse = sides[step], inverses[step]
        if step == 0:
            columns = [lanes(side, base + b) for b in range(SUB)]
        entry = {(a, b): sublanes(columns[b], a) for b in range(SUB) for a in range(b, SUB)}
        vectors = [[sublanes(side, a) for a in range(SUB)], [sublanes(inverse, a) for a in range(SUB)]]
        if step + 1 < tiles_count:
            vectors.append([lanes(sides[step + 1], base + b) for b in range(SUB)])
            columns = [lanes(sides[step + 1], base + SUB + b) for b in range(SUB)]
        scale = [None] * SUB
        for m in range(0, SUB, 2):
            n = m + 1
            first, cross, second = entry[m, m], entry[n, m], entry[n, n]
            root = lax.rsqrt(first)
            det_root = lax.rsqrt(first * second - cross * cross)
            scale[m], scale[n] = root, det_root * (first * root)
            det_square = det_root * det_root
            link = cross * root
            entry[n, m] = link
            rest = range(n + 1, SUB)
            for x in rest:
                entry[x, m] = entry[x, m] * root
                entry[x, n] = entry[x, n] - entry[x, m] * link
            weighted = {x: entry[x, n] * first for x in rest}
            for y in rest:
                for x in range(y, SUB):
                    entry[x, y] = (entry[x, y] - entry[x, m] * entry[y, m]) - (weighted[x] * entry[y, n]) * det_square
            for x in rest:
                entry[x, n] = entry[x, n] * scale[n]
            for vector in vectors:
                vector[m] = vector[m] * root
                vector[n] = (vector[n] - link * vector[m]) * scale[n]
                for x in rest:
                    vector[x] = (vector[x] - entry[x, m] * vector[m]) - entry[x, n] * vector[n]
            if step + 1 < tiles_count:
                left, right = vectors[2][m], vectors[2][n]
                columns = [
                    (column - left * sublanes(left, b)) - right * sublanes(right, b)
                    for b, column in enumerate(columns)
                ]
        tops, insides = vectors[:2]
        upper, lower_inverse = tops[0], insides[0]
        for m in range(1, SUB):
            upper = jnp.where(row_in_tile == m, tops[m], upper)
            lower_inverse = jnp.where(row_in_tile == m, insides[m], lower_inverse)
        uppers.append(jnp.where(lane >= row_in_tile + base, upper, 0.0))
        inverse_ref[pl.ds(base, SUB), :] = lower_inverse
        if step + 1 < tiles_count:
            ahead = vectors[2]
            for m in range(SUB):
                sides[step + 1] = sides[step + 1] - ahead[m] * tops[m]
                inverses[step + 1] = inverses[step + 1] - ahead[m] * insides[m]
        if step + 2 < tiles_count:
            weights_top, weights_in = [None] * SUB, [None] * SUB
            for m in reversed(range(SUB)):
                top, inside = tops[m], insides[m]
                for b in range(m + 1, SUB):
                    top = top - entry[b, m] * weights_top[b]
                    inside = inside - entry[b, m] * weights_in[b]
                weights_top[m], weights_in[m] = top * scale[m], inside * scale[m]
            for t in range(step + 2, tiles_count):
                for m in range(SUB):
                    column = lanes(sides[t], base + m)
                    if m == 0:
                        top_sum, in_sum = column * weights_top[m], column * weights_in[m]
                    else:
                        top_sum = top_sum + column * weights_top[m]
                        in_sum = in_sum + column * weights_in[m]
                sides[t] = sides[t] - top_sum
                inverses[t] = inverses[t] - in_sum
    block_ref[...] = jnp.concatenate(uppers, 0).T


def place_pieces(place_ref, first, pieces, helds, sem):
    waits = []
    for i, (piece, held_ref) in enumerate(zip(pieces, helds)):
        rows, users = piece.shape
        row = place_ref[first + 2 * i]
        user = pl.multiple_of(place_ref[first + 2 * i + 1], users)
        to = held_ref.at[pl.ds(pl.multiple_of(jnp.maximum(row, 0), rows), rows), pl.ds(user, users)]
        copy = pltpu.make_async_copy(piece, to, sem.at[i])
        pl.when(row >= 0)(copy.start)
        waits.append(functools.partial(pl.when(row >= 0), copy.wait))
    return waits


def panel_kernel(views, count, width, place_ref, *refs):
    pieces, refs = refs[:count], refs[count:]
    outs, (high_ref, low_ref, inv_high_ref, inv_low_ref, lower_ref, coming_ref, *refs) = refs[:4], refs[4:]
    block_ref, inverse_ref, items_ref, parts_ref, sem, out_sem = refs
    held = [parts_ref if is_part else items_ref for _, _, _, is_part in views]
    views = [pieces[which].at[pl.ds(start, rows)] for which, start, rows, _ in views]
    waits = place_pieces(place_ref, 0, views, held, sem)
    for k in range(1, NBLOCKS):
        for ref in (high_ref, low_ref):
            ref[pl.ds(0, k * BLOCK), pl.ds(k * BLOCK, BLOCK)] = jnp.zeros((k * BLOCK, BLOCK), bf16)
    for wait in waits:
        wait()
    on_diagonal = lax.broadcasted_iota(jnp.int32, (BLOCK, BLOCK), 0) == lax.broadcasted_iota(
        jnp.int32, (BLOCK, BLOCK), 1
    )

    def before(k):
        start = k * BLOCK
        here, rest = pl.ds(start, BLOCK), pl.ds(start, PANEL - start)
        if k % 2 == 0:
            both = pl.ds(start, 2 * BLOCK)
            columns = dot_nt(items_ref[rest, :], items_ref[both, :])
            if k > 0:
                columns = columns - dot_nt3(
                    (high_ref[rest, :start], low_ref[rest, :start]), (high_ref[both, :start], low_ref[both, :start])
                )
            column = columns[:, :BLOCK]
            coming_ref[pl.ds(start + BLOCK, PANEL - start - BLOCK), :] = columns[BLOCK:, BLOCK:]
        else:
            last = pl.ds(start - BLOCK, BLOCK)
            high, low = high_ref[rest, last], low_ref[rest, last]
            column = coming_ref[rest, :] - dot_nt3((high, low), (high[:BLOCK], low[:BLOCK]))
        part, lane = PARTS * (start // width), start % width
        parts = parts_ref[pl.ds(part, PARTS), pl.ds(lane, BLOCK)].astype(f32)
        block_ref[...] = column[:BLOCK] + jnp.where(on_diagonal, parts[0:1] + parts[1:2] + parts[2:3], 0.0)
        if k + 1 < NBLOCKS:
            lower_ref[pl.ds(start + BLOCK, PANEL - start - BLOCK), :] = column[BLOCK:]

    def after(k):
        start = k * BLOCK
        here = pl.ds(start, BLOCK)
        inverse = split(inverse_ref[...])
        inv_high_ref[here, :], inv_low_ref[here, :] = inverse
        high_ref[here, here], low_ref[here, here] = split(block_ref[...])
        if k + 1 < NBLOCKS:
            rest = pl.ds(start + BLOCK, PANEL - start - BLOCK)
            high_ref[rest, here], low_ref[rest, here] = split(dot_nt3(split(lower_ref[rest, :]), inverse))

    def leave(k):
        column = pl.ds(k * BLOCK, BLOCK)
        return [
            pltpu.make_async_copy(high_ref.at[:, column], outs[0].at[:, column], out_sem.at[0, k]),
            pltpu.make_async_copy(low_ref.at[:, column], outs[1].at[:, column], out_sem.at[1, k]),
            pltpu.make_async_copy(inv_high_ref.at[column, :], outs[2].at[column, :], out_sem.at[2, k]),
            pltpu.make_async_copy(inv_low_ref.at[column, :], outs[3].at[column, :], out_sem.at[3, k]),
        ]

    before(0)

    def turn(k, carry):
        factor_block(block_ref, inverse_ref)
        for which in range(NBLOCKS):

            @pl.when(k == which)
            def _():
                after(which)
                for copy in leave(which):
                    copy.start()
                if which + 1 < NBLOCKS:
                    before(which + 1)

        return carry

    lax.fori_loop(0, NBLOCKS, turn, 0)
    for k in range(NBLOCKS):
        for copy in leave(k):
            copy.wait()


def room(*arrays):
    return sum(math.prod(shape) * jnp.dtype(dtype).itemsize for shape, dtype in arrays) + 8 * 2**20


def factor_panel(place, pieces, views, width, users):
    outs = [
        ((PANEL, PANEL), bf16),
        ((PANEL, PANEL), bf16),
        ((PANEL, BLOCK), bf16),
        ((PANEL, BLOCK), bf16),
    ]
    held = [
        ((PANEL, BLOCK), f32),
        ((PANEL, BLOCK), f32),
        ((BLOCK, BLOCK), f32),
        ((BLOCK, BLOCK), f32),
        ((PANEL, users), bf16),
        ((PANEL // width * PARTS, users), bf16),
    ]
    return pl.pallas_call(
        functools.partial(panel_kernel, views, len(pieces), width),
        out_shape=[pltpu.HBM(*out) for out in outs],
        in_specs=[pl.BlockSpec(memory_space=pltpu.SMEM)]
        + [pl.BlockSpec(memory_space=pl.ANY)] * len(pieces),
        out_specs=[pl.BlockSpec(memory_space=pltpu.HBM)] * len(outs),
        scratch_shapes=[VMEM(*one) for one in outs + held]
        + [pltpu.SemaphoreType.DMA((len(views),)), pltpu.SemaphoreType.DMA((len(outs), NBLOCKS))],
        compiler_params=pltpu.CompilerParams(vmem_limit_bytes=room(*outs, *held)),
        cost_estimate=pl.CostEstimate(flops=4 * 10**10, bytes_accessed=16 * 2**20, transcendentals=1024),
        name="factor_panel",
    )(place, *pieces)


def tile_kernel(counts, views, place_ref, regular_ref, *refs):
    factors, refs = refs[:4], refs[4:]
    pieces, refs = refs[: sum(counts)], refs[sum(counts) :]
    out_ref, refs = refs[0], refs[1:]
    high_ref, low_ref, inv_high_ref, inv_low_ref, left_high_ref, left_low_ref, wide_high_ref, wide_low_ref = refs[:8]
    panel_ref, rows_ref, cols_ref, sem, factor_sem = refs[8:]
    targets = [panel_ref] * counts[0] + [rows_ref] * counts[1] + [cols_ref] * counts[2]
    held = [targets[which] for which, *_ in views]
    views = [pieces[which].at[pl.ds(start, rows)] for which, start, rows in views]
    fetches = [
        pltpu.make_async_copy(factor, ref, factor_sem.at[i])
        for i, (factor, ref) in enumerate(zip(factors, (high_ref, low_ref, inv_high_ref, inv_low_ref)))
    ]
    for fetch in fetches:
        fetch.start()
    waits = place_pieces(place_ref, 2, views, held, sem)
    row_index, col_index = place_ref[0], place_ref[1]
    width, band = cols_ref.shape[0], rows_ref.shape[0] // (SPAN - 1)
    row_count = (SPAN - 1) * band
    panel_blocks = PANEL // width
    in_panel = col_index < panel_blocks
    slot = jnp.minimum(col_index, panel_blocks - 1)
    at = pl.ds(pl.multiple_of(slot * width, width), width)
    below, right = pl.ds(0, row_count), pl.ds(row_count, width)

    def solve(with_cols):
        for wait in waits:
            wait()
        step = min(WIDE, width)
        groups = [(rows_ref, at_row, pl.ds(at_row, band), band) for at_row in range(0, row_count, band)]
        if with_cols:
            groups = [
                (cols_ref, at_row, pl.ds(row_count + at_row, step), step) for at_row in range(0, width, step)
            ] + groups

        def grams(start):
            block = panel_ref[pl.ds(start, WIDE), :]
            return [dot_nt(ref[pl.ds(at_row, count), :], block) for ref, at_row, _, count in groups]

        columns = grams(0)
        for fetch in fetches:
            fetch.wait()

        for start in range(0, PANEL, WIDE):
            first, second = pl.ds(start, BLOCK), pl.ds(start + BLOCK, BLOCK)
            between = dot_nn3((high_ref[second, first], low_ref[second, first]), (inv_high_ref[first, :], inv_low_ref[first, :]))
            corner = split(-dot_nn3((inv_high_ref[second, :], inv_low_ref[second, :]), split(between)))
            for wide_ref, inv_ref, part in ((wide_high_ref, inv_high_ref, corner[0]), (wide_low_ref, inv_low_ref, corner[1])):
                wide_ref[first, pl.ds(0, BLOCK)] = inv_ref[first, :]
                wide_ref[first, pl.ds(BLOCK, BLOCK)] = jnp.zeros((BLOCK, BLOCK), bf16)
                wide_ref[second, pl.ds(0, BLOCK)] = part
                wide_ref[second, pl.ds(BLOCK, BLOCK)] = inv_ref[second, :]

        for start in range(0, PANEL, WIDE):
            here = pl.ds(start, WIDE)
            if start > 0:
                columns = [
                    column
                    - dot_nt3(
                        (left_high_ref[mine, :start], left_low_ref[mine, :start]), (high_ref[here, :start], low_ref[here, :start])
                    )
                    for column, (_, _, mine, _) in zip(grams(start), groups)
                ]
            for column, (_, _, mine, _) in zip(columns, groups):
                column = dot_nt3(split(column), (wide_high_ref[here, :], wide_low_ref[here, :]))
                left_high_ref[mine, here], left_low_ref[mine, here] = split(column)

    @pl.when(in_panel)
    def _():
        solve(False)
        mine = pl.ds(pl.multiple_of(row_index * band, band), band)
        out_ref[pl.ds(0, band), :] = high_ref[mine, at].astype(f32) + low_ref[mine, at].astype(f32)
        out_ref[pl.ds(band, row_count), :] = left_high_ref[below, at].astype(f32) + left_low_ref[below, at].astype(f32)

    @pl.when(jnp.logical_not(in_panel))
    def _():
        solve(True)
        out_ref[pl.ds(0, band), :] = jnp.zeros((band, width), f32)
        items = lax.broadcasted_iota(jnp.int32, (band, width), 0) + row_index * band
        columns = lax.broadcasted_iota(jnp.int32, (band, width), 1) + col_index * width
        for part in range(SPAN - 1):
            mine = pl.ds(part * band, band)
            tile = dot_nt(rows_ref[mine, :], cols_ref[...])
            tile = tile + jnp.where(items + (part + 1) * PANEL == columns, regular_ref[...], 0.0)
            out_ref[pl.ds((part + 1) * band, band), :] = tile - dot_nt3(
                (left_high_ref[mine, :], left_low_ref[mine, :]), (left_high_ref[right, :], left_low_ref[right, :])
            )


def finish_tile(place, regular, factors, panel, rows, cols, views, band, users):
    spec = pl.BlockSpec(memory_space=VMEM)
    width = regular.shape[1]
    factors = [pltpu.with_memory_space_constraint(x, pltpu.HBM) for x in factors]
    pieces = panel + rows + cols
    out = ((SPAN * band, width), f32)
    below = (SPAN - 1) * band + width
    held = [
        ((below, PANEL), bf16),
        ((below, PANEL), bf16),
        ((PANEL, WIDE), bf16),
        ((PANEL, WIDE), bf16),
        ((PANEL, users), bf16),
        (((SPAN - 1) * band, users), bf16),
        ((width, users), bf16),
    ]
    return pl.pallas_call(
        functools.partial(tile_kernel, (len(panel), len(rows), len(cols)), views),
        out_shape=jax.ShapeDtypeStruct(*out),
        in_specs=[pl.BlockSpec(memory_space=pltpu.SMEM)]
        + [spec]
        + [pl.BlockSpec(memory_space=pltpu.HBM)] * len(factors)
        + [pl.BlockSpec(memory_space=pl.ANY)] * len(pieces),
        out_specs=spec,
        scratch_shapes=[VMEM(factor.shape, factor.dtype) for factor in factors]
        + [VMEM(*one) for one in held]
        + [pltpu.SemaphoreType.DMA((len(views),)), pltpu.SemaphoreType.DMA((len(factors),))],
        compiler_params=pltpu.CompilerParams(vmem_limit_bytes=room(out, *held, *((factor.shape, factor.dtype) for factor in factors))),
        cost_estimate=pl.CostEstimate(flops=20 * 10**9, bytes_accessed=24 * 2**20, transcendentals=0),
        name="finish_tile",
    )(place, regular, *factors, *pieces)


CORES = 2


def body(interactions, regular):
    row_count, col_count = lax.axis_size("row"), lax.axis_size("col")
    row_index, col_index = lax.axis_index("row"), lax.axis_index("col")
    width, users = interactions.shape
    band = PANEL // row_count
    ways = PANEL // width
    assert row_count == CORES * ways and col_count == SPAN * ways and users >= width
    slot, way = col_index // ways, col_index % ways
    pair, core = row_index // CORES, row_index % CORES
    all_users = row_count * users

    def exchange(value, move, only=None):
        perm = []
        for source_row in range(row_count):
            for source_col in range(col_count):
                place = (source_row // CORES, source_row % CORES, source_col // ways, source_col % ways)
                if only is None or only(*place):
                    to = move(*place)
                    target = (to[0] * CORES + to[1]) * col_count + to[2] * ways + to[3]
                    perm.append((source_row * col_count + source_col, target))
        return lax.ppermute(value, ("row", "col"), perm)

    def after(value, *others):
        return lax.optimization_barrier((value, *others))[0]

    high = lax.reduce_precision(regular, 8, 7)
    middle = lax.reduce_precision(regular - high, 8, 7)
    parts = jnp.stack([high, middle, regular - high - middle]).astype(bf16)
    parts = jnp.pad(parts, ((0, PARTS - 3), (0, users - width)))

    raised = exchange(interactions, lambda p, h, s, w: (p, h, 0, w), lambda p, h, s, w: s == SPAN - 1)
    halves = (jnp.where(slot == 0, raised, interactions) if ways == 2 else interactions).reshape(CORES, band, users)
    offers = [lax.dynamic_index_in_dim(halves, core ^ flip, 0, False) for flip in range(CORES)]

    half = width // 2
    shared = jnp.concatenate([interactions, parts], 0)
    quarters, quarter_users = [], []
    reach = SPAN // 2
    while reach:
        got = exchange(
            shared, lambda p, h, s, w: (p, h, s + reach, w), lambda p, h, s, w: s % (2 * reach) == 0
        )
        if reach == SPAN // 2:
            for turn in range(ways):
                for flip in range(CORES):
                    quarters.append(
                        exchange(offers[flip], lambda p, h, s, w: (w, h ^ flip, s, (p + turn) % ways))
                    )
                    quarter_users.append(((way - turn) % ways * CORES + (core ^ flip)) * users)
        shared = jnp.where(slot % (2 * reach) == reach, got, shared)
        reach //= 2
    quarters = jnp.concatenate(quarters, 0)

    def numbers(values):
        return jnp.stack([jnp.asarray(v, jnp.int32) for v in values])

    panel, panel_views, panel_place, part_views, part_place = [], [], [], [], []
    cols, cols_place = [interactions], [0, row_index * users]
    rows, rows_views, rows_place = [], [], []

    def over_core(value):
        return exchange(value, lambda p, h, s, w: (p, 1 - h, s, w))

    def over_pair(value):
        return exchange(value, lambda p, h, s, w: (1 - p, h, s, w))

    def over_way(value, only=None):
        return exchange(value, lambda p, h, s, w: (p, h, s, 1 - w), only)

    if ways == 2:
        twin_items = over_core(interactions)
        shared = after(shared, quarters, twin_items)
        pair_side, way_side = over_pair(shared), over_way(shared)
        own_twin = over_core(shared)
        diagonal = [over_way(after(pair_side, own_twin)[:half]), over_pair(after(way_side, own_twin)[half:])]
        for from_pair, from_way, first_row, piece in (
            (pair, way, 0, shared),
            (1 - pair, way, 0, pair_side),
            (pair, 1 - way, 0, way_side),
            (1 - pair, 1 - way, 0, diagonal[0]),
            (1 - pair, 1 - way, half, diagonal[1]),
        ):
            twin = own_twin if piece is shared else over_core(piece)
            for from_core, value in ((core, piece), (1 - core, twin)):
                if value is shared or value is way_side:
                    part_views.append((len(panel), width, PARTS, True))
                    part_place += [from_way * PARTS, 0]
                count = min(value.shape[0], half if value.shape[0] < width else width)
                panel_views.append((len(panel), 0, count, False))
                panel_place += [from_way * width + first_row, (from_pair * CORES + from_core) * users]
                panel.append(value)
        crossed = [pair_side, way_side, *diagonal]
        held = after(interactions, *crossed)
        cols += [twin_items, over_pair(held), exchange(held, lambda p, h, s, w: (1 - p, 1 - h, s, w))]
        cols_place += [0, (row_index ^ 1) * users, 0, (row_index ^ 2) * users, 0, (row_index ^ 3) * users]
        first = exchange(quarters, lambda p, h, s, w: (p, h, s - 1, w), lambda p, h, s, w: s > 0)
        relayed, ready = lax.optimization_barrier((first, quarters, *crossed))[:2]
        second = exchange(relayed, lambda p, h, s, w: (p, h, s - 1, w), lambda p, h, s, w: 0 < s < SPAN - 1)
        ring = exchange(ready, lambda p, h, s, w: (p, h, s + 1, w), lambda p, h, s, w: 0 < s < SPAN - 1)
        leap = exchange(ready, lambda p, h, s, w: (p, h, s + 2, w), lambda p, h, s, w: s == 1)
        rows = [quarters, first, second, ring, leap]
        from_slots = [
            jnp.where(slot == 0, 3, slot),
            jnp.where(slot < 3, slot + 1, 0),
            jnp.where(slot < 2, slot + 2, 0),
            jnp.where(slot > 1, slot - 1, 0),
            jnp.where(slot == 3, 1, 0),
        ]
        for from_slot, piece in enumerate(rows):
            for which, from_users in enumerate(quarter_users):
                rows_views.append((from_slot, which * band, band))
                rows_place += [(from_slots[from_slot] - 1) * band, from_users]
    else:
        groups = [[s * ways + w for w in range(ways)] for s in range(SPAN)]
        shared = lax.all_gather(shared, "col", axis=0, axis_index_groups=groups)
        parts = shared[:, width:].reshape(ways * PARTS, users)
        shared = shared[:, :width].reshape(PANEL, users)
        panel, panel_place = [lax.all_gather(shared, "row", axis=1, tiled=True), parts], [0, 0]
        panel_views = [(0, 0, PANEL, False)]
        part_views, part_place = [(1, 0, ways * PARTS, True)], [0, 0]
        cols, cols_place = [lax.all_gather(interactions, "row", axis=1, tiled=True)], [0, 0]
        groups = [[s * ways + w for s in range(SPAN)] for w in range(ways)]
        rows = [lax.all_gather(quarters, "col", axis=0, tiled=True, axis_index_groups=groups)]
        for from_slot in range(1, SPAN):
            for which, from_users in enumerate(quarter_users):
                rows_views.append((0, (from_slot * len(quarter_users) + which) * band, band))
                rows_place += [(from_slot - 1) * band, from_users]

    factors = factor_panel(
        numbers(panel_place + part_place), panel, panel_views + part_views, width, all_users
    )
    views = [view[:3] for view in panel_views]
    views += [(len(panel) + i, start, count) for i, start, count in rows_views]
    views += [(len(panel) + len(rows) + i, 0, width) for i in range(len(cols))]
    tile = finish_tile(
        numbers([row_index, col_index] + panel_place + rows_place + cols_place),
        regular[None, :], factors, panel, rows, cols, views, band, all_users,
    )
    return tile.reshape(SPAN, band, width)


def solution(mesh):
    return jax.shard_map(
        body,
        mesh=mesh,
        in_specs=(P("col", "row"), P("col")),
        out_specs=P(None, "row", "col"),
        check_vma=False,
    )
```

```python
import functools
import math
import jax
import jax.numpy as jnp
from jax import lax
from jax.experimental import pallas as pl
from jax.experimental.pallas import tpu as pltpu
from jax.sharding import PartitionSpec as P

PANEL = 1024
SPAN = 4
BLOCK = 128
WIDE = 256
SUB = 8
NBLOCKS = PANEL // BLOCK
PARTS = 16
VMEM = pltpu.VMEM
f32 = jnp.float32
bf16 = jnp.bfloat16


def dot_nt(a, b):
    return lax.dot_general(a, b, (((1,), (1,)), ((), ())), preferred_element_type=f32)


def split(value):
    high = value.astype(bf16)
    return high, (value - high.astype(f32)).astype(bf16)


def dot_nt3(a, b):
    return dot_nt(a[0], b[0]) + (dot_nt(a[0], b[1]) + dot_nt(a[1], b[0]))


def dot_nn3(a, b):
    def dot(x, y):
        return jnp.dot(x, y, preferred_element_type=f32)

    return dot(a[0], b[0]) + (dot(a[0], b[1]) + dot(a[1], b[0]))


def lanes(value, lane):
    return jnp.broadcast_to(value[:, lane : lane + 1], (SUB, BLOCK))


def sublanes(value, row):
    return jnp.broadcast_to(value[row : row + 1, :], (SUB, BLOCK))


def factor_block(block_ref, inverse_ref):
    tiles_count = BLOCK // SUB
    row_in_tile = lax.broadcasted_iota(jnp.int32, (SUB, BLOCK), 0)
    lane = lax.broadcasted_iota(jnp.int32, (SUB, BLOCK), 1)
    sides = [block_ref[pl.ds(SUB * t, SUB), :] for t in range(tiles_count)]
    inverses = [(lane == row_in_tile + SUB * t).astype(f32) for t in range(tiles_count)]
    uppers = []
    for step in range(tiles_count):
        base = SUB * step
        side, inverse = sides[step], inverses[step]
        if step == 0:
            columns = [lanes(side, base + b) for b in range(SUB)]
        entry = {(a, b): sublanes(columns[b], a) for b in range(SUB) for a in range(b, SUB)}
        vectors = [[sublanes(side, a) for a in range(SUB)], [sublanes(inverse, a) for a in range(SUB)]]
        if step + 1 < tiles_count:
            vectors.append([lanes(sides[step + 1], base + b) for b in range(SUB)])
            columns = [lanes(sides[step + 1], base + SUB + b) for b in range(SUB)]
        scale = [None] * SUB
        for m in range(0, SUB, 2):
            n = m + 1
            first, cross, second = entry[m, m], entry[n, m], entry[n, n]
            root = lax.rsqrt(first)
            det_root = lax.rsqrt(first * second - cross * cross)
            scale[m], scale[n] = root, det_root * (first * root)
            det_square = det_root * det_root
            link = cross * root
            entry[n, m] = link
            rest = range(n + 1, SUB)
            for x in rest:
                entry[x, m] = entry[x, m] * root
                entry[x, n] = entry[x, n] - entry[x, m] * link
            weighted = {x: entry[x, n] * first for x in rest}
            for y in rest:
                for x in range(y, SUB):
                    entry[x, y] = (entry[x, y] - entry[x, m] * entry[y, m]) - (weighted[x] * entry[y, n]) * det_square
            for x in rest:
                entry[x, n] = entry[x, n] * scale[n]
            for vector in vectors:
                vector[m] = vector[m] * root
                vector[n] = (vector[n] - link * vector[m]) * scale[n]
                for x in rest:
                    vector[x] = (vector[x] - entry[x, m] * vector[m]) - entry[x, n] * vector[n]
            if step + 1 < tiles_count:
                left, right = vectors[2][m], vectors[2][n]
                columns = [
                    (column - left * sublanes(left, b)) - right * sublanes(right, b)
                    for b, column in enumerate(columns)
                ]
        tops, insides = vectors[:2]
        upper, lower_inverse = tops[0], insides[0]
        for m in range(1, SUB):
            upper = jnp.where(row_in_tile == m, tops[m], upper)
            lower_inverse = jnp.where(row_in_tile == m, insides[m], lower_inverse)
        uppers.append(jnp.where(lane >= row_in_tile + base, upper, 0.0))
        inverse_ref[pl.ds(base, SUB), :] = lower_inverse
        if step + 1 < tiles_count:
            ahead = vectors[2]
            for m in range(SUB):
                sides[step + 1] = sides[step + 1] - ahead[m] * tops[m]
                inverses[step + 1] = inverses[step + 1] - ahead[m] * insides[m]
        if step + 2 < tiles_count:
            weights_top, weights_in = [None] * SUB, [None] * SUB
            for m in reversed(range(SUB)):
                top, inside = tops[m], insides[m]
                for b in range(m + 1, SUB):
                    top = top - entry[b, m] * weights_top[b]
                    inside = inside - entry[b, m] * weights_in[b]
                weights_top[m], weights_in[m] = top * scale[m], inside * scale[m]
            for t in range(step + 2, tiles_count):
                for m in range(SUB):
                    column = lanes(sides[t], base + m)
                    if m == 0:
                        top_sum, in_sum = column * weights_top[m], column * weights_in[m]
                    else:
                        top_sum = top_sum + column * weights_top[m]
                        in_sum = in_sum + column * weights_in[m]
                sides[t] = sides[t] - top_sum
                inverses[t] = inverses[t] - in_sum
    block_ref[...] = jnp.concatenate(uppers, 0).T


def place_pieces(place_ref, first, pieces, helds, sem):
    waits = []
    for i, (piece, held_ref) in enumerate(zip(pieces, helds)):
        rows, users = piece.shape
        row = place_ref[first + 2 * i]
        user = pl.multiple_of(place_ref[first + 2 * i + 1], users)
        to = held_ref.at[pl.ds(pl.multiple_of(jnp.maximum(row, 0), rows), rows), pl.ds(user, users)]
        copy = pltpu.make_async_copy(piece, to, sem.at[i])
        pl.when(row >= 0)(copy.start)
        waits.append(functools.partial(pl.when(row >= 0), copy.wait))
    return waits


def panel_kernel(views, count, width, place_ref, *refs):
    pieces, refs = refs[:count], refs[count:]
    outs, (high_ref, low_ref, inv_high_ref, inv_low_ref, lower_ref, coming_ref, *refs) = refs[:4], refs[4:]
    block_ref, inverse_ref, items_ref, parts_ref, sem, out_sem = refs
    held = [parts_ref if is_part else items_ref for _, _, _, is_part in views]
    views = [pieces[which].at[pl.ds(start, rows)] for which, start, rows, _ in views]
    waits = place_pieces(place_ref, 0, views, held, sem)
    for k in range(1, NBLOCKS):
        for ref in (high_ref, low_ref):
            ref[pl.ds(0, k * BLOCK), pl.ds(k * BLOCK, BLOCK)] = jnp.zeros((k * BLOCK, BLOCK), bf16)
    for wait in waits:
        wait()
    on_diagonal = lax.broadcasted_iota(jnp.int32, (BLOCK, BLOCK), 0) == lax.broadcasted_iota(
        jnp.int32, (BLOCK, BLOCK), 1
    )

    def before(k):
        start = k * BLOCK
        here, rest = pl.ds(start, BLOCK), pl.ds(start, PANEL - start)
        if k % 2 == 0:
            both = pl.ds(start, 2 * BLOCK)
            columns = dot_nt(items_ref[rest, :], items_ref[both, :])
            if k > 0:
                columns = columns - dot_nt3(
                    (high_ref[rest, :start], low_ref[rest, :start]), (high_ref[both, :start], low_ref[both, :start])
                )
            column = columns[:, :BLOCK]
            coming_ref[pl.ds(start + BLOCK, PANEL - start - BLOCK), :] = columns[BLOCK:, BLOCK:]
        else:
            last = pl.ds(start - BLOCK, BLOCK)
            high, low = high_ref[rest, last], low_ref[rest, last]
            column = coming_ref[rest, :] - dot_nt3((high, low), (high[:BLOCK], low[:BLOCK]))
        part, lane = PARTS * (start // width), start % width
        parts = parts_ref[pl.ds(part, PARTS), pl.ds(lane, BLOCK)].astype(f32)
        block_ref[...] = column[:BLOCK] + jnp.where(on_diagonal, parts[0:1] + parts[1:2] + parts[2:3], 0.0)
        if k + 1 < NBLOCKS:
            lower_ref[pl.ds(start + BLOCK, PANEL - start - BLOCK), :] = column[BLOCK:]

    def after(k):
        start = k * BLOCK
        here = pl.ds(start, BLOCK)
        inverse = split(inverse_ref[...])
        inv_high_ref[here, :], inv_low_ref[here, :] = inverse
        high_ref[here, here], low_ref[here, here] = split(block_ref[...])
        if k + 1 < NBLOCKS:
            rest = pl.ds(start + BLOCK, PANEL - start - BLOCK)
            high_ref[rest, here], low_ref[rest, here] = split(dot_nt3(split(lower_ref[rest, :]), inverse))

    def leave(k):
        column = pl.ds(k * BLOCK, BLOCK)
        return [
            pltpu.make_async_copy(high_ref.at[:, column], outs[0].at[:, column], out_sem.at[0, k]),
            pltpu.make_async_copy(low_ref.at[:, column], outs[1].at[:, column], out_sem.at[1, k]),
            pltpu.make_async_copy(inv_high_ref.at[column, :], outs[2].at[column, :], out_sem.at[2, k]),
            pltpu.make_async_copy(inv_low_ref.at[column, :], outs[3].at[column, :], out_sem.at[3, k]),
        ]

    before(0)

    def turn(k, carry):
        factor_block(block_ref, inverse_ref)
        for which in range(NBLOCKS):

            @pl.when(k == which)
            def _():
                after(which)
                for copy in leave(which):
                    copy.start()
                if which + 1 < NBLOCKS:
                    before(which + 1)

        return carry

    lax.fori_loop(0, NBLOCKS, turn, 0)
    for k in range(NBLOCKS):
        for copy in leave(k):
            copy.wait()


def room(*arrays):
    return sum(math.prod(shape) * jnp.dtype(dtype).itemsize for shape, dtype in arrays) + 8 * 2**20


def factor_panel(place, pieces, views, width, users):
    outs = [
        ((PANEL, PANEL), bf16),
        ((PANEL, PANEL), bf16),
        ((PANEL, BLOCK), bf16),
        ((PANEL, BLOCK), bf16),
    ]
    held = [
        ((PANEL, BLOCK), f32),
        ((PANEL, BLOCK), f32),
        ((BLOCK, BLOCK), f32),
        ((BLOCK, BLOCK), f32),
        ((PANEL, users), bf16),
        ((PANEL // width * PARTS, users), bf16),
    ]
    return pl.pallas_call(
        functools.partial(panel_kernel, views, len(pieces), width),
        out_shape=[pltpu.HBM(*out) for out in outs],
        in_specs=[pl.BlockSpec(memory_space=pltpu.SMEM)]
        + [pl.BlockSpec(memory_space=pl.ANY)] * len(pieces),
        out_specs=[pl.BlockSpec(memory_space=pltpu.HBM)] * len(outs),
        scratch_shapes=[VMEM(*one) for one in outs + held]
        + [pltpu.SemaphoreType.DMA((len(views),)), pltpu.SemaphoreType.DMA((len(outs), NBLOCKS))],
        compiler_params=pltpu.CompilerParams(vmem_limit_bytes=room(*outs, *held)),
        cost_estimate=pl.CostEstimate(flops=8 * 10**9, bytes_accessed=2**20, transcendentals=1024),
        name="factor_panel",
    )(place, *pieces)


def tile_kernel(total, counts, views, place_ref, regular_ref, *refs):
    factors, refs = refs[:4], refs[4:]
    pieces, refs = refs[:total], refs[total:]
    out_ref, refs = refs[0], refs[1:]
    high_ref, low_ref, inv_high_ref, inv_low_ref, left_high_ref, left_low_ref, wide_high_ref, wide_low_ref = refs[:8]
    panel_ref, rows_ref, cols_ref, sem, factor_sem = refs[8:]
    held = [ref for ref, count in zip((panel_ref, rows_ref, cols_ref), counts) for _ in range(count)]
    views = [pieces[which].at[pl.ds(start, rows)] for which, start, rows in views]
    fetches = [
        pltpu.make_async_copy(factor, ref, factor_sem.at[i])
        for i, (factor, ref) in enumerate(zip(factors, (high_ref, low_ref, inv_high_ref, inv_low_ref)))
    ]
    for fetch in fetches:
        fetch.start()
    waits = place_pieces(place_ref, 2, views, held, sem)
    row_index, col_index = place_ref[0], place_ref[1]
    width, band = cols_ref.shape[0], rows_ref.shape[0] // (SPAN - 1)
    row_count = (SPAN - 1) * band
    panel_blocks = PANEL // width
    in_panel = col_index < panel_blocks
    slot = jnp.minimum(col_index, panel_blocks - 1)
    at = pl.ds(pl.multiple_of(slot * width, width), width)
    below, right = pl.ds(0, row_count), pl.ds(row_count, width)

    def solve(with_cols):
        for wait in waits:
            wait()
        step = min(WIDE, width)
        groups = [(rows_ref, at_row, pl.ds(at_row, band), band) for at_row in range(0, row_count, band)]
        if with_cols:
            groups = [
                (cols_ref, at_row, pl.ds(row_count + at_row, step), step) for at_row in range(0, width, step)
            ] + groups

        def grams(start):
            block = panel_ref[pl.ds(start, WIDE), :]
            return [dot_nt(ref[pl.ds(at_row, count), :], block) for ref, at_row, _, count in groups]

        columns = grams(0)
        for fetch in fetches:
            fetch.wait()

        for start in range(0, PANEL, WIDE):
            first, second = pl.ds(start, BLOCK), pl.ds(start + BLOCK, BLOCK)
            between = dot_nn3((high_ref[second, first], low_ref[second, first]), (inv_high_ref[first, :], inv_low_ref[first, :]))
            corner = split(-dot_nn3((inv_high_ref[second, :], inv_low_ref[second, :]), split(between)))
            for wide_ref, inv_ref, part in ((wide_high_ref, inv_high_ref, corner[0]), (wide_low_ref, inv_low_ref, corner[1])):
                wide_ref[first, pl.ds(0, BLOCK)] = inv_ref[first, :]
                wide_ref[first, pl.ds(BLOCK, BLOCK)] = jnp.zeros((BLOCK, BLOCK), bf16)
                wide_ref[second, pl.ds(0, BLOCK)] = part
                wide_ref[second, pl.ds(BLOCK, BLOCK)] = inv_ref[second, :]

        for start in range(0, PANEL, WIDE):
            here = pl.ds(start, WIDE)
            if start > 0:
                columns = [
                    column
                    - dot_nt3(
                        (left_high_ref[mine, :start], left_low_ref[mine, :start]), (high_ref[here, :start], low_ref[here, :start])
                    )
                    for column, (_, _, mine, _) in zip(grams(start), groups)
                ]
            for column, (_, _, mine, _) in zip(columns, groups):
                column = dot_nt3(split(column), (wide_high_ref[here, :], wide_low_ref[here, :]))
                left_high_ref[mine, here], left_low_ref[mine, here] = split(column)

    @pl.when(in_panel)
    def _():
        solve(False)
        mine = pl.ds(pl.multiple_of(row_index * band, band), band)
        out_ref[pl.ds(0, band), :] = high_ref[mine, at].astype(f32) + low_ref[mine, at].astype(f32)
        out_ref[pl.ds(band, row_count), :] = left_high_ref[below, at].astype(f32) + left_low_ref[below, at].astype(f32)

    @pl.when(jnp.logical_not(in_panel))
    def _():
        solve(True)
        out_ref[pl.ds(0, band), :] = jnp.zeros((band, width), f32)
        items = lax.broadcasted_iota(jnp.int32, (band, width), 0) + row_index * band
        columns = lax.broadcasted_iota(jnp.int32, (band, width), 1) + col_index * width
        for part in range(SPAN - 1):
            mine = pl.ds(part * band, band)
            tile = dot_nt(rows_ref[mine, :], cols_ref[...])
            tile = tile + jnp.where(items + (part + 1) * PANEL == columns, regular_ref[...], 0.0)
            out_ref[pl.ds((part + 1) * band, band), :] = tile - dot_nt3(
                (left_high_ref[mine, :], left_low_ref[mine, :]), (left_high_ref[right, :], left_low_ref[right, :])
            )


def finish_tile(place, regular, factors, panel, rows, cols, counts, views, band, users):
    spec = pl.BlockSpec(memory_space=VMEM)
    width = regular.shape[1]
    factors = [pltpu.with_memory_space_constraint(x, pltpu.HBM) for x in factors]
    pieces = panel + rows + cols
    out = ((SPAN * band, width), f32)
    below = (SPAN - 1) * band + width
    held = [
        ((below, PANEL), bf16),
        ((below, PANEL), bf16),
        ((PANEL, WIDE), bf16),
        ((PANEL, WIDE), bf16),
        ((PANEL, users), bf16),
        (((SPAN - 1) * band, users), bf16),
        ((width, users), bf16),
    ]
    return pl.pallas_call(
        functools.partial(tile_kernel, len(pieces), counts, views),
        out_shape=jax.ShapeDtypeStruct(*out),
        in_specs=[pl.BlockSpec(memory_space=pltpu.SMEM)]
        + [spec]
        + [pl.BlockSpec(memory_space=pltpu.HBM)] * len(factors)
        + [pl.BlockSpec(memory_space=pl.ANY)] * len(pieces),
        out_specs=spec,
        scratch_shapes=[VMEM(factor.shape, factor.dtype) for factor in factors]
        + [VMEM(*one) for one in held]
        + [pltpu.SemaphoreType.DMA((len(views),)), pltpu.SemaphoreType.DMA((len(factors),))],
        compiler_params=pltpu.CompilerParams(vmem_limit_bytes=room(out, *held, *((factor.shape, factor.dtype) for factor in factors))),
        cost_estimate=pl.CostEstimate(flops=20 * 10**9, bytes_accessed=24 * 2**20, transcendentals=0),
        name="finish_tile",
    )(place, regular, *factors, *pieces)


CORES = 2


def body(interactions, regular):
    row_count, col_count = lax.axis_size("row"), lax.axis_size("col")
    row_index, col_index = lax.axis_index("row"), lax.axis_index("col")
    width, users = interactions.shape
    band = PANEL // row_count
    ways = PANEL // width
    assert row_count == CORES * ways and col_count == SPAN * ways and users >= width
    slot, way = col_index // ways, col_index % ways
    pair, core = row_index // CORES, row_index % CORES
    all_users = row_count * users

    def exchange(value, move, only=None):
        perm = []
        for source_row in range(row_count):
            for source_col in range(col_count):
                place = (source_row // CORES, source_row % CORES, source_col // ways, source_col % ways)
                if only is None or only(*place):
                    to = move(*place)
                    target = (to[0] * CORES + to[1]) * col_count + to[2] * ways + to[3]
                    perm.append((source_row * col_count + source_col, target))
        return lax.ppermute(value, ("row", "col"), perm)

    def after(value, *others):
        return lax.optimization_barrier((value, *others))[0]

    high = lax.reduce_precision(regular, 8, 7)
    middle = lax.reduce_precision(regular - high, 8, 7)
    parts = jnp.stack([high, middle, regular - high - middle]).astype(bf16)
    parts = jnp.pad(parts, ((0, PARTS - 3), (0, users - width)))

    def over_core(value, only=None):
        return exchange(value, lambda p, h, s, w: (p, 1 - h, s, w), only)

    def over_pair(value):
        return exchange(value, lambda p, h, s, w: (1 - p, h, s, w))

    def over_way(value):
        return exchange(value, lambda p, h, s, w: (p, h, s, 1 - w))

    def traded(items, only):
        halves = items.reshape(CORES, band, users)
        kept, given = (lax.dynamic_index_in_dim(halves, core ^ flip, 0, False) for flip in range(CORES))
        return jnp.concatenate([kept, over_core(given, only)], 0)

    paired = traded(interactions, lambda p, h, s, w: s > 0)
    if ways == 2:
        raised = exchange(interactions, lambda p, h, s, w: (p, h, 0, w), lambda p, h, s, w: s == SPAN - 1)

    half = width // 2
    shared = jnp.concatenate([interactions, parts], 0)
    quarters, quarter_users = [], []
    reach = SPAN // 2
    while reach:
        got = exchange(
            shared, lambda p, h, s, w: (p, h, s + reach, w), lambda p, h, s, w: s % (2 * reach) == 0
        )
        if reach == SPAN // 2:
            for turn in range(ways):
                quarters.append(
                    exchange(
                        paired, lambda p, h, s, w: (w, h, s, (p + turn) % ways), lambda p, h, s, w: s > 0
                    )
                )
                quarter_users += [((way - turn) % ways * CORES + (core ^ flip)) * users for flip in range(CORES)]
            if ways == 2:
                got = after(got, raised)
        shared = jnp.where(slot % (2 * reach) == reach, got, shared)
        reach //= 2
    quarters = jnp.concatenate(quarters, 0)

    def numbers(values):
        return jnp.stack([jnp.asarray(v, jnp.int32) for v in values])

    panel, panel_views, panel_place, part_views, part_place = [], [], [], [], []
    cols, cols_place = [interactions], [0, row_index * users]
    rows, rows_views, rows_place = [], [], []

    if ways == 2:
        twin_items = over_core(interactions)
        mixed = jnp.where(slot == 0, traded(raised, lambda p, h, s, w: s == 0), interactions)
        shared = after(shared, quarters, twin_items, mixed)
        pair_side, way_side = over_pair(shared), over_way(shared)
        own_twin, way_twin = over_core(shared), over_core(way_side)
        diagonal = [over_way(after(pair_side, own_twin, way_twin)[:half]), over_pair(after(way_side, own_twin)[half:])]
        for from_pair, from_way, first_row, piece in (
            (pair, way, 0, shared),
            (1 - pair, way, 0, pair_side),
            (pair, 1 - way, 0, way_side),
            (1 - pair, 1 - way, 0, diagonal[0]),
            (1 - pair, 1 - way, half, diagonal[1]),
        ):
            twin = own_twin if piece is shared else way_twin if piece is way_side else over_core(piece)
            for from_core, value in ((core, piece), (1 - core, twin)):
                if value is shared or value is way_side:
                    part_views.append((len(panel), width, PARTS, True))
                    part_place += [from_way * PARTS, 0]
                count = min(value.shape[0], half if value.shape[0] < width else width)
                panel_views.append((len(panel), 0, count, False))
                panel_place += [from_way * width + first_row, (from_pair * CORES + from_core) * users]
                panel.append(value)
        crossed = [pair_side, way_side, *diagonal]
        down = exchange(quarters, lambda p, h, s, w: (p, h, s - 1, w), lambda p, h, s, w: s > 0)
        up = exchange(quarters, lambda p, h, s, w: (p, h, s + 1, w), lambda p, h, s, w: 0 < s < SPAN - 1)
        down_held, up_held, mixed = lax.optimization_barrier(
            (down, up, mixed, *crossed)
        )[:3]
        down_again = exchange(down_held, lambda p, h, s, w: (p, h, s - 1, w), lambda p, h, s, w: 0 < s < SPAN - 1)
        up_again = exchange(up_held, lambda p, h, s, w: (p, h, s + 1, w), lambda p, h, s, w: s == 2)
        rows = [quarters, down, down_again, up, up_again]
        from_slots = [
            slot,
            jnp.where(slot < 3, slot + 1, 0),
            jnp.where(slot < 2, slot + 2, 0),
            jnp.where(slot > 1, slot - 1, 0),
            jnp.where(slot == 3, 1, 0),
        ]
        cols += [twin_items]
        cols_place += [0, (row_index ^ 1) * users]
        for turn in range(ways):
            mix = exchange(
                mixed, lambda p, h, s, w: (w, h, s, (p + turn) % ways) if s == 0 else (1 - p, h ^ turn, s, w)
            )
            cols.append(mix)
            cols_place += [jnp.where(slot == 0, -1, 0), (row_index ^ (CORES + turn)) * users]
        for from_slot, piece in enumerate(rows):
            for which, from_users in enumerate(quarter_users):
                rows_views.append((from_slot, which * band, band))
                rows_place += [(from_slots[from_slot] - 1) * band, from_users]
        for which, from_users in enumerate(quarter_users):
            rows_views.append((len(rows) + 2 + which // CORES, which % CORES * band, band))
            rows_place += [jnp.where(slot == 0, (SPAN - 2) * band, -1), from_users]
    else:
        groups = [[s * ways + w for w in range(ways)] for s in range(SPAN)]
        shared = lax.all_gather(shared, "col", axis=0, axis_index_groups=groups)
        parts = shared[:, width:].reshape(ways * PARTS, users)
        shared = shared[:, :width].reshape(PANEL, users)
        panel, panel_place = [lax.all_gather(shared, "row", axis=1, tiled=True), parts], [0, 0]
        panel_views = [(0, 0, PANEL, False)]
        part_views, part_place = [(1, 0, ways * PARTS, True)], [0, 0]
        cols, cols_place = [lax.all_gather(interactions, "row", axis=1, tiled=True)], [0, 0]
        groups = [[s * ways + w for s in range(SPAN)] for w in range(ways)]
        rows = [lax.all_gather(quarters, "col", axis=0, tiled=True, axis_index_groups=groups)]
        for from_slot in range(1, SPAN):
            for which, from_users in enumerate(quarter_users):
                rows_views.append((0, (from_slot * len(quarter_users) + which) * band, band))
                rows_place += [(from_slot - 1) * band, from_users]

    factors = factor_panel(
        numbers(panel_place + part_place), panel, panel_views + part_views, width, all_users
    )
    views = [view[:3] for view in panel_views]
    views += [(len(panel) + i, start, count) for i, start, count in rows_views]
    views += [(len(panel) + len(rows) + i, 0, width) for i in range(len(cols))]
    counts = len(panel_views), len(rows_views), len(cols)
    tile = finish_tile(
        numbers([row_index, col_index] + panel_place + rows_place + cols_place),
        regular[None, :], factors, panel, rows, cols, counts, views, band, all_users,
    )
    return tile.reshape(SPAN, band, width)


def solution(mesh):
    return jax.shard_map(
        body,
        mesh=mesh,
        in_specs=(P("col", "row"), P("col")),
        out_specs=P(None, "row", "col"),
        check_vma=False,
    )
```

```python
import functools
import math
import jax
import jax.numpy as jnp
from jax import lax
from jax.experimental import pallas as pl
from jax.experimental.pallas import tpu as pltpu
from jax.sharding import PartitionSpec as P

PANEL = 1024
SPAN = 4
BLOCK = 128
WIDE = 256
SUB = 8
NBLOCKS = PANEL // BLOCK
PARTS = 16
VMEM = pltpu.VMEM
f32 = jnp.float32
bf16 = jnp.bfloat16


def dot_nt(a, b):
    return lax.dot_general(a, b, (((1,), (1,)), ((), ())), preferred_element_type=f32)


def split(value):
    high = value.astype(bf16)
    return high, (value - high.astype(f32)).astype(bf16)


def dot_nt3(a, b):
    return dot_nt(a[0], b[0]) + (dot_nt(a[0], b[1]) + dot_nt(a[1], b[0]))


def dot_nn3(a, b):
    def dot(x, y):
        return jnp.dot(x, y, preferred_element_type=f32)

    return dot(a[0], b[0]) + (dot(a[0], b[1]) + dot(a[1], b[0]))


def lanes(value, lane):
    return jnp.broadcast_to(value[:, lane : lane + 1], (SUB, BLOCK))


def sublanes(value, row):
    return jnp.broadcast_to(value[row : row + 1, :], (SUB, BLOCK))


def factor_block(block_ref, inverse_ref):
    tiles_count = BLOCK // SUB
    row_in_tile = lax.broadcasted_iota(jnp.int32, (SUB, BLOCK), 0)
    lane = lax.broadcasted_iota(jnp.int32, (SUB, BLOCK), 1)
    sides = [block_ref[pl.ds(SUB * t, SUB), :] for t in range(tiles_count)]
    inverses = [(lane == row_in_tile + SUB * t).astype(f32) for t in range(tiles_count)]
    uppers = []
    for step in range(tiles_count):
        base = SUB * step
        side, inverse = sides[step], inverses[step]
        if step == 0:
            columns = [lanes(side, base + b) for b in range(SUB)]
        entry = {(a, b): sublanes(columns[b], a) for b in range(SUB) for a in range(b, SUB)}
        vectors = [[sublanes(side, a) for a in range(SUB)], [sublanes(inverse, a) for a in range(SUB)]]
        if step + 1 < tiles_count:
            vectors.append([lanes(sides[step + 1], base + b) for b in range(SUB)])
            columns = [lanes(sides[step + 1], base + SUB + b) for b in range(SUB)]
        scale = [None] * SUB
        for m in range(0, SUB, 2):
            n = m + 1
            first, cross, second = entry[m, m], entry[n, m], entry[n, n]
            root = lax.rsqrt(first)
            det_root = lax.rsqrt(first * second - cross * cross)
            scale[m], scale[n] = root, det_root * (first * root)
            det_square = det_root * det_root
            link = cross * root
            entry[n, m] = link
            rest = range(n + 1, SUB)
            for x in rest:
                entry[x, m] = entry[x, m] * root
                entry[x, n] = entry[x, n] - entry[x, m] * link
            weighted = {x: entry[x, n] * first for x in rest}
            for y in rest:
                for x in range(y, SUB):
                    entry[x, y] = (entry[x, y] - entry[x, m] * entry[y, m]) - (weighted[x] * entry[y, n]) * det_square
            for x in rest:
                entry[x, n] = entry[x, n] * scale[n]
            for vector in vectors:
                vector[m] = vector[m] * root
                vector[n] = (vector[n] - link * vector[m]) * scale[n]
                for x in rest:
                    vector[x] = (vector[x] - entry[x, m] * vector[m]) - entry[x, n] * vector[n]
            if step + 1 < tiles_count:
                left, right = vectors[2][m], vectors[2][n]
                columns = [
                    (column - left * sublanes(left, b)) - right * sublanes(right, b)
                    for b, column in enumerate(columns)
                ]
        tops, insides = vectors[:2]
        upper, lower_inverse = tops[0], insides[0]
        for m in range(1, SUB):
            upper = jnp.where(row_in_tile == m, tops[m], upper)
            lower_inverse = jnp.where(row_in_tile == m, insides[m], lower_inverse)
        uppers.append(jnp.where(lane >= row_in_tile + base, upper, 0.0))
        inverse_ref[pl.ds(base, SUB), :] = lower_inverse
        if step + 1 < tiles_count:
            ahead = vectors[2]
            for m in range(SUB):
                sides[step + 1] = sides[step + 1] - ahead[m] * tops[m]
                inverses[step + 1] = inverses[step + 1] - ahead[m] * insides[m]
        if step + 2 < tiles_count:
            weights_top, weights_in = [None] * SUB, [None] * SUB
            for m in reversed(range(SUB)):
                top, inside = tops[m], insides[m]
                for b in range(m + 1, SUB):
                    top = top - entry[b, m] * weights_top[b]
                    inside = inside - entry[b, m] * weights_in[b]
                weights_top[m], weights_in[m] = top * scale[m], inside * scale[m]
            for t in range(step + 2, tiles_count):
                for m in range(SUB):
                    column = lanes(sides[t], base + m)
                    if m == 0:
                        top_sum, in_sum = column * weights_top[m], column * weights_in[m]
                    else:
                        top_sum = top_sum + column * weights_top[m]
                        in_sum = in_sum + column * weights_in[m]
                sides[t] = sides[t] - top_sum
                inverses[t] = inverses[t] - in_sum
    block_ref[...] = jnp.concatenate(uppers, 0).T


def place_pieces(place_ref, first, pieces, helds, sem):
    waits = []
    for i, (piece, held_ref) in enumerate(zip(pieces, helds)):
        rows, users = piece.shape
        row = place_ref[first + 2 * i]
        user = pl.multiple_of(place_ref[first + 2 * i + 1], users)
        to = held_ref.at[pl.ds(pl.multiple_of(jnp.maximum(row, 0), rows), rows), pl.ds(user, users)]
        copy = pltpu.make_async_copy(piece, to, sem.at[i])
        pl.when(row >= 0)(copy.start)
        waits.append(functools.partial(pl.when(row >= 0), copy.wait))
    return waits


def panel_kernel(views, count, width, place_ref, *refs):
    pieces, refs = refs[:count], refs[count:]
    outs, (high_ref, low_ref, inv_high_ref, inv_low_ref, lower_ref, coming_ref, *refs) = refs[:4], refs[4:]
    block_ref, inverse_ref, items_ref, parts_ref, sem, out_sem = refs
    held = [parts_ref if is_part else items_ref for _, _, _, is_part in views]
    views = [pieces[which].at[pl.ds(start, rows)] for which, start, rows, _ in views]
    waits = place_pieces(place_ref, 0, views, held, sem)
    for k in range(1, NBLOCKS):
        for ref in (high_ref, low_ref):
            ref[pl.ds(0, k * BLOCK), pl.ds(k * BLOCK, BLOCK)] = jnp.zeros((k * BLOCK, BLOCK), bf16)
    for wait in waits:
        wait()
    on_diagonal = lax.broadcasted_iota(jnp.int32, (BLOCK, BLOCK), 0) == lax.broadcasted_iota(
        jnp.int32, (BLOCK, BLOCK), 1
    )

    def before(k):
        start = k * BLOCK
        here, rest = pl.ds(start, BLOCK), pl.ds(start, PANEL - start)
        if k % 2 == 0:
            both = pl.ds(start, 2 * BLOCK)
            columns = dot_nt(items_ref[rest, :], items_ref[both, :])
            if k > 0:
                columns = columns - dot_nt3(
                    (high_ref[rest, :start], low_ref[rest, :start]), (high_ref[both, :start], low_ref[both, :start])
                )
            column = columns[:, :BLOCK]
            coming_ref[pl.ds(start + BLOCK, PANEL - start - BLOCK), :] = columns[BLOCK:, BLOCK:]
        else:
            last = pl.ds(start - BLOCK, BLOCK)
            high, low = high_ref[rest, last], low_ref[rest, last]
            column = coming_ref[rest, :] - dot_nt3((high, low), (high[:BLOCK], low[:BLOCK]))
        part, lane = PARTS * (start // width), start % width
        parts = parts_ref[pl.ds(part, PARTS), pl.ds(lane, BLOCK)].astype(f32)
        block_ref[...] = column[:BLOCK] + jnp.where(on_diagonal, parts[0:1] + parts[1:2] + parts[2:3], 0.0)
        if k + 1 < NBLOCKS:
            lower_ref[pl.ds(start + BLOCK, PANEL - start - BLOCK), :] = column[BLOCK:]

    def after(k):
        start = k * BLOCK
        here = pl.ds(start, BLOCK)
        inverse = split(inverse_ref[...])
        inv_high_ref[here, :], inv_low_ref[here, :] = inverse
        high_ref[here, here], low_ref[here, here] = split(block_ref[...])
        if k + 1 < NBLOCKS:
            rest = pl.ds(start + BLOCK, PANEL - start - BLOCK)
            high_ref[rest, here], low_ref[rest, here] = split(dot_nt3(split(lower_ref[rest, :]), inverse))

    def leave(k):
        column = pl.ds(k * BLOCK, BLOCK)
        return [
            pltpu.make_async_copy(high_ref.at[:, column], outs[0].at[:, column], out_sem.at[0, k]),
            pltpu.make_async_copy(low_ref.at[:, column], outs[1].at[:, column], out_sem.at[1, k]),
            pltpu.make_async_copy(inv_high_ref.at[column, :], outs[2].at[column, :], out_sem.at[2, k]),
            pltpu.make_async_copy(inv_low_ref.at[column, :], outs[3].at[column, :], out_sem.at[3, k]),
        ]

    before(0)

    def turn(k, carry):
        factor_block(block_ref, inverse_ref)
        for which in range(NBLOCKS):

            @pl.when(k == which)
            def _():
                after(which)
                for copy in leave(which):
                    copy.start()
                if which + 1 < NBLOCKS:
                    before(which + 1)

        return carry

    lax.fori_loop(0, NBLOCKS, turn, 0)
    for k in range(NBLOCKS):
        for copy in leave(k):
            copy.wait()


def room(*arrays):
    return sum(math.prod(shape) * jnp.dtype(dtype).itemsize for shape, dtype in arrays) + 8 * 2**20


def factor_panel(place, pieces, views, width, users):
    outs = [
        ((PANEL, PANEL), bf16),
        ((PANEL, PANEL), bf16),
        ((PANEL, BLOCK), bf16),
        ((PANEL, BLOCK), bf16),
    ]
    held = [
        ((PANEL, BLOCK), f32),
        ((PANEL, BLOCK), f32),
        ((BLOCK, BLOCK), f32),
        ((BLOCK, BLOCK), f32),
        ((PANEL, users), bf16),
        ((PANEL // width * PARTS, users), bf16),
    ]
    return pl.pallas_call(
        functools.partial(panel_kernel, views, len(pieces), width),
        out_shape=[pltpu.HBM(*out) for out in outs],
        in_specs=[pl.BlockSpec(memory_space=pltpu.SMEM)]
        + [pl.BlockSpec(memory_space=pl.ANY)] * len(pieces),
        out_specs=[pl.BlockSpec(memory_space=pltpu.HBM)] * len(outs),
        scratch_shapes=[VMEM(*one) for one in outs + held]
        + [pltpu.SemaphoreType.DMA((len(views),)), pltpu.SemaphoreType.DMA((len(outs), NBLOCKS))],
        compiler_params=pltpu.CompilerParams(vmem_limit_bytes=room(*outs, *held)),
        cost_estimate=pl.CostEstimate(flops=8 * 10**9, bytes_accessed=2**20, transcendentals=1024),
        name="factor_panel",
    )(place, *pieces)


def tile_kernel(total, counts, views, place_ref, regular_ref, *refs):
    factors, refs = refs[:4], refs[4:]
    pieces, refs = refs[:total], refs[total:]
    out_ref, refs = refs[0], refs[1:]
    high_ref, low_ref, inv_high_ref, inv_low_ref, left_high_ref, left_low_ref, wide_high_ref, wide_low_ref = refs[:8]
    panel_ref, rows_ref, cols_ref, sem, factor_sem = refs[8:]
    held = [ref for ref, count in zip((panel_ref, rows_ref, cols_ref), counts) for _ in range(count)]
    views = [pieces[which].at[pl.ds(start, rows)] for which, start, rows in views]
    fetches = [
        pltpu.make_async_copy(factor, ref, factor_sem.at[i])
        for i, (factor, ref) in enumerate(zip(factors, (high_ref, low_ref, inv_high_ref, inv_low_ref)))
    ]
    for fetch in fetches:
        fetch.start()
    waits = place_pieces(place_ref, 2, views, held, sem)
    row_index, col_index = place_ref[0], place_ref[1]
    width, band = cols_ref.shape[0], rows_ref.shape[0] // (SPAN - 1)
    row_count = (SPAN - 1) * band
    panel_blocks = PANEL // width
    in_panel = col_index < panel_blocks
    slot = jnp.minimum(col_index, panel_blocks - 1)
    at = pl.ds(pl.multiple_of(slot * width, width), width)
    below, right = pl.ds(0, row_count), pl.ds(row_count, width)

    def solve(with_cols):
        for wait in waits:
            wait()
        step = min(WIDE, width)
        groups = [(rows_ref, at_row, pl.ds(at_row, band), band) for at_row in range(0, row_count, band)]
        if with_cols:
            groups = [
                (cols_ref, at_row, pl.ds(row_count + at_row, step), step) for at_row in range(0, width, step)
            ] + groups

        def grams(start):
            block = panel_ref[pl.ds(start, WIDE), :]
            return [dot_nt(ref[pl.ds(at_row, count), :], block) for ref, at_row, _, count in groups]

        columns = grams(0)
        for fetch in fetches:
            fetch.wait()

        for start in range(0, PANEL, WIDE):
            first, second = pl.ds(start, BLOCK), pl.ds(start + BLOCK, BLOCK)
            between = dot_nn3((high_ref[second, first], low_ref[second, first]), (inv_high_ref[first, :], inv_low_ref[first, :]))
            corner = split(-dot_nn3((inv_high_ref[second, :], inv_low_ref[second, :]), split(between)))
            for wide_ref, inv_ref, part in ((wide_high_ref, inv_high_ref, corner[0]), (wide_low_ref, inv_low_ref, corner[1])):
                wide_ref[first, pl.ds(0, BLOCK)] = inv_ref[first, :]
                wide_ref[first, pl.ds(BLOCK, BLOCK)] = jnp.zeros((BLOCK, BLOCK), bf16)
                wide_ref[second, pl.ds(0, BLOCK)] = part
                wide_ref[second, pl.ds(BLOCK, BLOCK)] = inv_ref[second, :]

        for start in range(0, PANEL, WIDE):
            here = pl.ds(start, WIDE)
            if start > 0:
                columns = [
                    column
                    - dot_nt3(
                        (left_high_ref[mine, :start], left_low_ref[mine, :start]), (high_ref[here, :start], low_ref[here, :start])
                    )
                    for column, (_, _, mine, _) in zip(grams(start), groups)
                ]
            for column, (_, _, mine, _) in zip(columns, groups):
                column = dot_nt3(split(column), (wide_high_ref[here, :], wide_low_ref[here, :]))
                left_high_ref[mine, here], left_low_ref[mine, here] = split(column)

    @pl.when(in_panel)
    def _():
        solve(False)
        mine = pl.ds(pl.multiple_of(row_index * band, band), band)
        out_ref[pl.ds(0, band), :] = high_ref[mine, at].astype(f32) + low_ref[mine, at].astype(f32)
        out_ref[pl.ds(band, row_count), :] = left_high_ref[below, at].astype(f32) + left_low_ref[below, at].astype(f32)

    @pl.when(jnp.logical_not(in_panel))
    def _():
        solve(True)
        out_ref[pl.ds(0, band), :] = jnp.zeros((band, width), f32)
        items = lax.broadcasted_iota(jnp.int32, (band, width), 0) + row_index * band
        columns = lax.broadcasted_iota(jnp.int32, (band, width), 1) + col_index * width
        for part in range(SPAN - 1):
            mine = pl.ds(part * band, band)
            tile = dot_nt(rows_ref[mine, :], cols_ref[...])
            tile = tile + jnp.where(items + (part + 1) * PANEL == columns, regular_ref[...], 0.0)
            out_ref[pl.ds((part + 1) * band, band), :] = tile - dot_nt3(
                (left_high_ref[mine, :], left_low_ref[mine, :]), (left_high_ref[right, :], left_low_ref[right, :])
            )


def finish_tile(place, regular, factors, panel, rows, cols, counts, views, band, users):
    spec = pl.BlockSpec(memory_space=VMEM)
    width = regular.shape[1]
    factors = [pltpu.with_memory_space_constraint(x, pltpu.HBM) for x in factors]
    pieces = panel + rows + cols
    out = ((SPAN * band, width), f32)
    below = (SPAN - 1) * band + width
    held = [
        ((below, PANEL), bf16),
        ((below, PANEL), bf16),
        ((PANEL, WIDE), bf16),
        ((PANEL, WIDE), bf16),
        ((PANEL, users), bf16),
        (((SPAN - 1) * band, users), bf16),
        ((width, users), bf16),
    ]
    return pl.pallas_call(
        functools.partial(tile_kernel, len(pieces), counts, views),
        out_shape=jax.ShapeDtypeStruct(*out),
        in_specs=[pl.BlockSpec(memory_space=pltpu.SMEM)]
        + [spec]
        + [pl.BlockSpec(memory_space=pltpu.HBM)] * len(factors)
        + [pl.BlockSpec(memory_space=pl.ANY)] * len(pieces),
        out_specs=spec,
        scratch_shapes=[VMEM(factor.shape, factor.dtype) for factor in factors]
        + [VMEM(*one) for one in held]
        + [pltpu.SemaphoreType.DMA((len(views),)), pltpu.SemaphoreType.DMA((len(factors),))],
        compiler_params=pltpu.CompilerParams(vmem_limit_bytes=room(out, *held, *((factor.shape, factor.dtype) for factor in factors))),
        cost_estimate=pl.CostEstimate(flops=20 * 10**9, bytes_accessed=24 * 2**20, transcendentals=0),
        name="finish_tile",
    )(place, regular, *factors, *pieces)


CORES = 2


def body(interactions, regular):
    row_count, col_count = lax.axis_size("row"), lax.axis_size("col")
    row_index, col_index = lax.axis_index("row"), lax.axis_index("col")
    width, users = interactions.shape
    band = PANEL // row_count
    ways = PANEL // width
    assert row_count == CORES * ways and col_count == SPAN * ways and users >= width
    slot, way = col_index // ways, col_index % ways
    pair, core = row_index // CORES, row_index % CORES
    all_users = row_count * users

    def exchange(value, move, only=None):
        perm = []
        for source_row in range(row_count):
            for source_col in range(col_count):
                place = (source_row // CORES, source_row % CORES, source_col // ways, source_col % ways)
                if only is None or only(*place):
                    to = move(*place)
                    target = (to[0] * CORES + to[1]) * col_count + to[2] * ways + to[3]
                    perm.append((source_row * col_count + source_col, target))
        return lax.ppermute(value, ("row", "col"), perm)

    def after(value, *others):
        return lax.optimization_barrier((value, *others))[0]

    high = lax.reduce_precision(regular, 8, 7)
    middle = lax.reduce_precision(regular - high, 8, 7)
    parts = jnp.stack([high, middle, regular - high - middle]).astype(bf16)
    parts = jnp.pad(parts, ((0, PARTS - 3), (0, users - width)))

    def over_core(value, only=None):
        return exchange(value, lambda p, h, s, w: (p, 1 - h, s, w), only)

    def over_pair(value):
        return exchange(value, lambda p, h, s, w: (1 - p, h, s, w))

    def over_way(value):
        return exchange(value, lambda p, h, s, w: (p, h, s, 1 - w))

    def traded(items, only):
        halves = items.reshape(CORES, band, users)
        kept, given = (lax.dynamic_index_in_dim(halves, core ^ flip, 0, False) for flip in range(CORES))
        return jnp.concatenate([kept, over_core(given, only)], 0)

    halves = interactions.reshape(CORES, band, users)
    offers = [lax.dynamic_index_in_dim(halves, core ^ flip, 0, False) for flip in range(CORES)]
    if ways == 2:
        raised = exchange(interactions, lambda p, h, s, w: (p, h, 0, w), lambda p, h, s, w: s == SPAN - 1)

    half = width // 2
    shared = jnp.concatenate([interactions, parts], 0)
    quarters, quarter_users = [], []
    reach = SPAN // 2
    while reach:
        got = exchange(
            shared, lambda p, h, s, w: (p, h, s + reach, w), lambda p, h, s, w: s % (2 * reach) == 0
        )
        if reach == SPAN // 2:
            for turn in range(ways):
                for flip in range(CORES):
                    quarters.append(
                        exchange(
                            offers[flip],
                            lambda p, h, s, w: (w, h ^ flip, s, (p + turn) % ways),
                            lambda p, h, s, w: s > 0,
                        )
                    )
                    quarter_users.append(((way - turn) % ways * CORES + (core ^ flip)) * users)
            if ways == 2:
                got = after(got, raised)
        shared = jnp.where(slot % (2 * reach) == reach, got, shared)
        reach //= 2
    quarters = jnp.concatenate(quarters, 0)

    def numbers(values):
        return jnp.stack([jnp.asarray(v, jnp.int32) for v in values])

    panel, panel_views, panel_place, part_views, part_place = [], [], [], [], []
    cols, cols_place = [interactions], [0, row_index * users]
    rows, rows_views, rows_place = [], [], []

    if ways == 2:
        mixed = jnp.where(slot == 0, traded(raised, lambda p, h, s, w: s == 0), interactions)
        shared = after(shared, quarters, mixed)
        pair_side, way_side = over_pair(shared), over_way(shared)
        own_twin, way_twin = over_core(shared), over_core(way_side)
        diagonal = [over_way(after(pair_side, own_twin, way_twin)[:half]), over_pair(after(way_side, own_twin)[half:])]
        for from_pair, from_way, first_row, piece in (
            (pair, way, 0, shared),
            (1 - pair, way, 0, pair_side),
            (pair, 1 - way, 0, way_side),
            (1 - pair, 1 - way, 0, diagonal[0]),
            (1 - pair, 1 - way, half, diagonal[1]),
        ):
            twin = own_twin if piece is shared else way_twin if piece is way_side else over_core(piece)
            for from_core, value in ((core, piece), (1 - core, twin)):
                if value is shared or value is way_side:
                    part_views.append((len(panel), width, PARTS, True))
                    part_place += [from_way * PARTS, 0]
                count = min(value.shape[0], half if value.shape[0] < width else width)
                panel_views.append((len(panel), 0, count, False))
                panel_place += [from_way * width + first_row, (from_pair * CORES + from_core) * users]
                panel.append(value)
        crossed = [pair_side, way_side, *diagonal]
        down = exchange(quarters, lambda p, h, s, w: (p, h, s - 1, w), lambda p, h, s, w: s > 0)
        up = exchange(quarters, lambda p, h, s, w: (p, h, s + 1, w), lambda p, h, s, w: 0 < s < SPAN - 1)
        down_held, up_held, mixed = lax.optimization_barrier(
            (down, up, mixed, *crossed)
        )[:3]
        down_again = exchange(down_held, lambda p, h, s, w: (p, h, s - 1, w), lambda p, h, s, w: 0 < s < SPAN - 1)
        up_again = exchange(up_held, lambda p, h, s, w: (p, h, s + 1, w), lambda p, h, s, w: s == 2)
        rows = [quarters, down, down_again, up, up_again]
        from_slots = [
            slot,
            jnp.where(slot < 3, slot + 1, 0),
            jnp.where(slot < 2, slot + 2, 0),
            jnp.where(slot > 1, slot - 1, 0),
            jnp.where(slot == 3, 1, 0),
        ]
        cols += [over_core(after(interactions, *crossed))]
        cols_place += [0, (row_index ^ 1) * users]
        for turn in range(ways):
            mix = exchange(
                mixed, lambda p, h, s, w: (w, h, s, (p + turn) % ways) if s == 0 else (1 - p, h ^ turn, s, w)
            )
            cols.append(mix)
            cols_place += [jnp.where(slot == 0, -1, 0), (row_index ^ (CORES + turn)) * users]
        for from_slot, piece in enumerate(rows):
            for which, from_users in enumerate(quarter_users):
                rows_views.append((from_slot, which * band, band))
                rows_place += [(from_slots[from_slot] - 1) * band, from_users]
        for which, from_users in enumerate(quarter_users):
            rows_views.append((len(rows) + 2 + which // CORES, which % CORES * band, band))
            rows_place += [jnp.where(slot == 0, (SPAN - 2) * band, -1), from_users]
    else:
        groups = [[s * ways + w for w in range(ways)] for s in range(SPAN)]
        shared = lax.all_gather(shared, "col", axis=0, axis_index_groups=groups)
        parts = shared[:, width:].reshape(ways * PARTS, users)
        shared = shared[:, :width].reshape(PANEL, users)
        panel, panel_place = [lax.all_gather(shared, "row", axis=1, tiled=True), parts], [0, 0]
        panel_views = [(0, 0, PANEL, False)]
        part_views, part_place = [(1, 0, ways * PARTS, True)], [0, 0]
        cols, cols_place = [lax.all_gather(interactions, "row", axis=1, tiled=True)], [0, 0]
        groups = [[s * ways + w for s in range(SPAN)] for w in range(ways)]
        rows = [lax.all_gather(quarters, "col", axis=0, tiled=True, axis_index_groups=groups)]
        for from_slot in range(1, SPAN):
            for which, from_users in enumerate(quarter_users):
                rows_views.append((0, (from_slot * len(quarter_users) + which) * band, band))
                rows_place += [(from_slot - 1) * band, from_users]

    factors = factor_panel(
        numbers(panel_place + part_place), panel, panel_views + part_views, width, all_users
    )
    views = [view[:3] for view in panel_views]
    views += [(len(panel) + i, start, count) for i, start, count in rows_views]
    views += [(len(panel) + len(rows) + i, 0, width) for i in range(len(cols))]
    counts = len(panel_views), len(rows_views), len(cols)
    tile = finish_tile(
        numbers([row_index, col_index] + panel_place + rows_place + cols_place),
        regular[None, :], factors, panel, rows, cols, counts, views, band, all_users,
    )
    return tile.reshape(SPAN, band, width)


def solution(mesh):
    return jax.shard_map(
        body,
        mesh=mesh,
        in_specs=(P("col", "row"), P("col")),
        out_specs=P(None, "row", "col"),
        check_vma=False,
    )
```

```python
import functools
import math
import jax
import jax.numpy as jnp
from jax import lax
from jax.experimental import pallas as pl
from jax.experimental.pallas import tpu as pltpu
from jax.sharding import PartitionSpec as P

PANEL = 1024
SPAN = 4
BLOCK = 128
WIDE = 256
SUB = 8
NBLOCKS = PANEL // BLOCK
PARTS = 16
VMEM = pltpu.VMEM
f32 = jnp.float32
bf16 = jnp.bfloat16


def dot_nt(a, b):
    return lax.dot_general(a, b, (((1,), (1,)), ((), ())), preferred_element_type=f32)


def split(value):
    high = value.astype(bf16)
    return high, (value - high.astype(f32)).astype(bf16)


def dot_nt3(a, b):
    return dot_nt(a[0], b[0]) + (dot_nt(a[0], b[1]) + dot_nt(a[1], b[0]))


def dot_nn3(a, b):
    def dot(x, y):
        return jnp.dot(x, y, preferred_element_type=f32)

    return dot(a[0], b[0]) + (dot(a[0], b[1]) + dot(a[1], b[0]))


def lanes(value, lane):
    return jnp.broadcast_to(value[:, lane : lane + 1], (SUB, BLOCK))


def sublanes(value, row):
    return jnp.broadcast_to(value[row : row + 1, :], (SUB, BLOCK))


def factor_block(block_ref, inverse_ref):
    tiles_count = BLOCK // SUB
    row_in_tile = lax.broadcasted_iota(jnp.int32, (SUB, BLOCK), 0)
    lane = lax.broadcasted_iota(jnp.int32, (SUB, BLOCK), 1)
    sides = [block_ref[pl.ds(SUB * t, SUB), :] for t in range(tiles_count)]
    inverses = [(lane == row_in_tile + SUB * t).astype(f32) for t in range(tiles_count)]
    uppers = []
    for step in range(tiles_count):
        base = SUB * step
        side, inverse = sides[step], inverses[step]
        if step == 0:
            columns = [lanes(side, base + b) for b in range(SUB)]
        entry = {(a, b): sublanes(columns[b], a) for b in range(SUB) for a in range(b, SUB)}
        vectors = [[sublanes(side, a) for a in range(SUB)], [sublanes(inverse, a) for a in range(SUB)]]
        if step + 1 < tiles_count:
            vectors.append([lanes(sides[step + 1], base + b) for b in range(SUB)])
            columns = [lanes(sides[step + 1], base + SUB + b) for b in range(SUB)]
        scale = [None] * SUB
        for m in range(0, SUB, 2):
            n = m + 1
            first, cross, second = entry[m, m], entry[n, m], entry[n, n]
            root = lax.rsqrt(first)
            det_root = lax.rsqrt(first * second - cross * cross)
            scale[m], scale[n] = root, det_root * (first * root)
            det_square = det_root * det_root
            link = cross * root
            entry[n, m] = link
            rest = range(n + 1, SUB)
            for x in rest:
                entry[x, m] = entry[x, m] * root
                entry[x, n] = entry[x, n] - entry[x, m] * link
            weighted = {x: entry[x, n] * first for x in rest}
            for y in rest:
                for x in range(y, SUB):
                    entry[x, y] = (entry[x, y] - entry[x, m] * entry[y, m]) - (weighted[x] * entry[y, n]) * det_square
            for x in rest:
                entry[x, n] = entry[x, n] * scale[n]
            for vector in vectors:
                vector[m] = vector[m] * root
                vector[n] = (vector[n] - link * vector[m]) * scale[n]
                for x in rest:
                    vector[x] = (vector[x] - entry[x, m] * vector[m]) - entry[x, n] * vector[n]
            if step + 1 < tiles_count:
                left, right = vectors[2][m], vectors[2][n]
                columns = [
                    (column - left * sublanes(left, b)) - right * sublanes(right, b)
                    for b, column in enumerate(columns)
                ]
        tops, insides = vectors[:2]
        upper, lower_inverse = tops[0], insides[0]
        for m in range(1, SUB):
            upper = jnp.where(row_in_tile == m, tops[m], upper)
            lower_inverse = jnp.where(row_in_tile == m, insides[m], lower_inverse)
        uppers.append(jnp.where(lane >= row_in_tile + base, upper, 0.0))
        inverse_ref[pl.ds(base, SUB), :] = lower_inverse
        if step + 1 < tiles_count:
            ahead = vectors[2]
            for m in range(SUB):
                sides[step + 1] = sides[step + 1] - ahead[m] * tops[m]
                inverses[step + 1] = inverses[step + 1] - ahead[m] * insides[m]
        if step + 2 < tiles_count:
            weights_top, weights_in = [None] * SUB, [None] * SUB
            for m in reversed(range(SUB)):
                top, inside = tops[m], insides[m]
                for b in range(m + 1, SUB):
                    top = top - entry[b, m] * weights_top[b]
                    inside = inside - entry[b, m] * weights_in[b]
                weights_top[m], weights_in[m] = top * scale[m], inside * scale[m]
            for t in range(step + 2, tiles_count):
                for m in range(SUB):
                    column = lanes(sides[t], base + m)
                    if m == 0:
                        top_sum, in_sum = column * weights_top[m], column * weights_in[m]
                    else:
                        top_sum = top_sum + column * weights_top[m]
                        in_sum = in_sum + column * weights_in[m]
                sides[t] = sides[t] - top_sum
                inverses[t] = inverses[t] - in_sum
    block_ref[...] = jnp.concatenate(uppers, 0).T


def place_pieces(place_ref, first, pieces, helds, sem):
    waits = []
    for i, (piece, held_ref) in enumerate(zip(pieces, helds)):
        rows, users = piece.shape
        row = place_ref[first + 2 * i]
        user = pl.multiple_of(place_ref[first + 2 * i + 1], users)
        to = held_ref.at[pl.ds(pl.multiple_of(jnp.maximum(row, 0), rows), rows), pl.ds(user, users)]
        copy = pltpu.make_async_copy(piece, to, sem.at[i])
        pl.when(row >= 0)(copy.start)
        waits.append(functools.partial(pl.when(row >= 0), copy.wait))
    return waits


def panel_kernel(views, count, width, place_ref, *refs):
    pieces, refs = refs[:count], refs[count:]
    outs, (high_ref, low_ref, inv_high_ref, inv_low_ref, lower_ref, coming_ref, *refs) = refs[:4], refs[4:]
    block_ref, inverse_ref, items_ref, parts_ref, sem, out_sem = refs
    held = [parts_ref if is_part else items_ref for _, _, _, is_part in views]
    views = [pieces[which].at[pl.ds(start, rows)] for which, start, rows, _ in views]
    waits = place_pieces(place_ref, 0, views, held, sem)
    for k in range(1, NBLOCKS):
        for ref in (high_ref, low_ref):
            ref[pl.ds(0, k * BLOCK), pl.ds(k * BLOCK, BLOCK)] = jnp.zeros((k * BLOCK, BLOCK), bf16)
    for wait in waits:
        wait()
    on_diagonal = lax.broadcasted_iota(jnp.int32, (BLOCK, BLOCK), 0) == lax.broadcasted_iota(
        jnp.int32, (BLOCK, BLOCK), 1
    )

    def before(k):
        start = k * BLOCK
        here, rest = pl.ds(start, BLOCK), pl.ds(start, PANEL - start)
        if k % 2 == 0:
            both = pl.ds(start, 2 * BLOCK)
            columns = dot_nt(items_ref[rest, :], items_ref[both, :])
            if k > 0:
                columns = columns - dot_nt3(
                    (high_ref[rest, :start], low_ref[rest, :start]), (high_ref[both, :start], low_ref[both, :start])
                )
            column = columns[:, :BLOCK]
            coming_ref[pl.ds(start + BLOCK, PANEL - start - BLOCK), :] = columns[BLOCK:, BLOCK:]
        else:
            last = pl.ds(start - BLOCK, BLOCK)
            high, low = high_ref[rest, last], low_ref[rest, last]
            column = coming_ref[rest, :] - dot_nt3((high, low), (high[:BLOCK], low[:BLOCK]))
        part, lane = PARTS * (start // width), start % width
        parts = parts_ref[pl.ds(part, PARTS), pl.ds(lane, BLOCK)].astype(f32)
        block_ref[...] = column[:BLOCK] + jnp.where(on_diagonal, parts[0:1] + parts[1:2] + parts[2:3], 0.0)
        if k + 1 < NBLOCKS:
            lower_ref[pl.ds(start + BLOCK, PANEL - start - BLOCK), :] = column[BLOCK:]

    def after(k):
        start = k * BLOCK
        here = pl.ds(start, BLOCK)
        inverse = split(inverse_ref[...])
        inv_high_ref[here, :], inv_low_ref[here, :] = inverse
        high_ref[here, here], low_ref[here, here] = split(block_ref[...])
        if k + 1 < NBLOCKS:
            rest = pl.ds(start + BLOCK, PANEL - start - BLOCK)
            high_ref[rest, here], low_ref[rest, here] = split(dot_nt3(split(lower_ref[rest, :]), inverse))

    def leave(k):
        column = pl.ds(k * BLOCK, BLOCK)
        return [
            pltpu.make_async_copy(high_ref.at[:, column], outs[0].at[:, column], out_sem.at[0, k]),
            pltpu.make_async_copy(low_ref.at[:, column], outs[1].at[:, column], out_sem.at[1, k]),
            pltpu.make_async_copy(inv_high_ref.at[column, :], outs[2].at[column, :], out_sem.at[2, k]),
            pltpu.make_async_copy(inv_low_ref.at[column, :], outs[3].at[column, :], out_sem.at[3, k]),
        ]

    before(0)

    def turn(k, carry):
        factor_block(block_ref, inverse_ref)
        for which in range(NBLOCKS):

            @pl.when(k == which)
            def _():
                after(which)
                for copy in leave(which):
                    copy.start()
                if which + 1 < NBLOCKS:
                    before(which + 1)

        return carry

    lax.fori_loop(0, NBLOCKS, turn, 0)
    for k in range(NBLOCKS):
        for copy in leave(k):
            copy.wait()


def room(*arrays):
    return sum(math.prod(shape) * jnp.dtype(dtype).itemsize for shape, dtype in arrays) + 8 * 2**20


def factor_panel(place, pieces, views, width, users):
    outs = [
        ((PANEL, PANEL), bf16),
        ((PANEL, PANEL), bf16),
        ((PANEL, BLOCK), bf16),
        ((PANEL, BLOCK), bf16),
    ]
    held = [
        ((PANEL, BLOCK), f32),
        ((PANEL, BLOCK), f32),
        ((BLOCK, BLOCK), f32),
        ((BLOCK, BLOCK), f32),
        ((PANEL, users), bf16),
        ((PANEL // width * PARTS, users), bf16),
    ]
    return pl.pallas_call(
        functools.partial(panel_kernel, views, len(pieces), width),
        out_shape=[pltpu.HBM(*out) for out in outs],
        in_specs=[pl.BlockSpec(memory_space=pltpu.SMEM)]
        + [pl.BlockSpec(memory_space=pl.ANY)] * len(pieces),
        out_specs=[pl.BlockSpec(memory_space=pltpu.HBM)] * len(outs),
        scratch_shapes=[VMEM(*one) for one in outs + held]
        + [pltpu.SemaphoreType.DMA((len(views),)), pltpu.SemaphoreType.DMA((len(outs), NBLOCKS))],
        compiler_params=pltpu.CompilerParams(vmem_limit_bytes=room(*outs, *held)),
        cost_estimate=pl.CostEstimate(flops=8 * 10**9, bytes_accessed=2**20, transcendentals=1024),
        name="factor_panel",
    )(place, *pieces)


def tile_kernel(total, counts, views, place_ref, regular_ref, *refs):
    factors, refs = refs[:4], refs[4:]
    pieces, refs = refs[:total], refs[total:]
    out_ref, refs = refs[0], refs[1:]
    high_ref, low_ref, inv_high_ref, inv_low_ref, left_high_ref, left_low_ref, wide_high_ref, wide_low_ref = refs[:8]
    panel_ref, rows_ref, cols_ref, sem, factor_sem = refs[8:]
    held = [ref for ref, count in zip((panel_ref, rows_ref, cols_ref), counts) for _ in range(count)]
    views = [pieces[which].at[pl.ds(start, rows)] for which, start, rows in views]
    fetches = [
        pltpu.make_async_copy(factor, ref, factor_sem.at[i])
        for i, (factor, ref) in enumerate(zip(factors, (high_ref, low_ref, inv_high_ref, inv_low_ref)))
    ]
    for fetch in fetches:
        fetch.start()
    waits = place_pieces(place_ref, 2, views, held, sem)
    row_index, col_index = place_ref[0], place_ref[1]
    width, band = cols_ref.shape[0], rows_ref.shape[0] // (SPAN - 1)
    row_count = (SPAN - 1) * band
    panel_blocks = PANEL // width
    in_panel = col_index < panel_blocks
    slot = jnp.minimum(col_index, panel_blocks - 1)
    at = pl.ds(pl.multiple_of(slot * width, width), width)
    below, right = pl.ds(0, row_count), pl.ds(row_count, width)

    def solve(with_cols):
        for wait in waits:
            wait()
        step = min(WIDE, width)
        groups = [(rows_ref, at_row, pl.ds(at_row, band), band) for at_row in range(0, row_count, band)]
        if with_cols:
            groups = [
                (cols_ref, at_row, pl.ds(row_count + at_row, step), step) for at_row in range(0, width, step)
            ] + groups

        def grams(start):
            block = panel_ref[pl.ds(start, WIDE), :]
            return [dot_nt(ref[pl.ds(at_row, count), :], block) for ref, at_row, _, count in groups]

        columns = grams(0)
        for fetch in fetches:
            fetch.wait()

        for start in range(0, PANEL, WIDE):
            first, second = pl.ds(start, BLOCK), pl.ds(start + BLOCK, BLOCK)
            between = dot_nn3((high_ref[second, first], low_ref[second, first]), (inv_high_ref[first, :], inv_low_ref[first, :]))
            corner = split(-dot_nn3((inv_high_ref[second, :], inv_low_ref[second, :]), split(between)))
            for wide_ref, inv_ref, part in ((wide_high_ref, inv_high_ref, corner[0]), (wide_low_ref, inv_low_ref, corner[1])):
                wide_ref[first, pl.ds(0, BLOCK)] = inv_ref[first, :]
                wide_ref[first, pl.ds(BLOCK, BLOCK)] = jnp.zeros((BLOCK, BLOCK), bf16)
                wide_ref[second, pl.ds(0, BLOCK)] = part
                wide_ref[second, pl.ds(BLOCK, BLOCK)] = inv_ref[second, :]

        for start in range(0, PANEL, WIDE):
            here = pl.ds(start, WIDE)
            if start > 0:
                columns = [
                    column
                    - dot_nt3(
                        (left_high_ref[mine, :start], left_low_ref[mine, :start]), (high_ref[here, :start], low_ref[here, :start])
                    )
                    for column, (_, _, mine, _) in zip(grams(start), groups)
                ]
            for column, (_, _, mine, _) in zip(columns, groups):
                column = dot_nt3(split(column), (wide_high_ref[here, :], wide_low_ref[here, :]))
                left_high_ref[mine, here], left_low_ref[mine, here] = split(column)

    @pl.when(in_panel)
    def _():
        solve(False)
        mine = pl.ds(pl.multiple_of(row_index * band, band), band)
        out_ref[pl.ds(0, band), :] = high_ref[mine, at].astype(f32) + low_ref[mine, at].astype(f32)
        out_ref[pl.ds(band, row_count), :] = left_high_ref[below, at].astype(f32) + left_low_ref[below, at].astype(f32)

    @pl.when(jnp.logical_not(in_panel))
    def _():
        solve(True)
        out_ref[pl.ds(0, band), :] = jnp.zeros((band, width), f32)
        items = lax.broadcasted_iota(jnp.int32, (band, width), 0) + row_index * band
        columns = lax.broadcasted_iota(jnp.int32, (band, width), 1) + col_index * width
        for part in range(SPAN - 1):
            mine = pl.ds(part * band, band)
            tile = dot_nt(rows_ref[mine, :], cols_ref[...])
            tile = tile + jnp.where(items + (part + 1) * PANEL == columns, regular_ref[...], 0.0)
            out_ref[pl.ds((part + 1) * band, band), :] = tile - dot_nt3(
                (left_high_ref[mine, :], left_low_ref[mine, :]), (left_high_ref[right, :], left_low_ref[right, :])
            )


def finish_tile(place, regular, factors, panel, rows, cols, counts, views, band, users):
    spec = pl.BlockSpec(memory_space=VMEM)
    width = regular.shape[1]
    factors = [pltpu.with_memory_space_constraint(x, pltpu.HBM) for x in factors]
    pieces = panel + rows + cols
    out = ((SPAN * band, width), f32)
    below = (SPAN - 1) * band + width
    held = [
        ((below, PANEL), bf16),
        ((below, PANEL), bf16),
        ((PANEL, WIDE), bf16),
        ((PANEL, WIDE), bf16),
        ((PANEL, users), bf16),
        (((SPAN - 1) * band, users), bf16),
        ((width, users), bf16),
    ]
    return pl.pallas_call(
        functools.partial(tile_kernel, len(pieces), counts, views),
        out_shape=jax.ShapeDtypeStruct(*out),
        in_specs=[pl.BlockSpec(memory_space=pltpu.SMEM)]
        + [spec]
        + [pl.BlockSpec(memory_space=pltpu.HBM)] * len(factors)
        + [pl.BlockSpec(memory_space=pl.ANY)] * len(pieces),
        out_specs=spec,
        scratch_shapes=[VMEM(factor.shape, factor.dtype) for factor in factors]
        + [VMEM(*one) for one in held]
        + [pltpu.SemaphoreType.DMA((len(views),)), pltpu.SemaphoreType.DMA((len(factors),))],
        compiler_params=pltpu.CompilerParams(vmem_limit_bytes=room(out, *held, *((factor.shape, factor.dtype) for factor in factors))),
        cost_estimate=pl.CostEstimate(flops=20 * 10**9, bytes_accessed=24 * 2**20, transcendentals=0),
        name="finish_tile",
    )(place, regular, *factors, *pieces)


CORES = 2


def body(interactions, regular):
    row_count, col_count = lax.axis_size("row"), lax.axis_size("col")
    row_index, col_index = lax.axis_index("row"), lax.axis_index("col")
    width, users = interactions.shape
    band = PANEL // row_count
    ways = PANEL // width
    assert row_count == CORES * ways and col_count == SPAN * ways and users >= width
    slot, way = col_index // ways, col_index % ways
    pair, core = row_index // CORES, row_index % CORES
    all_users = row_count * users

    def exchange(value, move, only=None):
        perm = []
        for source_row in range(row_count):
            for source_col in range(col_count):
                place = (source_row // CORES, source_row % CORES, source_col // ways, source_col % ways)
                if only is None or only(*place):
                    to = move(*place)
                    target = (to[0] * CORES + to[1]) * col_count + to[2] * ways + to[3]
                    perm.append((source_row * col_count + source_col, target))
        return lax.ppermute(value, ("row", "col"), perm)

    def after(value, *others):
        return lax.optimization_barrier((value, *others))[0]

    high = lax.reduce_precision(regular, 8, 7)
    middle = lax.reduce_precision(regular - high, 8, 7)
    parts = jnp.stack([high, middle, regular - high - middle]).astype(bf16)
    parts = jnp.pad(parts, ((0, PARTS - 3), (0, users - width)))

    def over_core(value, only=None):
        return exchange(value, lambda p, h, s, w: (p, 1 - h, s, w), only)

    def over_pair(value):
        return exchange(value, lambda p, h, s, w: (1 - p, h, s, w))

    def over_way(value):
        return exchange(value, lambda p, h, s, w: (p, h, s, 1 - w))

    def traded(items, only):
        halves = items.reshape(CORES, band, users)
        kept, given = (lax.dynamic_index_in_dim(halves, core ^ flip, 0, False) for flip in range(CORES))
        return jnp.concatenate([kept, over_core(given, only)], 0)

    halves = interactions.reshape(CORES, band, users)
    offers = [lax.dynamic_index_in_dim(halves, core ^ flip, 0, False) for flip in range(CORES)]
    if ways == 2:
        raised = exchange(interactions, lambda p, h, s, w: (p, h, 0, w), lambda p, h, s, w: s == SPAN - 1)

    half = width // 2
    shared = jnp.concatenate([interactions, parts], 0)
    quarters, quarter_users = [], []
    reach = SPAN // 2
    while reach:
        got = exchange(
            shared, lambda p, h, s, w: (p, h, s + reach, w), lambda p, h, s, w: s % (2 * reach) == 0
        )
        if reach == SPAN // 2:
            for turn in range(ways):
                for flip in range(CORES):
                    quarters.append(
                        exchange(
                            offers[flip],
                            lambda p, h, s, w: (w, h ^ flip, s, (p + turn) % ways),
                            lambda p, h, s, w: s > 0,
                        )
                    )
                    quarter_users.append(((way - turn) % ways * CORES + (core ^ flip)) * users)
            if ways == 2:
                got = after(got, raised)
        shared = jnp.where(slot % (2 * reach) == reach, got, shared)
        reach //= 2
    quarters = jnp.concatenate(quarters, 0)

    def numbers(values):
        return jnp.stack([jnp.asarray(v, jnp.int32) for v in values])

    panel, panel_views, panel_place, part_views, part_place = [], [], [], [], []
    cols, cols_place = [interactions], [0, row_index * users]
    rows, rows_views, rows_place = [], [], []

    if ways == 2:
        mixed = jnp.where(slot == 0, traded(raised, lambda p, h, s, w: s == 0), interactions)
        shared = after(shared, quarters, mixed)
        pair_side, way_side = over_pair(shared), over_way(shared)
        own_twin, way_twin = over_core(shared), over_core(way_side)
        diagonal = [over_way(after(pair_side, own_twin, way_twin)[:half]), over_pair(after(way_side, own_twin)[half:])]
        for from_pair, from_way, first_row, piece in (
            (pair, way, 0, shared),
            (1 - pair, way, 0, pair_side),
            (pair, 1 - way, 0, way_side),
            (1 - pair, 1 - way, 0, diagonal[0]),
            (1 - pair, 1 - way, half, diagonal[1]),
        ):
            twin = own_twin if piece is shared else way_twin if piece is way_side else over_core(piece)
            for from_core, value in ((core, piece), (1 - core, twin)):
                if value is shared or value is way_side:
                    part_views.append((len(panel), width, PARTS, True))
                    part_place += [from_way * PARTS, 0]
                count = min(value.shape[0], half if value.shape[0] < width else width)
                panel_views.append((len(panel), 0, count, False))
                panel_place += [from_way * width + first_row, (from_pair * CORES + from_core) * users]
                panel.append(value)
        crossed = [pair_side, way_side, *diagonal]
        down = exchange(quarters, lambda p, h, s, w: (p, h, s - 1, w), lambda p, h, s, w: s > 0)
        up = exchange(
            after(quarters, pair_side, way_side), lambda p, h, s, w: (p, h, s + 1, w), lambda p, h, s, w: 0 < s < SPAN - 1
        )
        own_core = over_core(after(interactions, pair_side, way_side))
        down_held, ready, mixed = lax.optimization_barrier((down, quarters, mixed, own_core, *crossed))[:3]
        down_again = exchange(down_held, lambda p, h, s, w: (p, h, s - 1, w), lambda p, h, s, w: 0 < s < SPAN - 1)
        up_again = exchange(ready, lambda p, h, s, w: (p, h, s + 2, w), lambda p, h, s, w: s == 1)
        rows = [quarters, down, down_again, up, up_again]
        from_slots = [
            slot,
            jnp.where(slot < 3, slot + 1, 0),
            jnp.where(slot < 2, slot + 2, 0),
            jnp.where(slot > 1, slot - 1, 0),
            jnp.where(slot == 3, 1, 0),
        ]
        cols += [own_core]
        cols_place += [0, (row_index ^ 1) * users]
        for turn in range(ways):
            mix = exchange(
                mixed, lambda p, h, s, w: (w, h, s, (p + turn) % ways) if s == 0 else (1 - p, h ^ turn, s, w)
            )
            cols.append(mix)
            cols_place += [jnp.where(slot == 0, -1, 0), (row_index ^ (CORES + turn)) * users]
        for from_slot, piece in enumerate(rows):
            for which, from_users in enumerate(quarter_users):
                rows_views.append((from_slot, which * band, band))
                rows_place += [(from_slots[from_slot] - 1) * band, from_users]
        for which, from_users in enumerate(quarter_users):
            rows_views.append((len(rows) + 2 + which // CORES, which % CORES * band, band))
            rows_place += [jnp.where(slot == 0, (SPAN - 2) * band, -1), from_users]
    else:
        groups = [[s * ways + w for w in range(ways)] for s in range(SPAN)]
        shared = lax.all_gather(shared, "col", axis=0, axis_index_groups=groups)
        parts = shared[:, width:].reshape(ways * PARTS, users)
        shared = shared[:, :width].reshape(PANEL, users)
        panel, panel_place = [lax.all_gather(shared, "row", axis=1, tiled=True), parts], [0, 0]
        panel_views = [(0, 0, PANEL, False)]
        part_views, part_place = [(1, 0, ways * PARTS, True)], [0, 0]
        cols, cols_place = [lax.all_gather(interactions, "row", axis=1, tiled=True)], [0, 0]
        groups = [[s * ways + w for s in range(SPAN)] for w in range(ways)]
        rows = [lax.all_gather(quarters, "col", axis=0, tiled=True, axis_index_groups=groups)]
        for from_slot in range(1, SPAN):
            for which, from_users in enumerate(quarter_users):
                rows_views.append((0, (from_slot * len(quarter_users) + which) * band, band))
                rows_place += [(from_slot - 1) * band, from_users]

    factors = factor_panel(
        numbers(panel_place + part_place), panel, panel_views + part_views, width, all_users
    )
    views = [view[:3] for view in panel_views]
    views += [(len(panel) + i, start, count) for i, start, count in rows_views]
    views += [(len(panel) + len(rows) + i, 0, width) for i in range(len(cols))]
    counts = len(panel_views), len(rows_views), len(cols)
    tile = finish_tile(
        numbers([row_index, col_index] + panel_place + rows_place + cols_place),
        regular[None, :], factors, panel, rows, cols, counts, views, band, all_users,
    )
    return tile.reshape(SPAN, band, width)


def solution(mesh):
    return jax.shard_map(
        body,
        mesh=mesh,
        in_specs=(P("col", "row"), P("col")),
        out_specs=P(None, "row", "col"),
        check_vma=False,
    )
```

```python
import functools
import math
import jax
import jax.numpy as jnp
from jax import lax
from jax.experimental import pallas as pl
from jax.experimental.pallas import tpu as pltpu
from jax.sharding import PartitionSpec as P

PANEL = 1024
SPAN = 4
BLOCK = 128
WIDE = 256
SUB = 8
NBLOCKS = PANEL // BLOCK
PARTS = 16
VMEM = pltpu.VMEM
f32 = jnp.float32
bf16 = jnp.bfloat16


def dot_nt(a, b):
    return lax.dot_general(a, b, (((1,), (1,)), ((), ())), preferred_element_type=f32)


def split(value):
    high = value.astype(bf16)
    return high, (value - high.astype(f32)).astype(bf16)


def dot_nt3(a, b):
    return dot_nt(a[0], b[0]) + (dot_nt(a[0], b[1]) + dot_nt(a[1], b[0]))


def dot_nn3(a, b):
    def dot(x, y):
        return jnp.dot(x, y, preferred_element_type=f32)

    return dot(a[0], b[0]) + (dot(a[0], b[1]) + dot(a[1], b[0]))


def lanes(value, lane):
    return jnp.broadcast_to(value[:, lane : lane + 1], (SUB, BLOCK))


def sublanes(value, row):
    return jnp.broadcast_to(value[row : row + 1, :], (SUB, BLOCK))


def factor_block(block_ref, inverse_ref):
    tiles_count = BLOCK // SUB
    row_in_tile = lax.broadcasted_iota(jnp.int32, (SUB, BLOCK), 0)
    lane = lax.broadcasted_iota(jnp.int32, (SUB, BLOCK), 1)
    sides = [block_ref[pl.ds(SUB * t, SUB), :] for t in range(tiles_count)]
    inverses = [(lane == row_in_tile + SUB * t).astype(f32) for t in range(tiles_count)]
    uppers = []
    for step in range(tiles_count):
        base = SUB * step
        side, inverse = sides[step], inverses[step]
        if step == 0:
            columns = [lanes(side, base + b) for b in range(SUB)]
        entry = {(a, b): sublanes(columns[b], a) for b in range(SUB) for a in range(b, SUB)}
        vectors = [[sublanes(side, a) for a in range(SUB)], [sublanes(inverse, a) for a in range(SUB)]]
        if step + 1 < tiles_count:
            vectors.append([lanes(sides[step + 1], base + b) for b in range(SUB)])
            columns = [lanes(sides[step + 1], base + SUB + b) for b in range(SUB)]
        scale = [None] * SUB
        for m in range(0, SUB, 2):
            n = m + 1
            first, cross, second = entry[m, m], entry[n, m], entry[n, n]
            root = lax.rsqrt(first)
            det_root = lax.rsqrt(first * second - cross * cross)
            scale[m], scale[n] = root, det_root * (first * root)
            det_square = det_root * det_root
            link = cross * root
            entry[n, m] = link
            rest = range(n + 1, SUB)
            for x in rest:
                entry[x, m] = entry[x, m] * root
                entry[x, n] = entry[x, n] - entry[x, m] * link
            weighted = {x: entry[x, n] * first for x in rest}
            for y in rest:
                for x in range(y, SUB):
                    entry[x, y] = (entry[x, y] - entry[x, m] * entry[y, m]) - (weighted[x] * entry[y, n]) * det_square
            for x in rest:
                entry[x, n] = entry[x, n] * scale[n]
            for vector in vectors:
                vector[m] = vector[m] * root
                vector[n] = (vector[n] - link * vector[m]) * scale[n]
                for x in rest:
                    vector[x] = (vector[x] - entry[x, m] * vector[m]) - entry[x, n] * vector[n]
            if step + 1 < tiles_count:
                left, right = vectors[2][m], vectors[2][n]
                columns = [
                    (column - left * sublanes(left, b)) - right * sublanes(right, b)
                    for b, column in enumerate(columns)
                ]
        tops, insides = vectors[:2]
        upper, lower_inverse = tops[0], insides[0]
        for m in range(1, SUB):
            upper = jnp.where(row_in_tile == m, tops[m], upper)
            lower_inverse = jnp.where(row_in_tile == m, insides[m], lower_inverse)
        uppers.append(jnp.where(lane >= row_in_tile + base, upper, 0.0))
        inverse_ref[pl.ds(base, SUB), :] = lower_inverse
        if step + 1 < tiles_count:
            ahead = vectors[2]
            for m in range(SUB):
                sides[step + 1] = sides[step + 1] - ahead[m] * tops[m]
                inverses[step + 1] = inverses[step + 1] - ahead[m] * insides[m]
        if step + 2 < tiles_count:
            weights_top, weights_in = [None] * SUB, [None] * SUB
            for m in reversed(range(SUB)):
                top, inside = tops[m], insides[m]
                for b in range(m + 1, SUB):
                    top = top - entry[b, m] * weights_top[b]
                    inside = inside - entry[b, m] * weights_in[b]
                weights_top[m], weights_in[m] = top * scale[m], inside * scale[m]
            for t in range(step + 2, tiles_count):
                for m in range(SUB):
                    column = lanes(sides[t], base + m)
                    if m == 0:
                        top_sum, in_sum = column * weights_top[m], column * weights_in[m]
                    else:
                        top_sum = top_sum + column * weights_top[m]
                        in_sum = in_sum + column * weights_in[m]
                sides[t] = sides[t] - top_sum
                inverses[t] = inverses[t] - in_sum
    block_ref[...] = jnp.concatenate(uppers, 0).T


def place_pieces(place_ref, first, pieces, helds, sem):
    waits = []
    for i, (piece, held_ref) in enumerate(zip(pieces, helds)):
        rows, users = piece.shape
        row = place_ref[first + 2 * i]
        user = pl.multiple_of(place_ref[first + 2 * i + 1], users)
        to = held_ref.at[pl.ds(pl.multiple_of(jnp.maximum(row, 0), rows), rows), pl.ds(user, users)]
        copy = pltpu.make_async_copy(piece, to, sem.at[i])
        pl.when(row >= 0)(copy.start)
        waits.append(functools.partial(pl.when(row >= 0), copy.wait))
    return waits


def panel_kernel(views, count, width, place_ref, *refs):
    pieces, refs = refs[:count], refs[count:]
    outs, (high_ref, low_ref, inv_high_ref, inv_low_ref, lower_ref, coming_ref, *refs) = refs[:4], refs[4:]
    block_ref, inverse_ref, items_ref, parts_ref, sem, out_sem = refs
    held = [parts_ref if is_part else items_ref for _, _, _, is_part in views]
    views = [pieces[which].at[pl.ds(start, rows)] for which, start, rows, _ in views]
    waits = place_pieces(place_ref, 0, views, held, sem)
    for k in range(1, NBLOCKS):
        for ref in (high_ref, low_ref):
            ref[pl.ds(0, k * BLOCK), pl.ds(k * BLOCK, BLOCK)] = jnp.zeros((k * BLOCK, BLOCK), bf16)
    for wait in waits:
        wait()
    on_diagonal = lax.broadcasted_iota(jnp.int32, (BLOCK, BLOCK), 0) == lax.broadcasted_iota(
        jnp.int32, (BLOCK, BLOCK), 1
    )

    def before(k):
        start = k * BLOCK
        here, rest = pl.ds(start, BLOCK), pl.ds(start, PANEL - start)
        if k % 2 == 0:
            both = pl.ds(start, 2 * BLOCK)
            columns = dot_nt(items_ref[rest, :], items_ref[both, :])
            if k > 0:
                columns = columns - dot_nt3(
                    (high_ref[rest, :start], low_ref[rest, :start]), (high_ref[both, :start], low_ref[both, :start])
                )
            column = columns[:, :BLOCK]
            coming_ref[pl.ds(start + BLOCK, PANEL - start - BLOCK), :] = columns[BLOCK:, BLOCK:]
        else:
            last = pl.ds(start - BLOCK, BLOCK)
            high, low = high_ref[rest, last], low_ref[rest, last]
            column = coming_ref[rest, :] - dot_nt3((high, low), (high[:BLOCK], low[:BLOCK]))
        part, lane = PARTS * (start // width), start % width
        parts = parts_ref[pl.ds(part, PARTS), pl.ds(lane, BLOCK)].astype(f32)
        block_ref[...] = column[:BLOCK] + jnp.where(on_diagonal, parts[0:1] + parts[1:2] + parts[2:3], 0.0)
        if k + 1 < NBLOCKS:
            lower_ref[pl.ds(start + BLOCK, PANEL - start - BLOCK), :] = column[BLOCK:]

    def after(k):
        start = k * BLOCK
        here = pl.ds(start, BLOCK)
        inverse = split(inverse_ref[...])
        inv_high_ref[here, :], inv_low_ref[here, :] = inverse
        high_ref[here, here], low_ref[here, here] = split(block_ref[...])
        if k + 1 < NBLOCKS:
            rest = pl.ds(start + BLOCK, PANEL - start - BLOCK)
            high_ref[rest, here], low_ref[rest, here] = split(dot_nt3(split(lower_ref[rest, :]), inverse))

    def leave(k):
        column = pl.ds(k * BLOCK, BLOCK)
        return [
            pltpu.make_async_copy(high_ref.at[:, column], outs[0].at[:, column], out_sem.at[0, k]),
            pltpu.make_async_copy(low_ref.at[:, column], outs[1].at[:, column], out_sem.at[1, k]),
            pltpu.make_async_copy(inv_high_ref.at[column, :], outs[2].at[column, :], out_sem.at[2, k]),
            pltpu.make_async_copy(inv_low_ref.at[column, :], outs[3].at[column, :], out_sem.at[3, k]),
        ]

    before(0)

    def turn(k, carry):
        factor_block(block_ref, inverse_ref)
        for which in range(NBLOCKS):

            @pl.when(k == which)
            def _():
                after(which)
                for copy in leave(which):
                    copy.start()
                if which + 1 < NBLOCKS:
                    before(which + 1)

        return carry

    lax.fori_loop(0, NBLOCKS, turn, 0)
    for k in range(NBLOCKS):
        for copy in leave(k):
            copy.wait()


def room(*arrays):
    return sum(math.prod(shape) * jnp.dtype(dtype).itemsize for shape, dtype in arrays) + 8 * 2**20


def factor_panel(place, pieces, views, width, users):
    outs = [
        ((PANEL, PANEL), bf16),
        ((PANEL, PANEL), bf16),
        ((PANEL, BLOCK), bf16),
        ((PANEL, BLOCK), bf16),
    ]
    held = [
        ((PANEL, BLOCK), f32),
        ((PANEL, BLOCK), f32),
        ((BLOCK, BLOCK), f32),
        ((BLOCK, BLOCK), f32),
        ((PANEL, users), bf16),
        ((PANEL // width * PARTS, users), bf16),
    ]
    return pl.pallas_call(
        functools.partial(panel_kernel, views, len(pieces), width),
        out_shape=[pltpu.HBM(*out) for out in outs],
        in_specs=[pl.BlockSpec(memory_space=pltpu.SMEM)]
        + [pl.BlockSpec(memory_space=pl.ANY)] * len(pieces),
        out_specs=[pl.BlockSpec(memory_space=pltpu.HBM)] * len(outs),
        scratch_shapes=[VMEM(*one) for one in outs + held]
        + [pltpu.SemaphoreType.DMA((len(views),)), pltpu.SemaphoreType.DMA((len(outs), NBLOCKS))],
        compiler_params=pltpu.CompilerParams(vmem_limit_bytes=room(*outs, *held)),
        cost_estimate=pl.CostEstimate(flops=8 * 10**9, bytes_accessed=2**20, transcendentals=1024),
        name="factor_panel",
    )(place, *pieces)


def tile_kernel(total, counts, views, place_ref, regular_ref, *refs):
    factors, refs = refs[:4], refs[4:]
    pieces, refs = refs[:total], refs[total:]
    out_ref, refs = refs[0], refs[1:]
    high_ref, low_ref, inv_high_ref, inv_low_ref, left_high_ref, left_low_ref, wide_high_ref, wide_low_ref = refs[:8]
    panel_ref, rows_ref, cols_ref, sem, factor_sem = refs[8:]
    held = [ref for ref, count in zip((panel_ref, rows_ref, cols_ref), counts) for _ in range(count)]
    views = [pieces[which].at[pl.ds(start, rows)] for which, start, rows in views]
    fetches = [
        pltpu.make_async_copy(factor, ref, factor_sem.at[i])
        for i, (factor, ref) in enumerate(zip(factors, (high_ref, low_ref, inv_high_ref, inv_low_ref)))
    ]
    for fetch in fetches:
        fetch.start()
    waits = place_pieces(place_ref, 2, views, held, sem)
    row_index, col_index = place_ref[0], place_ref[1]
    width, band = cols_ref.shape[0], rows_ref.shape[0] // (SPAN - 1)
    row_count = (SPAN - 1) * band
    panel_blocks = PANEL // width
    in_panel = col_index < panel_blocks
    slot = jnp.minimum(col_index, panel_blocks - 1)
    at = pl.ds(pl.multiple_of(slot * width, width), width)
    below, right = pl.ds(0, row_count), pl.ds(row_count, width)

    def solve(with_cols):
        for wait in waits:
            wait()
        step = min(WIDE, width)
        groups = [(rows_ref, at_row, pl.ds(at_row, band), band) for at_row in range(0, row_count, band)]
        if with_cols:
            groups = [
                (cols_ref, at_row, pl.ds(row_count + at_row, step), step) for at_row in range(0, width, step)
            ] + groups

        def grams(start):
            block = panel_ref[pl.ds(start, WIDE), :]
            return [dot_nt(ref[pl.ds(at_row, count), :], block) for ref, at_row, _, count in groups]

        columns = grams(0)
        for fetch in fetches:
            fetch.wait()

        for start in range(0, PANEL, WIDE):
            first, second = pl.ds(start, BLOCK), pl.ds(start + BLOCK, BLOCK)
            between = dot_nn3((high_ref[second, first], low_ref[second, first]), (inv_high_ref[first, :], inv_low_ref[first, :]))
            corner = split(-dot_nn3((inv_high_ref[second, :], inv_low_ref[second, :]), split(between)))
            for wide_ref, inv_ref, part in ((wide_high_ref, inv_high_ref, corner[0]), (wide_low_ref, inv_low_ref, corner[1])):
                wide_ref[first, pl.ds(0, BLOCK)] = inv_ref[first, :]
                wide_ref[first, pl.ds(BLOCK, BLOCK)] = jnp.zeros((BLOCK, BLOCK), bf16)
                wide_ref[second, pl.ds(0, BLOCK)] = part
                wide_ref[second, pl.ds(BLOCK, BLOCK)] = inv_ref[second, :]

        for start in range(0, PANEL, WIDE):
            here = pl.ds(start, WIDE)
            if start > 0:
                columns = [
                    column
                    - dot_nt3(
                        (left_high_ref[mine, :start], left_low_ref[mine, :start]), (high_ref[here, :start], low_ref[here, :start])
                    )
                    for column, (_, _, mine, _) in zip(grams(start), groups)
                ]
            for column, (_, _, mine, _) in zip(columns, groups):
                column = dot_nt3(split(column), (wide_high_ref[here, :], wide_low_ref[here, :]))
                left_high_ref[mine, here], left_low_ref[mine, here] = split(column)

    @pl.when(in_panel)
    def _():
        solve(False)
        mine = pl.ds(pl.multiple_of(row_index * band, band), band)
        out_ref[pl.ds(0, band), :] = high_ref[mine, at].astype(f32) + low_ref[mine, at].astype(f32)
        out_ref[pl.ds(band, row_count), :] = left_high_ref[below, at].astype(f32) + left_low_ref[below, at].astype(f32)

    @pl.when(jnp.logical_not(in_panel))
    def _():
        solve(True)
        out_ref[pl.ds(0, band), :] = jnp.zeros((band, width), f32)
        items = lax.broadcasted_iota(jnp.int32, (band, width), 0) + row_index * band
        columns = lax.broadcasted_iota(jnp.int32, (band, width), 1) + col_index * width
        for part in range(SPAN - 1):
            mine = pl.ds(part * band, band)
            tile = dot_nt(rows_ref[mine, :], cols_ref[...])
            tile = tile + jnp.where(items + (part + 1) * PANEL == columns, regular_ref[...], 0.0)
            out_ref[pl.ds((part + 1) * band, band), :] = tile - dot_nt3(
                (left_high_ref[mine, :], left_low_ref[mine, :]), (left_high_ref[right, :], left_low_ref[right, :])
            )


def finish_tile(place, regular, factors, panel, rows, cols, counts, views, band, users):
    spec = pl.BlockSpec(memory_space=VMEM)
    width = regular.shape[1]
    factors = [pltpu.with_memory_space_constraint(x, pltpu.HBM) for x in factors]
    pieces = panel + rows + cols
    out = ((SPAN * band, width), f32)
    below = (SPAN - 1) * band + width
    held = [
        ((below, PANEL), bf16),
        ((below, PANEL), bf16),
        ((PANEL, WIDE), bf16),
        ((PANEL, WIDE), bf16),
        ((PANEL, users), bf16),
        (((SPAN - 1) * band, users), bf16),
        ((width, users), bf16),
    ]
    return pl.pallas_call(
        functools.partial(tile_kernel, len(pieces), counts, views),
        out_shape=jax.ShapeDtypeStruct(*out),
        in_specs=[pl.BlockSpec(memory_space=pltpu.SMEM)]
        + [spec]
        + [pl.BlockSpec(memory_space=pltpu.HBM)] * len(factors)
        + [pl.BlockSpec(memory_space=pl.ANY)] * len(pieces),
        out_specs=spec,
        scratch_shapes=[VMEM(factor.shape, factor.dtype) for factor in factors]
        + [VMEM(*one) for one in held]
        + [pltpu.SemaphoreType.DMA((len(views),)), pltpu.SemaphoreType.DMA((len(factors),))],
        compiler_params=pltpu.CompilerParams(vmem_limit_bytes=room(out, *held, *((factor.shape, factor.dtype) for factor in factors))),
        cost_estimate=pl.CostEstimate(flops=20 * 10**9, bytes_accessed=24 * 2**20, transcendentals=0),
        name="finish_tile",
    )(place, regular, *factors, *pieces)


CORES = 2


def body(interactions, regular):
    row_count, col_count = lax.axis_size("row"), lax.axis_size("col")
    row_index, col_index = lax.axis_index("row"), lax.axis_index("col")
    width, users = interactions.shape
    band = PANEL // row_count
    ways = PANEL // width
    assert row_count == CORES * ways and col_count == SPAN * ways and users >= width
    slot, way = col_index // ways, col_index % ways
    pair, core = row_index // CORES, row_index % CORES
    all_users = row_count * users

    def exchange(value, move, only=None):
        perm = []
        for source_row in range(row_count):
            for source_col in range(col_count):
                place = (source_row // CORES, source_row % CORES, source_col // ways, source_col % ways)
                if only is None or only(*place):
                    to = move(*place)
                    target = (to[0] * CORES + to[1]) * col_count + to[2] * ways + to[3]
                    perm.append((source_row * col_count + source_col, target))
        return lax.ppermute(value, ("row", "col"), perm)

    def after(value, *others):
        return lax.optimization_barrier((value, *others))[0]

    high = lax.reduce_precision(regular, 8, 7)
    middle = lax.reduce_precision(regular - high, 8, 7)
    parts = jnp.stack([high, middle, regular - high - middle]).astype(bf16)
    parts = jnp.pad(parts, ((0, PARTS - 3), (0, users - width)))

    def over_core(value, only=None):
        return exchange(value, lambda p, h, s, w: (p, 1 - h, s, w), only)

    def over_pair(value):
        return exchange(value, lambda p, h, s, w: (1 - p, h, s, w))

    def over_way(value):
        return exchange(value, lambda p, h, s, w: (p, h, s, 1 - w))

    def traded(items, only):
        halves = items.reshape(CORES, band, users)
        kept, given = (lax.dynamic_index_in_dim(halves, core ^ flip, 0, False) for flip in range(CORES))
        return jnp.concatenate([kept, over_core(given, only)], 0)

    halves = interactions.reshape(CORES, band, users)
    offers = [lax.dynamic_index_in_dim(halves, core ^ flip, 0, False) for flip in range(CORES)]
    if ways == 2:
        raised = exchange(interactions, lambda p, h, s, w: (p, h, 0, w), lambda p, h, s, w: s == SPAN - 1)

    half = width // 2
    shared = jnp.concatenate([interactions, parts], 0)
    quarters, quarter_users = [], []
    reach = SPAN // 2
    while reach:
        got = exchange(
            shared, lambda p, h, s, w: (p, h, s + reach, w), lambda p, h, s, w: s % (2 * reach) == 0
        )
        if reach == SPAN // 2:
            for turn in range(ways):
                for flip in range(CORES):
                    quarters.append(
                        exchange(
                            offers[flip],
                            lambda p, h, s, w: (w, h ^ flip, s, (p + turn) % ways),
                            lambda p, h, s, w: s > 0,
                        )
                    )
                    quarter_users.append(((way - turn) % ways * CORES + (core ^ flip)) * users)
            if ways == 2:
                got = after(got, raised)
        shared = jnp.where(slot % (2 * reach) == reach, got, shared)
        reach //= 2
    quarters = jnp.concatenate(quarters, 0)

    def numbers(values):
        return jnp.stack([jnp.asarray(v, jnp.int32) for v in values])

    panel, panel_views, panel_place, part_views, part_place = [], [], [], [], []
    cols, cols_place = [interactions], [0, row_index * users]
    rows, rows_views, rows_place = [], [], []

    if ways == 2:
        mixed = jnp.where(slot == 0, traded(raised, lambda p, h, s, w: s == 0), interactions)
        shared = after(shared, quarters, mixed)
        pair_side, way_side = over_pair(shared), over_way(shared)
        own_twin, way_twin = over_core(shared), over_core(way_side)
        diagonal = exchange(
            jnp.where(core == 0, after(pair_side, own_twin), after(way_side, own_twin)),
            lambda p, h, s, w: (p, h, s, 1 - w) if h == 0 else (1 - p, h, s, w),
        )
        for from_pair, from_way, first_row, piece in (
            (pair, way, 0, shared),
            (1 - pair, way, 0, pair_side),
            (pair, 1 - way, 0, way_side),
            (1 - pair, 1 - way, 0, diagonal),
        ):
            twin = own_twin if piece is shared else way_twin if piece is way_side else over_core(piece)
            for from_core, value in ((core, piece), (1 - core, twin)):
                if value is shared or value is way_side:
                    part_views.append((len(panel), width, PARTS, True))
                    part_place += [from_way * PARTS, 0]
                count = min(value.shape[0], half if value.shape[0] < width else width)
                panel_views.append((len(panel), 0, count, False))
                panel_place += [from_way * width + first_row, (from_pair * CORES + from_core) * users]
                panel.append(value)
        crossed = [pair_side, way_side, diagonal]
        down = exchange(quarters, lambda p, h, s, w: (p, h, s - 1, w), lambda p, h, s, w: s > 0)
        up = exchange(quarters, lambda p, h, s, w: (p, h, s + 1, w), lambda p, h, s, w: 0 < s < SPAN - 1)
        down_held, up_held, mixed = lax.optimization_barrier(
            (down, up, mixed, *crossed)
        )[:3]
        down_again = exchange(down_held, lambda p, h, s, w: (p, h, s - 1, w), lambda p, h, s, w: 0 < s < SPAN - 1)
        up_again = exchange(up_held, lambda p, h, s, w: (p, h, s + 1, w), lambda p, h, s, w: s == 2)
        rows = [quarters, down, down_again, up, up_again]
        from_slots = [
            slot,
            jnp.where(slot < 3, slot + 1, 0),
            jnp.where(slot < 2, slot + 2, 0),
            jnp.where(slot > 1, slot - 1, 0),
            jnp.where(slot == 3, 1, 0),
        ]
        cols += [over_core(after(interactions, *crossed))]
        cols_place += [0, (row_index ^ 1) * users]
        for turn in range(ways):
            mix = exchange(
                mixed, lambda p, h, s, w: (w, h, s, (p + turn) % ways) if s == 0 else (1 - p, h ^ turn, s, w)
            )
            cols.append(mix)
            cols_place += [jnp.where(slot == 0, -1, 0), (row_index ^ (CORES + turn)) * users]
        for from_slot, piece in enumerate(rows):
            for which, from_users in enumerate(quarter_users):
                rows_views.append((from_slot, which * band, band))
                rows_place += [(from_slots[from_slot] - 1) * band, from_users]
        for which, from_users in enumerate(quarter_users):
            rows_views.append((len(rows) + 2 + which // CORES, which % CORES * band, band))
            rows_place += [jnp.where(slot == 0, (SPAN - 2) * band, -1), from_users]
    else:
        groups = [[s * ways + w for w in range(ways)] for s in range(SPAN)]
        shared = lax.all_gather(shared, "col", axis=0, axis_index_groups=groups)
        parts = shared[:, width:].reshape(ways * PARTS, users)
        shared = shared[:, :width].reshape(PANEL, users)
        panel, panel_place = [lax.all_gather(shared, "row", axis=1, tiled=True), parts], [0, 0]
        panel_views = [(0, 0, PANEL, False)]
        part_views, part_place = [(1, 0, ways * PARTS, True)], [0, 0]
        cols, cols_place = [lax.all_gather(interactions, "row", axis=1, tiled=True)], [0, 0]
        groups = [[s * ways + w for s in range(SPAN)] for w in range(ways)]
        rows = [lax.all_gather(quarters, "col", axis=0, tiled=True, axis_index_groups=groups)]
        for from_slot in range(1, SPAN):
            for which, from_users in enumerate(quarter_users):
                rows_views.append((0, (from_slot * len(quarter_users) + which) * band, band))
                rows_place += [(from_slot - 1) * band, from_users]

    factors = factor_panel(
        numbers(panel_place + part_place), panel, panel_views + part_views, width, all_users
    )
    views = [view[:3] for view in panel_views]
    views += [(len(panel) + i, start, count) for i, start, count in rows_views]
    views += [(len(panel) + len(rows) + i, 0, width) for i in range(len(cols))]
    counts = len(panel_views), len(rows_views), len(cols)
    tile = finish_tile(
        numbers([row_index, col_index] + panel_place + rows_place + cols_place),
        regular[None, :], factors, panel, rows, cols, counts, views, band, all_users,
    )
    return tile.reshape(SPAN, band, width)


def solution(mesh):
    return jax.shard_map(
        body,
        mesh=mesh,
        in_specs=(P("col", "row"), P("col")),
        out_specs=P(None, "row", "col"),
        check_vma=False,
    )
```

```python
import functools
import math
import jax
import jax.numpy as jnp
from jax import lax
from jax.experimental import pallas as pl
from jax.experimental.pallas import tpu as pltpu
from jax.sharding import PartitionSpec as P

PANEL = 1024
SPAN = 4
BLOCK = 128
WIDE = 256
SUB = 8
NBLOCKS = PANEL // BLOCK
PARTS = 16
VMEM = pltpu.VMEM
f32 = jnp.float32
bf16 = jnp.bfloat16


def dot_nt(a, b):
    return lax.dot_general(a, b, (((1,), (1,)), ((), ())), preferred_element_type=f32)


def split(value):
    high = value.astype(bf16)
    return high, (value - high.astype(f32)).astype(bf16)


def dot_nt3(a, b):
    return dot_nt(a[0], b[0]) + (dot_nt(a[0], b[1]) + dot_nt(a[1], b[0]))


def dot_nn3(a, b):
    def dot(x, y):
        return jnp.dot(x, y, preferred_element_type=f32)

    return dot(a[0], b[0]) + (dot(a[0], b[1]) + dot(a[1], b[0]))


def lanes(value, lane):
    return jnp.broadcast_to(value[:, lane : lane + 1], (SUB, BLOCK))


def sublanes(value, row):
    return jnp.broadcast_to(value[row : row + 1, :], (SUB, BLOCK))


def factor_block(block_ref, inverse_ref):
    tiles_count = BLOCK // SUB
    row_in_tile = lax.broadcasted_iota(jnp.int32, (SUB, BLOCK), 0)
    lane = lax.broadcasted_iota(jnp.int32, (SUB, BLOCK), 1)
    sides = [block_ref[pl.ds(SUB * t, SUB), :] for t in range(tiles_count)]
    inverses = [(lane == row_in_tile + SUB * t).astype(f32) for t in range(tiles_count)]
    uppers = []
    for step in range(tiles_count):
        base = SUB * step
        side, inverse = sides[step], inverses[step]
        if step == 0:
            columns = [lanes(side, base + b) for b in range(SUB)]
        entry = {(a, b): sublanes(columns[b], a) for b in range(SUB) for a in range(b, SUB)}
        vectors = [[sublanes(side, a) for a in range(SUB)], [sublanes(inverse, a) for a in range(SUB)]]
        if step + 1 < tiles_count:
            vectors.append([lanes(sides[step + 1], base + b) for b in range(SUB)])
            columns = [lanes(sides[step + 1], base + SUB + b) for b in range(SUB)]
        scale = [None] * SUB
        for m in range(0, SUB, 2):
            n = m + 1
            first, cross, second = entry[m, m], entry[n, m], entry[n, n]
            root = lax.rsqrt(first)
            det_root = lax.rsqrt(first * second - cross * cross)
            scale[m], scale[n] = root, det_root * (first * root)
            det_square = det_root * det_root
            link = cross * root
            entry[n, m] = link
            rest = range(n + 1, SUB)
            for x in rest:
                entry[x, m] = entry[x, m] * root
                entry[x, n] = entry[x, n] - entry[x, m] * link
            weighted = {x: entry[x, n] * first for x in rest}
            for y in rest:
                for x in range(y, SUB):
                    entry[x, y] = (entry[x, y] - entry[x, m] * entry[y, m]) - (weighted[x] * entry[y, n]) * det_square
            for x in rest:
                entry[x, n] = entry[x, n] * scale[n]
            for vector in vectors:
                vector[m] = vector[m] * root
                vector[n] = (vector[n] - link * vector[m]) * scale[n]
                for x in rest:
                    vector[x] = (vector[x] - entry[x, m] * vector[m]) - entry[x, n] * vector[n]
            if step + 1 < tiles_count:
                left, right = vectors[2][m], vectors[2][n]
                columns = [
                    (column - left * sublanes(left, b)) - right * sublanes(right, b)
                    for b, column in enumerate(columns)
                ]
        tops, insides = vectors[:2]
        upper, lower_inverse = tops[0], insides[0]
        for m in range(1, SUB):
            upper = jnp.where(row_in_tile == m, tops[m], upper)
            lower_inverse = jnp.where(row_in_tile == m, insides[m], lower_inverse)
        uppers.append(jnp.where(lane >= row_in_tile + base, upper, 0.0))
        inverse_ref[pl.ds(base, SUB), :] = lower_inverse
        if step + 1 < tiles_count:
            ahead = vectors[2]
            for m in range(SUB):
                sides[step + 1] = sides[step + 1] - ahead[m] * tops[m]
                inverses[step + 1] = inverses[step + 1] - ahead[m] * insides[m]
        if step + 2 < tiles_count:
            weights_top, weights_in = [None] * SUB, [None] * SUB
            for m in reversed(range(SUB)):
                top, inside = tops[m], insides[m]
                for b in range(m + 1, SUB):
                    top = top - entry[b, m] * weights_top[b]
                    inside = inside - entry[b, m] * weights_in[b]
                weights_top[m], weights_in[m] = top * scale[m], inside * scale[m]
            for t in range(step + 2, tiles_count):
                for m in range(SUB):
                    column = lanes(sides[t], base + m)
                    if m == 0:
                        top_sum, in_sum = column * weights_top[m], column * weights_in[m]
                    else:
                        top_sum = top_sum + column * weights_top[m]
                        in_sum = in_sum + column * weights_in[m]
                sides[t] = sides[t] - top_sum
                inverses[t] = inverses[t] - in_sum
    block_ref[...] = jnp.concatenate(uppers, 0).T


def place_pieces(place_ref, first, pieces, helds, sem):
    waits = []
    for i, (piece, held_ref) in enumerate(zip(pieces, helds)):
        rows, users = piece.shape
        row = place_ref[first + 2 * i]
        user = pl.multiple_of(place_ref[first + 2 * i + 1], users)
        to = held_ref.at[pl.ds(pl.multiple_of(jnp.maximum(row, 0), rows), rows), pl.ds(user, users)]
        copy = pltpu.make_async_copy(piece, to, sem.at[i])
        pl.when(row >= 0)(copy.start)
        waits.append(functools.partial(pl.when(row >= 0), copy.wait))
    return waits


def panel_kernel(views, count, width, place_ref, *refs):
    pieces, refs = refs[:count], refs[count:]
    outs, (high_ref, low_ref, inv_high_ref, inv_low_ref, lower_ref, coming_ref, *refs) = refs[:4], refs[4:]
    block_ref, inverse_ref, items_ref, parts_ref, sem, out_sem = refs
    held = [parts_ref if is_part else items_ref for _, _, _, is_part in views]
    views = [pieces[which].at[pl.ds(start, rows)] for which, start, rows, _ in views]
    waits = place_pieces(place_ref, 0, views, held, sem)
    for k in range(1, NBLOCKS):
        for ref in (high_ref, low_ref):
            ref[pl.ds(0, k * BLOCK), pl.ds(k * BLOCK, BLOCK)] = jnp.zeros((k * BLOCK, BLOCK), bf16)
    for wait in waits:
        wait()
    on_diagonal = lax.broadcasted_iota(jnp.int32, (BLOCK, BLOCK), 0) == lax.broadcasted_iota(
        jnp.int32, (BLOCK, BLOCK), 1
    )

    def before(k):
        start = k * BLOCK
        here, rest = pl.ds(start, BLOCK), pl.ds(start, PANEL - start)
        if k % 2 == 0:
            both = pl.ds(start, 2 * BLOCK)
            columns = dot_nt(items_ref[rest, :], items_ref[both, :])
            if k > 0:
                columns = columns - dot_nt3(
                    (high_ref[rest, :start], low_ref[rest, :start]), (high_ref[both, :start], low_ref[both, :start])
                )
            column = columns[:, :BLOCK]
            coming_ref[pl.ds(start + BLOCK, PANEL - start - BLOCK), :] = columns[BLOCK:, BLOCK:]
        else:
            last = pl.ds(start - BLOCK, BLOCK)
            high, low = high_ref[rest, last], low_ref[rest, last]
            column = coming_ref[rest, :] - dot_nt3((high, low), (high[:BLOCK], low[:BLOCK]))
        part, lane = PARTS * (start // width), start % width
        parts = parts_ref[pl.ds(part, PARTS), pl.ds(lane, BLOCK)].astype(f32)
        block_ref[...] = column[:BLOCK] + jnp.where(on_diagonal, parts[0:1] + parts[1:2] + parts[2:3], 0.0)
        if k + 1 < NBLOCKS:
            lower_ref[pl.ds(start + BLOCK, PANEL - start - BLOCK), :] = column[BLOCK:]

    def after(k):
        start = k * BLOCK
        here = pl.ds(start, BLOCK)
        inverse = split(inverse_ref[...])
        inv_high_ref[here, :], inv_low_ref[here, :] = inverse
        high_ref[here, here], low_ref[here, here] = split(block_ref[...])
        if k + 1 < NBLOCKS:
            rest = pl.ds(start + BLOCK, PANEL - start - BLOCK)
            high_ref[rest, here], low_ref[rest, here] = split(dot_nt3(split(lower_ref[rest, :]), inverse))

    def leave(k):
        column = pl.ds(k * BLOCK, BLOCK)
        return [
            pltpu.make_async_copy(high_ref.at[:, column], outs[0].at[:, column], out_sem.at[0, k]),
            pltpu.make_async_copy(low_ref.at[:, column], outs[1].at[:, column], out_sem.at[1, k]),
            pltpu.make_async_copy(inv_high_ref.at[column, :], outs[2].at[column, :], out_sem.at[2, k]),
            pltpu.make_async_copy(inv_low_ref.at[column, :], outs[3].at[column, :], out_sem.at[3, k]),
        ]

    before(0)

    def turn(k, carry):
        factor_block(block_ref, inverse_ref)
        for which in range(NBLOCKS):

            @pl.when(k == which)
            def _():
                after(which)
                for copy in leave(which):
                    copy.start()
                if which + 1 < NBLOCKS:
                    before(which + 1)

        return carry

    lax.fori_loop(0, NBLOCKS, turn, 0)
    for k in range(NBLOCKS):
        for copy in leave(k):
            copy.wait()


def room(*arrays):
    return sum(math.prod(shape) * jnp.dtype(dtype).itemsize for shape, dtype in arrays) + 8 * 2**20


def factor_panel(place, pieces, views, width, users):
    outs = [
        ((PANEL, PANEL), bf16),
        ((PANEL, PANEL), bf16),
        ((PANEL, BLOCK), bf16),
        ((PANEL, BLOCK), bf16),
    ]
    held = [
        ((PANEL, BLOCK), f32),
        ((PANEL, BLOCK), f32),
        ((BLOCK, BLOCK), f32),
        ((BLOCK, BLOCK), f32),
        ((PANEL, users), bf16),
        ((PANEL // width * PARTS, users), bf16),
    ]
    return pl.pallas_call(
        functools.partial(panel_kernel, views, len(pieces), width),
        out_shape=[pltpu.HBM(*out) for out in outs],
        in_specs=[pl.BlockSpec(memory_space=pltpu.SMEM)]
        + [pl.BlockSpec(memory_space=pl.ANY)] * len(pieces),
        out_specs=[pl.BlockSpec(memory_space=pltpu.HBM)] * len(outs),
        scratch_shapes=[VMEM(*one) for one in outs + held]
        + [pltpu.SemaphoreType.DMA((len(views),)), pltpu.SemaphoreType.DMA((len(outs), NBLOCKS))],
        compiler_params=pltpu.CompilerParams(vmem_limit_bytes=room(*outs, *held)),
        cost_estimate=pl.CostEstimate(flops=8 * 10**9, bytes_accessed=2**20, transcendentals=1024),
        name="factor_panel",
    )(place, *pieces)


def tile_kernel(total, counts, views, place_ref, regular_ref, *refs):
    factors, refs = refs[:4], refs[4:]
    pieces, refs = refs[:total], refs[total:]
    out_ref, refs = refs[0], refs[1:]
    high_ref, low_ref, inv_high_ref, inv_low_ref, left_high_ref, left_low_ref, wide_high_ref, wide_low_ref = refs[:8]
    panel_ref, rows_ref, cols_ref, sem, factor_sem = refs[8:]
    held = [ref for ref, count in zip((panel_ref, rows_ref, cols_ref), counts) for _ in range(count)]
    views = [pieces[which].at[pl.ds(start, rows)] for which, start, rows in views]
    fetches = [
        pltpu.make_async_copy(factor, ref, factor_sem.at[i])
        for i, (factor, ref) in enumerate(zip(factors, (high_ref, low_ref, inv_high_ref, inv_low_ref)))
    ]
    for fetch in fetches:
        fetch.start()
    waits = place_pieces(place_ref, 2, views, held, sem)
    row_index, col_index = place_ref[0], place_ref[1]
    width, band = cols_ref.shape[0], rows_ref.shape[0] // (SPAN - 1)
    row_count = (SPAN - 1) * band
    panel_blocks = PANEL // width
    in_panel = col_index < panel_blocks
    slot = jnp.minimum(col_index, panel_blocks - 1)
    at = pl.ds(pl.multiple_of(slot * width, width), width)
    below, right = pl.ds(0, row_count), pl.ds(row_count, width)

    def solve(with_cols):
        for wait in waits:
            wait()
        step = min(WIDE, width)
        groups = [(rows_ref, at_row, pl.ds(at_row, band), band) for at_row in range(0, row_count, band)]
        if with_cols:
            groups = [
                (cols_ref, at_row, pl.ds(row_count + at_row, step), step) for at_row in range(0, width, step)
            ] + groups

        def grams(start):
            block = panel_ref[pl.ds(start, WIDE), :]
            return [dot_nt(ref[pl.ds(at_row, count), :], block) for ref, at_row, _, count in groups]

        columns = grams(0)
        for fetch in fetches:
            fetch.wait()

        for start in range(0, PANEL, WIDE):
            first, second = pl.ds(start, BLOCK), pl.ds(start + BLOCK, BLOCK)
            between = dot_nn3((high_ref[second, first], low_ref[second, first]), (inv_high_ref[first, :], inv_low_ref[first, :]))
            corner = split(-dot_nn3((inv_high_ref[second, :], inv_low_ref[second, :]), split(between)))
            for wide_ref, inv_ref, part in ((wide_high_ref, inv_high_ref, corner[0]), (wide_low_ref, inv_low_ref, corner[1])):
                wide_ref[first, pl.ds(0, BLOCK)] = inv_ref[first, :]
                wide_ref[first, pl.ds(BLOCK, BLOCK)] = jnp.zeros((BLOCK, BLOCK), bf16)
                wide_ref[second, pl.ds(0, BLOCK)] = part
                wide_ref[second, pl.ds(BLOCK, BLOCK)] = inv_ref[second, :]

        for start in range(0, PANEL, WIDE):
            here = pl.ds(start, WIDE)
            if start > 0:
                columns = [
                    column
                    - dot_nt3(
                        (left_high_ref[mine, :start], left_low_ref[mine, :start]), (high_ref[here, :start], low_ref[here, :start])
                    )
                    for column, (_, _, mine, _) in zip(grams(start), groups)
                ]
            for column, (_, _, mine, _) in zip(columns, groups):
                column = dot_nt3(split(column), (wide_high_ref[here, :], wide_low_ref[here, :]))
                left_high_ref[mine, here], left_low_ref[mine, here] = split(column)

    @pl.when(in_panel)
    def _():
        solve(False)
        mine = pl.ds(pl.multiple_of(row_index * band, band), band)
        out_ref[pl.ds(0, band), :] = high_ref[mine, at].astype(f32) + low_ref[mine, at].astype(f32)
        out_ref[pl.ds(band, row_count), :] = left_high_ref[below, at].astype(f32) + left_low_ref[below, at].astype(f32)

    @pl.when(jnp.logical_not(in_panel))
    def _():
        solve(True)
        out_ref[pl.ds(0, band), :] = jnp.zeros((band, width), f32)
        items = lax.broadcasted_iota(jnp.int32, (band, width), 0) + row_index * band
        columns = lax.broadcasted_iota(jnp.int32, (band, width), 1) + col_index * width
        for part in range(SPAN - 1):
            mine = pl.ds(part * band, band)
            tile = dot_nt(rows_ref[mine, :], cols_ref[...])
            tile = tile + jnp.where(items + (part + 1) * PANEL == columns, regular_ref[...], 0.0)
            out_ref[pl.ds((part + 1) * band, band), :] = tile - dot_nt3(
                (left_high_ref[mine, :], left_low_ref[mine, :]), (left_high_ref[right, :], left_low_ref[right, :])
            )


def finish_tile(place, regular, factors, panel, rows, cols, counts, views, band, users):
    spec = pl.BlockSpec(memory_space=VMEM)
    width = regular.shape[1]
    factors = [pltpu.with_memory_space_constraint(x, pltpu.HBM) for x in factors]
    pieces = panel + rows + cols
    out = ((SPAN * band, width), f32)
    below = (SPAN - 1) * band + width
    held = [
        ((below, PANEL), bf16),
        ((below, PANEL), bf16),
        ((PANEL, WIDE), bf16),
        ((PANEL, WIDE), bf16),
        ((PANEL, users), bf16),
        (((SPAN - 1) * band, users), bf16),
        ((width, users), bf16),
    ]
    return pl.pallas_call(
        functools.partial(tile_kernel, len(pieces), counts, views),
        out_shape=jax.ShapeDtypeStruct(*out),
        in_specs=[pl.BlockSpec(memory_space=pltpu.SMEM)]
        + [spec]
        + [pl.BlockSpec(memory_space=pltpu.HBM)] * len(factors)
        + [pl.BlockSpec(memory_space=pl.ANY)] * len(pieces),
        out_specs=spec,
        scratch_shapes=[VMEM(factor.shape, factor.dtype) for factor in factors]
        + [VMEM(*one) for one in held]
        + [pltpu.SemaphoreType.DMA((len(views),)), pltpu.SemaphoreType.DMA((len(factors),))],
        compiler_params=pltpu.CompilerParams(vmem_limit_bytes=room(out, *held, *((factor.shape, factor.dtype) for factor in factors))),
        cost_estimate=pl.CostEstimate(flops=20 * 10**9, bytes_accessed=24 * 2**20, transcendentals=0),
        name="finish_tile",
    )(place, regular, *factors, *pieces)


CORES = 2


def body(interactions, regular):
    row_count, col_count = lax.axis_size("row"), lax.axis_size("col")
    row_index, col_index = lax.axis_index("row"), lax.axis_index("col")
    width, users = interactions.shape
    band = PANEL // row_count
    ways = PANEL // width
    assert row_count == CORES * ways and col_count == SPAN * ways and users >= width
    slot, way = col_index // ways, col_index % ways
    pair, core = row_index // CORES, row_index % CORES
    all_users = row_count * users

    def exchange(value, move, only=None):
        perm = []
        for source_row in range(row_count):
            for source_col in range(col_count):
                place = (source_row // CORES, source_row % CORES, source_col // ways, source_col % ways)
                if only is None or only(*place):
                    to = move(*place)
                    target = (to[0] * CORES + to[1]) * col_count + to[2] * ways + to[3]
                    perm.append((source_row * col_count + source_col, target))
        return lax.ppermute(value, ("row", "col"), perm)

    def after(value, *others):
        return lax.optimization_barrier((value, *others))[0]

    high = lax.reduce_precision(regular, 8, 7)
    middle = lax.reduce_precision(regular - high, 8, 7)
    parts = jnp.stack([high, middle, regular - high - middle]).astype(bf16)
    parts = jnp.pad(parts, ((0, PARTS - 3), (0, users - width)))

    def over_core(value, only=None):
        return exchange(value, lambda p, h, s, w: (p, 1 - h, s, w), only)

    def over_pair(value):
        return exchange(value, lambda p, h, s, w: (1 - p, h, s, w))

    def over_way(value):
        return exchange(value, lambda p, h, s, w: (p, h, s, 1 - w))

    def traded(items, only):
        halves = items.reshape(CORES, band, users)
        kept, given = (lax.dynamic_index_in_dim(halves, core ^ flip, 0, False) for flip in range(CORES))
        return jnp.concatenate([kept, over_core(given, only)], 0)

    halves = interactions.reshape(CORES, band, users)
    offers = [lax.dynamic_index_in_dim(halves, core ^ flip, 0, False) for flip in range(CORES)]
    if ways == 2:
        raised = exchange(interactions, lambda p, h, s, w: (p, h, 0, w), lambda p, h, s, w: s == SPAN - 1)

    half = width // 2
    shared = jnp.concatenate([interactions, parts], 0)
    quarters, quarter_users = [], []
    reach = SPAN // 2
    while reach:
        got = exchange(
            shared, lambda p, h, s, w: (p, h, s + reach, w), lambda p, h, s, w: s % (2 * reach) == 0
        )
        if reach == SPAN // 2:
            for turn in range(ways):
                for flip in range(CORES):
                    quarters.append(
                        exchange(
                            offers[flip],
                            lambda p, h, s, w: (w, h ^ flip, s, (p + turn) % ways),
                            lambda p, h, s, w: s > 0,
                        )
                    )
                    quarter_users.append(((way - turn) % ways * CORES + (core ^ flip)) * users)
            if ways == 2:
                got = after(got, raised)
        shared = jnp.where(slot % (2 * reach) == reach, got, shared)
        reach //= 2
    quarters = jnp.concatenate(quarters, 0)

    def numbers(values):
        return jnp.stack([jnp.asarray(v, jnp.int32) for v in values])

    panel, panel_views, panel_place, part_views, part_place = [], [], [], [], []
    cols, cols_place = [interactions], [0, row_index * users]
    rows, rows_views, rows_place = [], [], []

    if ways == 2:
        mixed = jnp.where(slot == 0, traded(raised, lambda p, h, s, w: s == 0), interactions)
        shared = after(shared, quarters, mixed)
        pair_side, way_side = over_pair(shared), over_way(shared)
        own_twin, way_twin = over_core(shared), over_core(way_side)
        diagonal = exchange(
            jnp.where(core == 0, after(pair_side, own_twin), after(way_side, own_twin)),
            lambda p, h, s, w: (p, h, s, 1 - w) if h == 0 else (1 - p, h, s, w),
        )
        for from_pair, from_way, first_row, piece in (
            (pair, way, 0, shared),
            (1 - pair, way, 0, pair_side),
            (pair, 1 - way, 0, way_side),
            (1 - pair, 1 - way, 0, diagonal),
        ):
            twin = own_twin if piece is shared else way_twin if piece is way_side else over_core(piece)
            for from_core, value in ((core, piece), (1 - core, twin)):
                if value is shared or value is way_side:
                    part_views.append((len(panel), width, PARTS, True))
                    part_place += [from_way * PARTS, 0]
                count = min(value.shape[0], half if value.shape[0] < width else width)
                panel_views.append((len(panel), 0, count, False))
                panel_place += [from_way * width + first_row, (from_pair * CORES + from_core) * users]
                panel.append(value)
        crossed = [pair_side, way_side, diagonal]
        down = exchange(quarters, lambda p, h, s, w: (p, h, s - 1, w), lambda p, h, s, w: s > 0)
        up = exchange(after(quarters, own_twin), lambda p, h, s, w: (p, h, s + 1, w), lambda p, h, s, w: 0 < s < SPAN - 1)
        down_held, up_held, mixed = lax.optimization_barrier(
            (down, up, mixed, *crossed)
        )[:3]
        down_again = exchange(down_held, lambda p, h, s, w: (p, h, s - 1, w), lambda p, h, s, w: 0 < s < SPAN - 1)
        up_again = exchange(up_held, lambda p, h, s, w: (p, h, s + 1, w), lambda p, h, s, w: s == 2)
        rows = [quarters, down, down_again, up, up_again]
        from_slots = [
            slot,
            jnp.where(slot < 3, slot + 1, 0),
            jnp.where(slot < 2, slot + 2, 0),
            jnp.where(slot > 1, slot - 1, 0),
            jnp.where(slot == 3, 1, 0),
        ]
        cols += [over_core(after(interactions, *crossed))]
        cols_place += [0, (row_index ^ 1) * users]
        for turn in range(ways):
            mix = exchange(
                mixed, lambda p, h, s, w: (w, h, s, (p + turn) % ways) if s == 0 else (1 - p, h ^ turn, s, w)
            )
            cols.append(mix)
            cols_place += [jnp.where(slot == 0, -1, 0), (row_index ^ (CORES + turn)) * users]
        for from_slot, piece in enumerate(rows):
            for which, from_users in enumerate(quarter_users):
                rows_views.append((from_slot, which * band, band))
                rows_place += [(from_slots[from_slot] - 1) * band, from_users]
        for which, from_users in enumerate(quarter_users):
            rows_views.append((len(rows) + 2 + which // CORES, which % CORES * band, band))
            rows_place += [jnp.where(slot == 0, (SPAN - 2) * band, -1), from_users]
    else:
        groups = [[s * ways + w for w in range(ways)] for s in range(SPAN)]
        shared = lax.all_gather(shared, "col", axis=0, axis_index_groups=groups)
        parts = shared[:, width:].reshape(ways * PARTS, users)
        shared = shared[:, :width].reshape(PANEL, users)
        panel, panel_place = [lax.all_gather(shared, "row", axis=1, tiled=True), parts], [0, 0]
        panel_views = [(0, 0, PANEL, False)]
        part_views, part_place = [(1, 0, ways * PARTS, True)], [0, 0]
        cols, cols_place = [lax.all_gather(interactions, "row", axis=1, tiled=True)], [0, 0]
        groups = [[s * ways + w for s in range(SPAN)] for w in range(ways)]
        rows = [lax.all_gather(quarters, "col", axis=0, tiled=True, axis_index_groups=groups)]
        for from_slot in range(1, SPAN):
            for which, from_users in enumerate(quarter_users):
                rows_views.append((0, (from_slot * len(quarter_users) + which) * band, band))
                rows_place += [(from_slot - 1) * band, from_users]

    factors = factor_panel(
        numbers(panel_place + part_place), panel, panel_views + part_views, width, all_users
    )
    views = [view[:3] for view in panel_views]
    views += [(len(panel) + i, start, count) for i, start, count in rows_views]
    views += [(len(panel) + len(rows) + i, 0, width) for i in range(len(cols))]
    counts = len(panel_views), len(rows_views), len(cols)
    tile = finish_tile(
        numbers([row_index, col_index] + panel_place + rows_place + cols_place),
        regular[None, :], factors, panel, rows, cols, counts, views, band, all_users,
    )
    return tile.reshape(SPAN, band, width)


def solution(mesh):
    return jax.shard_map(
        body,
        mesh=mesh,
        in_specs=(P("col", "row"), P("col")),
        out_specs=P(None, "row", "col"),
        check_vma=False,
    )
```
